32 devices in a mesh: rows: 16 (over z, y, x), grp: 2 (over core).
Axes of the slice: x: 2, y: 2, z: 4, core: 2. Of those that a mesh axis runs over, the one named last changes fastest.
Arguments:
- earlier: bfloat16 [131072, 1024], P(('rows', 'grp')), may hold values from -6 to 6
- snapshots: bfloat16 [131072, 512], P(('rows', 'grp')), may hold values from -8 to 8
- later: bfloat16 [131072, 512], P(('rows', 'grp')), may hold values from -8 to 8
Outputs:
- basis: bfloat16 [131072, 512], P(('rows', 'grp'))
- factors: float32 [2, 256, 256], replicated
- shift_block: float32 [512, 512], replicated
The draws below stay inside these ranges and needn't reach their ends.
All inputs are finite; a program needn't handle non-finite values.
Results may differ from the reference program's by a relative error of at most 0.0045.
The reference program's roundings to bfloat16 on the way count: a program that leaves them out, or rounds other values in their place, can miss the bound.
Values sent between devices are 32-bit elements; how exact they have to be, the bound alone decides.
No kernel may reach another device: no remote copies, remote signals or barrier semaphores. Data moves between devices by JAX's collectives and lax.ppermute only.
A program may use at most 128 MiB of HBM per device.

```python
import jax
import jax.numpy as jnp
from jax import lax

K0 = 1024
PANEL = 256
ROWS = 131072


def make_parts(key):
    space = jax.random.normal(jax.random.fold_in(key, 11), (ROWS, K0), jnp.float32)
    mixing = jax.random.normal(jax.random.fold_in(key, 12), (K0, 2 * PANEL + 1), jnp.float32) / K0 ** 0.5
    noise = jax.random.normal(jax.random.fold_in(key, 13), (ROWS, 2 * PANEL + 1), jnp.float32)
    height = 0.15
    space = jnp.clip(space, -6.0, 6.0)
    position = jnp.arange(ROWS, dtype=jnp.float32) / ROWS
    spread = height * jnp.exp(jnp.log(3.0) * position)
    return (space, mixing, noise, spread)


def draw_earlier(key, part):
    space, mixing, noise, spread = make_parts(key)
    return space.astype(jnp.bfloat16)


def draw_snapshots(key, part):
    space, mixing, noise, spread = make_parts(key)
    fields = jnp.dot(space, mixing[:, :2 * PANEL]) + spread[:, None] * noise[:, :2 * PANEL]
    return jnp.clip(fields, -8.0, 8.0).astype(jnp.bfloat16)


def draw_later(key, part):
    space, mixing, noise, spread = make_parts(key)
    mapping = jax.random.normal(jax.random.fold_in(key, 14), (2 * PANEL, 2 * PANEL), jnp.float32)
    carried = 0.6 * noise[:, 1:] + 0.8 * jnp.dot(noise[:, :2 * PANEL], mapping) / (2 * PANEL) ** 0.5
    fields = jnp.dot(space, mixing[:, 1:]) + spread[:, None] * carried
    return jnp.clip(fields, -8.0, 8.0).astype(jnp.bfloat16)


def setup_inputs(seed: int = 0) -> dict:
    seeds = jax.random.split(jax.random.key(seed), 4)
    earlier = draw_earlier(jax.random.fold_in(seeds[3], 71), 0)
    snapshots = draw_snapshots(jax.random.fold_in(seeds[3], 71), 0)
    later = draw_later(jax.random.fold_in(seeds[3], 71), 0)
    return {"earlier": earlier, "snapshots": snapshots, "later": later}


def inner(left, right):
    return jnp.dot(left.T.astype(jnp.float32), right.astype(jnp.float32), preferred_element_type=jnp.float32) / ROWS

def factor(gram, second):
    lower = jnp.linalg.cholesky(gram)
    inverse = jax.scipy.linalg.solve_triangular(lower, jnp.eye(gram.shape[0], dtype=jnp.float32), lower=True)
    newcols = jnp.dot(second, inverse.T, precision=lax.Precision.HIGHEST).astype(jnp.bfloat16)
    return (newcols, lower.T)

def orthogonalize(space, panel):
    first = inner(space, panel)
    once = (panel.astype(jnp.float32) - jnp.dot(space.astype(jnp.float32), first.astype(jnp.bfloat16).astype(jnp.float32), preferred_element_type=jnp.float32)).astype(jnp.bfloat16)
    second = inner(space, once)
    twice = once.astype(jnp.float32) - jnp.dot(space.astype(jnp.float32), second.astype(jnp.bfloat16).astype(jnp.float32), preferred_element_type=jnp.float32)
    gram = jnp.dot(twice.T, twice, precision=lax.Precision.HIGHEST) / ROWS
    return factor(gram, twice)

def reference(earlier, snapshots, later):
    q_first, r_first = orthogonalize(earlier, snapshots[:, :PANEL])
    space = jnp.concatenate([earlier, q_first], axis=1)
    q_second, r_second = orthogonalize(space, snapshots[:, PANEL:])
    basis = jnp.concatenate([q_first, q_second], axis=1)
    shift_block = inner(basis, later)
    return (basis, jnp.stack([r_first, r_second]), shift_block)
```

```python
import jax
import jax.numpy as jnp
from jax import lax
from jax.experimental import pallas as pl
from jax.experimental.pallas import tpu as pltpu
from jax.sharding import PartitionSpec as P

AXES = ("rows", "grp")
HIGHEST = lax.Precision.HIGHEST
BF16 = jnp.bfloat16
F32 = jnp.float32


def factor_tile(groups, emit):
    count = len(groups)
    lane = lax.broadcasted_iota(jnp.int32, (8, 128), 1)
    sub = lax.broadcasted_iota(jnp.int32, (8, 128), 0)
    rows = list(groups)
    for k in range(count):
        base = 8 * k
        strip = rows[k]
        inside = (lane >= base) & (lane < base + 8)
        eye = jnp.where(lane == base + sub, 1.0, 0.0).astype(F32)
        mixed = jnp.where(inside, eye, strip)
        cols = [jnp.broadcast_to(strip[:, base + j:base + j + 1], (8, 128)) for j in range(8)]
        entry = {}
        for j in range(8):
            for i in range(j, 8):
                entry[i, j] = jnp.broadcast_to(cols[j][i:i + 1, :], (8, 128))
        scale = []
        low = {}
        for j in range(8):
            r = lax.rsqrt(entry[j, j])
            scale.append(r)
            for i in range(j + 1, 8):
                low[i, j] = entry[i, j] * r
            for c in range(j + 1, 8):
                for i in range(c, 8):
                    entry[i, c] = entry[i, c] - low[i, j] * low[c, j]
        upper, both = [], []
        for j in range(8):
            u = jnp.broadcast_to(strip[j:j + 1, :], (8, 128))
            v = jnp.broadcast_to(mixed[j:j + 1, :], (8, 128))
            for i in range(j):
                u = u - low[j, i] * upper[i]
                v = v - low[j, i] * both[i]
            upper.append(u * scale[j])
            both.append(v * scale[j])
        out_r = upper[0]
        out_m = both[0]
        for j in range(1, 8):
            out_r = jnp.where(sub == j, upper[j], out_r)
            out_m = jnp.where(sub == j, both[j], out_m)
        emit(
            k,
            jnp.where(lane >= base + sub, out_r, 0.0),
            jnp.where(lane <= base + sub, out_m, 0.0),
        )
        for g in range(k + 1, count):
            w = rows[g]
            new = jnp.where(inside, 0.0, w)
            left = []
            for j in range(8):
                c = jnp.broadcast_to(w[:, base + j:base + j + 1], (8, 128))
                for i in range(j):
                    c = c - left[i] * low[j, i]
                c = c * scale[j]
                left.append(c)
                new = new - c * both[j]
            rows[g] = new


def factor_kernel(s_ref, r_ref, m_ref):
    n = s_ref.shape[0]
    tiles = n // 128

    def dot(a, b, dims):
        return lax.dot_general(a, b, (dims, ((), ())), precision=HIGHEST, preferred_element_type=F32)

    nn, tn = ((1,), (0,)), ((0,), (0,))
    r_ref[...] = s_ref[...]
    m_ref[...] = jnp.zeros_like(m_ref)

    def step(t, carry):
        top = pl.multiple_of(t * 128, 128)
        groups = [r_ref[pl.ds(pl.multiple_of(top + 8 * g, 8), 8), pl.ds(top, 128)] for g in range(16)]

        def emit(k, r, m):
            at = pl.ds(pl.multiple_of(top + 8 * k, 8), 8)
            r_ref[at, pl.ds(top, 128)] = r
            m_ref[at, pl.ds(top, 128)] = m

        factor_tile(groups, emit)
        return carry

    lax.fori_loop(0, 1, step, 0) if tiles == 1 else None
    if tiles > 1:
        def sweep(t, carry):
            step(t, carry)

            @pl.when(t == 0)
            def _():
                inv = m_ref[0:128, 0:128]
                u = dot(inv, s_ref[0:128, 128:n], nn)
                r_ref[0:128, 128:n] = u
                r_ref[128:n, 128:n] = s_ref[128:n, 128:n] - dot(u, u, tn)
                m_ref[128:n, 0:128] = dot(u, inv, tn)

            return carry

        lax.fori_loop(0, tiles, sweep, 0)
        r_ref[128:n, 0:128] = jnp.zeros((n - 128, 128), F32)
        m_ref[128:n, 0:128] = -dot(m_ref[128:n, 128:n], m_ref[128:n, 0:128], nn)


def factor(gram):
    n = gram.shape[0]
    shape = jax.ShapeDtypeStruct((n, n), F32)
    return pl.pallas_call(
        factor_kernel,
        out_shape=(shape, shape),
        in_specs=[pl.BlockSpec(memory_space=pltpu.VMEM)],
        out_specs=(pl.BlockSpec(memory_space=pltpu.VMEM),) * 2,
        name="factor",
    )(gram)


def bits_of(axis):
    size = lax.axis_size(axis)
    return [(axis, b) for b in range(size.bit_length() - 1)]


def exchange(x, axis, bit):
    size = lax.axis_size(axis)
    return lax.ppermute(x, axis, [(i, i ^ (1 << bit)) for i in range(size)])


def side(axis, bit):
    return (lax.axis_index(axis) >> bit) & 1


def powers():
    return all(lax.axis_size(a) & (lax.axis_size(a) - 1) == 0 for a in AXES)


def halves(parts, turns):
    if not powers():
        return [lax.psum(p, AXES) for p in parts]
    near, far = bits_of("grp"), bits_of("rows")
    orders = [near + far[t:] + far[:t] for t in turns]
    parts = list(parts)
    for step in range(len(near + far)):
        for n, order in enumerate(orders):
            x = parts[n]
            axis, bit = order[step]
            half = x.shape[0] // 2
            mine = side(axis, bit)
            send = lax.dynamic_slice_in_dim(x, (1 - mine) * half, half, 0)
            keep = lax.dynamic_slice_in_dim(x, mine * half, half, 0)
            parts[n] = keep + exchange(send, axis, bit)
    for step in reversed(range(len(near + far))):
        for n, order in enumerate(orders):
            x = parts[n]
            axis, bit = order[step]
            other = exchange(x, axis, bit)
            mine = side(axis, bit) == 1
            parts[n] = jnp.concatenate([jnp.where(mine, other, x), jnp.where(mine, x, other)], axis=0)
    return parts


def spread(x):
    n = lax.axis_size(AXES)
    block = x.shape[0] // n
    got = lax.all_to_all(x, AXES, 0, 0, tiled=True)
    mine = got.reshape(n, block, x.shape[1]).sum(0)
    out = jnp.broadcast_to(mine[None], (n, block, x.shape[1])).reshape(x.shape)
    return lax.all_to_all(out, AXES, 0, 0, tiled=True)


def rounded(x):
    return lax.reduce_precision(x, 8, 7)


def split(x):
    high = rounded(x)
    return high.astype(BF16), (x - high).astype(BF16)


def tn(a, b):
    return lax.dot_general(a, b, (((0,), (0,)), ((), ())), preferred_element_type=F32)


def nn(a, b):
    return jnp.dot(a, b, preferred_element_type=F32)


def full(a, b):
    return jnp.dot(a, b, precision=HIGHEST)


def body(earlier, snapshots, later):
    total = earlier.shape[0] * lax.axis_size(AXES)
    scale = 1.0 / total
    k = earlier.shape[1]
    p = snapshots.shape[1] // 2
    x_two = snapshots[:, p:]

    cross = tn(earlier, snapshots)
    square = tn(earlier, earlier)
    blocks = [cross[:, :p], cross[:, p:]]
    tiles = k // p
    for i in range(tiles):
        blocks.append(square[: (i + 1) * p, i * p:(i + 1) * p])
    packed = jnp.concatenate(blocks, axis=0)
    third = packed.shape[0] // 3
    one, two, three = halves([packed[:third], packed[third:2 * third], packed[2 * third:]], [0, 1, 2])
    packed = jnp.concatenate([one, two, three], axis=0) * scale
    c_all = jnp.concatenate([packed[:k], packed[k:2 * k]], axis=1)
    at = 2 * k
    columns = []
    for i in range(tiles):
        columns.append(packed[at:at + (i + 1) * p])
        at += (i + 1) * p
    rows_ = []
    for i in range(tiles):
        line = [columns[i][j * p:(j + 1) * p].T if j < i else columns[j][i * p:(i + 1) * p] for j in range(tiles)]
        rows_.append(jnp.concatenate(line, axis=1))
    square = jnp.concatenate(rows_, axis=0)

    b_all = rounded(c_all)
    b_all16 = b_all.astype(BF16)
    rest = nn(earlier, b_all16)
    once = rounded(snapshots[:, :p].astype(F32) - rest[:, :p])
    left_two = x_two.astype(F32) - rest[:, p:]

    off_high, off_low = split(square - jnp.eye(k, dtype=F32))
    after = (c_all - b_all) - nn(off_high, b_all16) - nn(off_low, b_all16)
    second = after[:, :p]
    second_b = rounded(second)
    second_b16 = second_b.astype(BF16)
    twice = once - nn(earlier, second_b16)
    against = (second - second_b) - nn(off_high, second_b16) - nn(off_low, second_b16)

    high, low = split(twice)
    hl = tn(high, low)
    gram = tn(high, high) + hl + hl.T
    with_two = tn(high, x_two) + tn(low, x_two)
    got = spread(jnp.concatenate([gram, with_two], axis=0)) * scale
    gram, with_two = got[:p], got[p:]
    r_one, inv_one = factor(gram)
    ih, il = split(inv_one.T)
    q_one = (nn(high, ih) + nn(high, il) + nn(low, ih)).astype(BF16)
    d = full(inv_one, with_two)
    d_b = rounded(d)
    left_two = rounded(left_two - nn(q_one, d_b.astype(BF16)))
    upper = after[:, p:] - full(against, full(inv_one.T, d_b))
    lower = (d - d_b) - full(inv_one, full(against.T, b_all[:, p:]))
    upper_b, lower_b = rounded(upper), rounded(lower)
    twice_two = left_two - nn(earlier, upper_b.astype(BF16)) - nn(q_one, lower_b.astype(BF16))
    expected = (lower - lower_b) - full(inv_one, full(against.T, upper_b))

    high2, low2 = split(twice_two)
    hl = tn(high2, low2)
    gram = tn(high2, high2) + hl + hl.T
    late = tn(high2, later) + tn(low2, later)
    early = tn(q_one, later)
    res = tn(q_one, high2) + tn(q_one, low2)
    a, b, c = halves(
        [
            jnp.concatenate([gram, res], axis=0),
            jnp.concatenate([late[:, :p], late[:, p:]], axis=0),
            jnp.concatenate([early[:, :p], early[:, p:]], axis=0),
        ],
        [0, 1, 2],
    )
    gram, res = a[:p] * scale, a[p:] * scale
    late = jnp.concatenate([b[:p], b[p:]], axis=1) * scale
    early = jnp.concatenate([c[:p], c[p:]], axis=1) * scale
    off = res - expected
    cut = full(res.T, off)
    gram = gram - cut - cut.T + full(off.T, off)
    late = late - full(off.T, early)
    r_two, inv_two = factor(gram)
    ih, il = split(inv_two.T)
    back = full(off, inv_two.T).astype(BF16)
    q_two = (nn(high2, ih) + nn(high2, il) + nn(low2, ih) - nn(q_one, back)).astype(BF16)
    basis = jnp.concatenate([q_one, q_two], axis=1)
    shift_block = jnp.concatenate([early, full(inv_two, late)], axis=0)
    return (basis, jnp.stack([r_one, r_two]), shift_block)


def solution(mesh):
    spec = P(("rows", "grp"), None)
    return jax.shard_map(
        body,
        mesh=mesh,
        in_specs=(spec, spec, spec),
        out_specs=(spec, P(), P()),
        check_vma=False,
    )
```

```python
import jax
import jax.numpy as jnp
from jax import lax
from jax.experimental import pallas as pl
from jax.experimental.pallas import tpu as pltpu
from jax.sharding import PartitionSpec as P

AXES = ("rows", "grp")
HIGHEST = lax.Precision.HIGHEST
BF16 = jnp.bfloat16
F32 = jnp.float32
VMEM_BYTES = 58 * 2**20


def dot(a, b):
    return jnp.dot(a, b, preferred_element_type=F32)


def full(a, b):
    return jnp.dot(a, b, precision=HIGHEST, preferred_element_type=F32)


def wide(x):
    return x.astype(F32)


def split(x):
    high = x.astype(BF16)
    return high, (x - wide(high)).astype(BF16)


def factor_tile(groups, emit):
    count = len(groups)
    lane = lax.broadcasted_iota(jnp.int32, (8, 128), 1)
    sub = lax.broadcasted_iota(jnp.int32, (8, 128), 0)
    rows = list(groups)
    for k in range(count):
        base = 8 * k
        strip = rows[k]
        inside = (lane >= base) & (lane < base + 8)
        eye = jnp.where(lane == base + sub, 1.0, 0.0).astype(F32)
        mixed = jnp.where(inside, eye, strip)
        cols = [jnp.broadcast_to(strip[:, base + j:base + j + 1], (8, 128)) for j in range(8)]
        entry = {}
        for j in range(8):
            for i in range(j, 8):
                entry[i, j] = jnp.broadcast_to(cols[j][i:i + 1, :], (8, 128))
        scale = []
        low = {}
        for j in range(8):
            r = lax.rsqrt(entry[j, j])
            scale.append(r)
            for i in range(j + 1, 8):
                low[i, j] = entry[i, j] * r
            for c in range(j + 1, 8):
                for i in range(c, 8):
                    entry[i, c] = entry[i, c] - low[i, j] * low[c, j]
        upper, both = [], []
        for j in range(8):
            u = jnp.broadcast_to(strip[j:j + 1, :], (8, 128))
            v = jnp.broadcast_to(mixed[j:j + 1, :], (8, 128))
            for i in range(j):
                u = u - low[j, i] * upper[i]
                v = v - low[j, i] * both[i]
            upper.append(u * scale[j])
            both.append(v * scale[j])
        out_r = upper[0]
        out_m = both[0]
        for j in range(1, 8):
            out_r = jnp.where(sub == j, upper[j], out_r)
            out_m = jnp.where(sub == j, both[j], out_m)
        emit(
            k,
            jnp.where(lane >= base + sub, out_r, 0.0),
            jnp.where(lane <= base + sub, out_m, 0.0),
        )
        for g in range(k + 1, count):
            w = rows[g]
            new = jnp.where(inside, 0.0, w)
            left = []
            for j in range(8):
                c = jnp.broadcast_to(w[:, base + j:base + j + 1], (8, 128))
                for i in range(j):
                    c = c - left[i] * low[j, i]
                c = c * scale[j]
                left.append(c)
                new = new - c * both[j]
            rows[g] = new


def factor(r_ref, m_ref):
    n = r_ref.shape[0]
    h = 128

    def step(t, carry):
        top = pl.multiple_of(t * h, h)
        groups = [r_ref[pl.ds(pl.multiple_of(top + 8 * g, 8), 8), pl.ds(top, h)] for g in range(h // 8)]

        def emit(k, r, m):
            at = pl.ds(pl.multiple_of(top + 8 * k, 8), 8)
            r_ref[at, pl.ds(top, h)] = r
            m_ref[at, pl.ds(top, h)] = m

        factor_tile(groups, emit)

        @pl.when(t == 0)
        def _():
            inv = m_ref[:h, :h]
            u = full(inv, r_ref[:h, h:])
            ut = u.T
            r_ref[:h, h:] = u
            r_ref[h:, h:] = r_ref[h:, h:] - full(ut, u)
            m_ref[h:, :h] = full(ut, inv)
            r_ref[h:, :h] = jnp.zeros((n - h, h), F32)
            m_ref[:h, h:] = jnp.zeros((h, n - h), F32)

        return carry

    lax.fori_loop(0, n // h, step, 0)
    m_ref[h:, :h] = -full(m_ref[h:, h:], m_ref[h:, :h])


def place(core_ref, sums, total_ref):
    mine = core_ref[0]
    at = 0
    for own, other in sums:
        h = own.shape[0]
        total_ref[pl.ds(pl.multiple_of(at + mine * h, 8), h)] = own[...]
        total_ref[pl.ds(pl.multiple_of(at + (1 - mine) * h, 8), h)] = other[...]
        at += 2 * h


def deal(core_ref, total_ref, sends, keeps):
    mine = core_ref[0]
    at = 0
    for send, keep in zip(sends, keeps):
        h = send.shape[0]
        keep[...] = total_ref[pl.ds(pl.multiple_of(at + mine * h, 8), h)]
        send[...] = total_ref[pl.ds(pl.multiple_of(at + (1 - mine) * h, 8), h)]
        at += 2 * h


def cross_kernel(parts, scale, core_ref, e_ref, x_ref, *refs):
    sends, keeps, acc = refs[:parts], refs[parts:2 * parts], refs[-1]
    k = e_ref.shape[1]
    p = x_ref.shape[1] // 2
    step = pl.program_id(0)

    @pl.when(step == 0)
    def _():
        acc[...] = jnp.zeros_like(acc)

    et = e_ref[...].T
    at = 0
    for c in range(2):
        acc[at:at + k] += dot(et, x_ref[:, c * p:(c + 1) * p])
        at += k
    for j in range(k // p):
        m = (j + 1) * p
        acc[at:at + m] += dot(et[:m], e_ref[:, j * p:(j + 1) * p])
        at += m

    @pl.when(step == pl.num_programs(0) - 1)
    def _():
        acc[...] = acc[...] * scale
        deal(core_ref, acc, sends, keeps)


def first_kernel(parts, scale, core_ref, *refs):
    own, other = refs[:parts], refs[parts:2 * parts]
    (e_ref, x_ref, u_ref, hi_ref, lo_ref, z_ref, h_ref, b2_ref, send, keep,
     total, b_ref, sb_ref, offh, offl, acc, hl) = refs[2 * parts:]
    k = e_ref.shape[1]
    p = x_ref.shape[1] // 2
    step = pl.program_id(0)

    @pl.when(step == 0)
    def _():
        place(core_ref, list(zip(own, other)), total)
        at = 2 * k
        for j in range(k // p):
            cols = slice(j * p, (j + 1) * p)
            for i in range(j + 1):
                block = total[at:at + p]
                at += p
                if i == j:
                    a = lax.broadcasted_iota(jnp.int32, (p, p), 0)
                    b = lax.broadcasted_iota(jnp.int32, (p, p), 1)
                    block = block - jnp.where(a == b, 1.0, 0.0)
                high, low = split(block)
                rows = slice(i * p, (i + 1) * p)
                offh[rows, cols] = high
                offl[rows, cols] = low
                if i < j:
                    offh[cols, rows] = high.T
                    offl[cols, rows] = low.T
        for c in range(2):
            cols = slice(c * p, (c + 1) * p)
            coef = total[c * k:(c + 1) * k]
            b = coef.astype(BF16)
            b_ref[:, cols] = b
            after = (coef - wide(b)) - dot(offh[...], b) - dot(offl[...], b)
            if c == 0:
                sb = after.astype(BF16)
                sb_ref[...] = sb
                h_ref[...] = (after - wide(sb)) - dot(offh[...], sb) - dot(offl[...], sb)
            else:
                z_ref[...] = after
                b2_ref[...] = b
        acc[...] = jnp.zeros_like(acc)
        hl[...] = jnp.zeros_like(hl)

    t = dot(e_ref[...], b_ref[...])
    once = wide((wide(x_ref[:, :p]) - t[:, :p]).astype(BF16))
    u_ref[...] = wide(x_ref[:, p:]) - t[:, p:]
    high, low = split(once - dot(e_ref[...], sb_ref[...]))
    hi_ref[...] = high
    lo_ref[...] = low
    ht, lt = high.T, low.T
    acc[:p] += dot(ht, high)
    hl[...] += dot(ht, low)
    acc[p:] += dot(ht, x_ref[:, p:]) + dot(lt, x_ref[:, p:])

    @pl.when(step == pl.num_programs(0) - 1)
    def _():
        acc[:p] = acc[:p] + hl[...] + hl[...].T
        acc[...] = acc[...] * scale
        deal(core_ref, acc, [send], [keep])


def second_kernel(parts, scale, core_ref, own, other, z_ref, h_ref, b2_ref, e_ref, u_ref, hi_ref, lo_ref, l_ref, *refs):
    q_ref, hi2_ref, lo2_ref, r_ref, x_ref = refs[:5]
    sends, keeps = refs[5:5 + parts], refs[5 + parts:5 + 2 * parts]
    total, m_ref, ih, il, db, ub, lb, acc, hl = refs[5 + 2 * parts:]
    p = r_ref.shape[0]
    step = pl.program_id(0)

    @pl.when(step == 0)
    def _():
        place(core_ref, [(own, other)], total)
        r_ref[...] = total[:p]
        factor(r_ref, m_ref)
        inv = m_ref[...]
        invt = inv.T
        high, low = split(invt)
        ih[...] = high
        il[...] = low
        d = full(inv, total[p:])
        d_b = wide(d.astype(BF16))
        db[...] = d.astype(BF16)
        against = h_ref[...]
        at = against.T
        upper = (z_ref[...] - full(against, full(invt, d_b))).astype(BF16)
        ub[...] = upper
        lower = (d - d_b) - full(inv, full(at, wide(b2_ref[...])))
        lower_b = lower.astype(BF16)
        lb[...] = lower_b
        x_ref[...] = (lower - wide(lower_b)) - full(inv, full(at, wide(upper)))
        acc[...] = jnp.zeros_like(acc)
        hl[...] = jnp.zeros_like(hl)

    high, low = hi_ref[...], lo_ref[...]
    q = (dot(high, ih[...]) + dot(high, il[...]) + dot(low, ih[...])).astype(BF16)
    q_ref[...] = q
    once = wide((u_ref[...] - dot(q, db[...])).astype(BF16))
    high, low = split(once - dot(e_ref[...], ub[...]) - dot(q, lb[...]))
    hi2_ref[...] = high
    lo2_ref[...] = low
    ht, lt, qt = high.T, low.T, q.T
    acc[:p] += dot(ht, high)
    hl[...] += dot(ht, low)
    acc[p:2 * p] += dot(qt, high) + dot(qt, low)
    for c in range(2):
        right = l_ref[:, c * p:(c + 1) * p]
        acc[(2 + c) * p:(3 + c) * p] += dot(ht, right) + dot(lt, right)
        acc[(4 + c) * p:(5 + c) * p] += dot(qt, right)

    @pl.when(step == pl.num_programs(0) - 1)
    def _():
        acc[:p] = acc[:p] + hl[...] + hl[...].T
        acc[...] = acc[...] * scale
        deal(core_ref, acc, sends, keeps)


def last_kernel(parts, core_ref, *refs):
    own, other = refs[:parts], refs[parts:2 * parts]
    x_ref, r1_ref, q_ref, hi_ref, lo_ref, basis, factors, shift, total, r_ref, m_ref, ih, il, back = refs[2 * parts:]
    p = r_ref.shape[0]

    @pl.when(pl.program_id(0) == 0)
    def _():
        place(core_ref, list(zip(own, other)), total)
        res = total[p:2 * p]
        off = res - x_ref[...]
        offt = off.T
        cut = full(offt, res)
        r_ref[...] = total[:p] - cut - cut.T + full(offt, off)
        factor(r_ref, m_ref)
        inv = m_ref[...]
        invt = inv.T
        high, low = split(invt)
        ih[...] = high
        il[...] = low
        back[...] = full(off, invt).astype(BF16)
        factors[0] = r1_ref[...]
        factors[1] = r_ref[...]
        for c in range(2):
            cols = slice(c * p, (c + 1) * p)
            early = total[(4 + c) * p:(5 + c) * p]
            shift[:p, cols] = early
            shift[p:, cols] = full(inv, total[(2 + c) * p:(3 + c) * p] - full(offt, early))

    high, low = hi_ref[...], lo_ref[...]
    q = dot(high, ih[...]) + dot(high, il[...]) + dot(low, ih[...]) - dot(q_ref[...], back[...])
    basis[:, :p] = q_ref[...]
    basis[:, p:] = q.astype(BF16)


def exchange(x, axis, bit):
    size = lax.axis_size(axis)
    return lax.ppermute(x, axis, [(i, i ^ (1 << bit)) for i in range(size)])


def summed(sends, keeps, tail):
    bits = list(range(lax.axis_size("rows").bit_length() - 1))
    turn, last = bits[:-1], bits[-1:]
    orders = [turn[n % len(turn):] + turn[:n % len(turn)] + last for n in range(len(sends))]
    me = lax.axis_index("rows")
    parts = [keep + exchange(send, "grp", 0) for send, keep in zip(sends, keeps)]
    halving = len(bits) - tail
    for step in range(halving):
        for n, order in enumerate(orders):
            x, bit = parts[n], order[step]
            half = x.shape[0] // 2
            mine = (me >> bit) & 1
            send = lax.dynamic_slice_in_dim(x, (1 - mine) * half, half, 0)
            keep = lax.dynamic_slice_in_dim(x, mine * half, half, 0)
            parts[n] = keep + exchange(send, "rows", bit)
    for step in range(halving, len(bits)):
        for n, order in enumerate(orders):
            parts[n] = parts[n] + exchange(parts[n], "rows", order[step])
    for step in reversed(range(halving)):
        for n, order in enumerate(orders):
            x, bit = parts[n], order[step]
            other = exchange(x, "rows", bit)
            mine = ((me >> bit) & 1) == 1
            parts[n] = jnp.concatenate([jnp.where(mine, other, x), jnp.where(mine, x, other)], axis=0)
    return parts, [exchange(x, "grp", 0) for x in parts]


def body(earlier, snapshots, later):
    n, k = earlier.shape
    p = snapshots.shape[1] // 2
    devices = lax.axis_size(AXES)
    scale = 1.0 / (n * devices)
    core = lax.axis_index("grp").astype(jnp.int32).reshape(1)
    blocks = k // p
    rows = (2 * blocks + blocks * (blocks + 1) // 2) * p
    unit = 2 * devices * 8
    parts = 3 if rows % (3 * unit) == 0 else 1
    tile = 512 if n % 512 == 0 else n
    tall = 1024 if n % 1024 == 0 else tile

    def smem():
        return pl.BlockSpec(memory_space=pltpu.SMEM)

    def whole(*shape):
        return pl.BlockSpec(shape, lambda i: (0,) * len(shape))

    def tiled(cols, height=tile):
        return pl.BlockSpec((height, cols), lambda i: (i, 0))

    def shape(*dims, dtype=F32):
        return jax.ShapeDtypeStruct(dims, dtype)

    def call(kernel, name, steps, ins, outs, scratch, flops, size, *args):
        return pl.pallas_call(
            kernel,
            grid=(steps,),
            in_specs=[s for s in ins],
            out_specs=[s for s, _ in outs],
            out_shape=[s for _, s in outs],
            scratch_shapes=scratch,
            name=name,
            cost_estimate=pl.CostEstimate(flops=flops, bytes_accessed=size, transcendentals=0),
            compiler_params=pltpu.CompilerParams(
                dimension_semantics=("arbitrary",), vmem_limit_bytes=VMEM_BYTES
            ),
        )(*args)

    half = rows // parts // 2
    halves = [(whole(half, p), shape(half, p))] * (2 * parts)
    got = call(
        lambda *r: cross_kernel(parts, scale, *r), "cross", n // tall,
        [smem(), tiled(k, tall), tiled(2 * p, tall)],
        halves,
        [pltpu.VMEM((rows, p), F32)],
        2 * n * rows * p, 2 * n * (k + 2 * p),
        core, earlier, snapshots,
    )
    own, other = summed(got[:parts], got[parts:], 1)

    u, hi, lo, z, h, b2, send, keep = call(
        lambda *r: first_kernel(parts, scale, *r), "first", n // tile,
        [smem()] + [whole(half, p)] * (2 * parts) + [tiled(k), tiled(2 * p)],
        [
            (tiled(p), shape(n, p)),
            (tiled(p), shape(n, p, dtype=BF16)),
            (tiled(p), shape(n, p, dtype=BF16)),
            (whole(k, p), shape(k, p)),
            (whole(k, p), shape(k, p)),
            (whole(k, p), shape(k, p, dtype=BF16)),
            (whole(p, p), shape(p, p)),
            (whole(p, p), shape(p, p)),
        ],
        [
            pltpu.VMEM((rows, p), F32),
            pltpu.VMEM((k, 2 * p), BF16),
            pltpu.VMEM((k, p), BF16),
            pltpu.VMEM((k, k), BF16),
            pltpu.VMEM((k, k), BF16),
            pltpu.VMEM((2 * p, p), F32),
            pltpu.VMEM((p, p), F32),
        ],
        2 * n * p * (3 * k + 4 * p) + 12 * k * k * p, n * (2 * k + 12 * p),
        core, *own, *other, earlier, snapshots,
    )
    (own,), (other,) = summed([send], [keep], 2)

    got = call(
        lambda *r: second_kernel(3, scale, *r), "second", n // tile,
        [smem(), whole(p, p), whole(p, p), whole(k, p), whole(k, p), whole(k, p),
         tiled(k), tiled(p), tiled(p), tiled(p), tiled(2 * p)],
        [
            (tiled(p), shape(n, p, dtype=BF16)),
            (tiled(p), shape(n, p, dtype=BF16)),
            (tiled(p), shape(n, p, dtype=BF16)),
            (whole(p, p), shape(p, p)),
            (whole(p, p), shape(p, p)),
        ] + [(whole(p, p), shape(p, p))] * 6,
        [
            pltpu.VMEM((2 * p, p), F32),
            pltpu.VMEM((p, p), F32),
            pltpu.VMEM((p, p), BF16),
            pltpu.VMEM((p, p), BF16),
            pltpu.VMEM((p, p), BF16),
            pltpu.VMEM((k, p), BF16),
            pltpu.VMEM((p, p), BF16),
            pltpu.VMEM((6 * p, p), F32),
            pltpu.VMEM((p, p), F32),
        ],
        2 * n * p * (k + 15 * p), n * (2 * k + 18 * p),
        core, own, other, z, h, b2, earlier, u, hi, lo, later,
    )
    q_one, hi2, lo2, r_one, expected = got[:5]
    own, other = summed(got[5:8], got[8:], 2)

    return tuple(call(
        lambda *r: last_kernel(3, *r), "last", n // tile,
        [smem()] + [whole(p, p)] * 8 + [tiled(p)] * 3,
        [
            (tiled(2 * p), shape(n, 2 * p, dtype=BF16)),
            (whole(2, p, p), shape(2, p, p)),
            (whole(2 * p, 2 * p), shape(2 * p, 2 * p)),
        ],
        [
            pltpu.VMEM((6 * p, p), F32),
            pltpu.VMEM((p, p), F32),
            pltpu.VMEM((p, p), F32),
            pltpu.VMEM((p, p), BF16),
            pltpu.VMEM((p, p), BF16),
            pltpu.VMEM((p, p), BF16),
        ],
        2 * n * p * 4 * p, n * 10 * p,
        core, *own, *other, expected, r_one, q_one, hi2, lo2,
    ))


def solution(mesh):
    spec = P(("rows", "grp"), None)
    return jax.shard_map(
        body,
        mesh=mesh,
        in_specs=(spec, spec, spec),
        out_specs=(spec, P(), P()),
        check_vma=False,
    )
```

```python
import jax
import jax.numpy as jnp
from jax import lax
from jax.experimental import pallas as pl
from jax.experimental.pallas import tpu as pltpu
from jax.sharding import PartitionSpec as P

AXES = ("rows", "grp")
HIGHEST = lax.Precision.HIGHEST
BF16 = jnp.bfloat16
F32 = jnp.float32
MIB = 2**20


def dot(a, b):
    return jnp.dot(a, b, preferred_element_type=F32)


def full(a, b):
    return jnp.dot(a, b, precision=HIGHEST, preferred_element_type=F32)


def wide(x):
    return x.astype(F32)


def split(x):
    high = x.astype(BF16)
    return high, (x - wide(high)).astype(BF16)


def thrice(a, b):
    return dot(a[0], b[0]) + dot(a[0], b[1]) + dot(a[1], b[0])


def factor_tile(groups, emit):
    count = len(groups)
    lane = lax.broadcasted_iota(jnp.int32, (8, 128), 1)
    sub = lax.broadcasted_iota(jnp.int32, (8, 128), 0)
    rows = list(groups)
    for k in range(count):
        base = 8 * k
        strip = rows[k]
        inside = (lane >= base) & (lane < base + 8)
        eye = jnp.where(lane == base + sub, 1.0, 0.0).astype(F32)
        mixed = jnp.where(inside, eye, strip)
        cols = [jnp.broadcast_to(strip[:, base + j:base + j + 1], (8, 128)) for j in range(8)]
        entry = {}
        for j in range(8):
            for i in range(j, 8):
                entry[i, j] = jnp.broadcast_to(cols[j][i:i + 1, :], (8, 128))
        scale = []
        low = {}
        for j in range(8):
            r = lax.rsqrt(entry[j, j])
            scale.append(r)
            for i in range(j + 1, 8):
                low[i, j] = entry[i, j] * r
            for c in range(j + 1, 8):
                for i in range(c, 8):
                    entry[i, c] = entry[i, c] - low[i, j] * low[c, j]
        upper, both = [], []
        for j in range(8):
            u = jnp.broadcast_to(strip[j:j + 1, :], (8, 128))
            v = jnp.broadcast_to(mixed[j:j + 1, :], (8, 128))
            for i in range(j):
                u = u - low[j, i] * upper[i]
                v = v - low[j, i] * both[i]
            upper.append(u * scale[j])
            both.append(v * scale[j])
        out_r = upper[0]
        out_m = both[0]
        for j in range(1, 8):
            out_r = jnp.where(sub == j, upper[j], out_r)
            out_m = jnp.where(sub == j, both[j], out_m)
        emit(
            k,
            jnp.where(lane >= base + sub, out_r, 0.0),
            jnp.where(lane <= base + sub, out_m, 0.0),
        )
        for g in range(k + 1, count):
            w = rows[g]
            new = jnp.where(inside, 0.0, w)
            left = []
            for j in range(8):
                c = jnp.broadcast_to(w[:, base + j:base + j + 1], (8, 128))
                for i in range(j):
                    c = c - left[i] * low[j, i]
                c = c * scale[j]
                left.append(c)
                new = new - c * both[j]
            rows[g] = new


def factor(r_ref, m_ref):
    n = r_ref.shape[0]
    h = 128

    def step(t, carry):
        top = pl.multiple_of(t * h, h)
        groups = [r_ref[pl.ds(pl.multiple_of(top + 8 * g, 8), 8), pl.ds(top, h)] for g in range(h // 8)]

        def emit(k, r, m):
            at = pl.ds(pl.multiple_of(top + 8 * k, 8), 8)
            r_ref[at, pl.ds(top, h)] = r
            m_ref[at, pl.ds(top, h)] = m

        factor_tile(groups, emit)

        @pl.when(t == 0)
        def _():
            inv = m_ref[:h, :h]
            u = full(inv, r_ref[:h, h:])
            ut = u.T
            r_ref[:h, h:] = u
            r_ref[h:, h:] = r_ref[h:, h:] - full(ut, u)
            m_ref[h:, :h] = full(ut, inv)
            r_ref[h:, :h] = jnp.zeros((n - h, h), F32)
            m_ref[:h, h:] = jnp.zeros((h, n - h), F32)

        return carry

    lax.fori_loop(0, n // h, step, 0)
    m_ref[h:, :h] = -full(m_ref[h:, h:], m_ref[h:, :h])


def place(core_ref, sums, total_ref):
    mine = core_ref[0]
    at = 0
    for own, other in sums:
        h = own.shape[0]
        total_ref[pl.ds(pl.multiple_of(at + mine * h, 8), h)] = own[...]
        total_ref[pl.ds(pl.multiple_of(at + (1 - mine) * h, 8), h)] = other[...]
        at += 2 * h


def deal(core_ref, total_ref, scale, sends, keeps):
    mine = core_ref[0]
    at = 0
    for send, keep in zip(sends, keeps):
        h = send.shape[0]
        keep[...] = total_ref[pl.ds(pl.multiple_of(at + mine * h, 8), h)] * scale
        send[...] = total_ref[pl.ds(pl.multiple_of(at + (1 - mine) * h, 8), h)] * scale
        at += 2 * h


def cross_kernel(parts, scale, core_ref, e_ref, x_ref, *refs):
    sends, keeps, acc = refs[:parts], refs[parts:2 * parts], refs[-1]
    k = e_ref.shape[1]
    p = x_ref.shape[1] // 2
    step = pl.program_id(0)

    @pl.when(step == 0)
    def _():
        acc[...] = jnp.zeros_like(acc)

    et = e_ref[...].T
    at = 0
    for c in range(2):
        acc[at:at + k] += dot(et, x_ref[:, c * p:(c + 1) * p])
        at += k
    for j in range(k // p):
        m = (j + 1) * p
        acc[at:at + m] += dot(et[:m], e_ref[:, j * p:(j + 1) * p])
        at += m

    @pl.when(step == pl.num_programs(0) - 1)
    def _():
        deal(core_ref, acc, scale, sends, keeps)


def first_kernel(parts, scale, core_ref, *refs):
    own, other = refs[:parts], refs[parts:2 * parts]
    (e_ref, x_ref, u_ref, hi_ref, lo_ref, z_ref, h_ref, b2_ref, send, keep,
     total, b_ref, sb_ref, offh, offl, acc, hl) = refs[2 * parts:]
    k = e_ref.shape[1]
    p = x_ref.shape[1] // 2
    step = pl.program_id(0)

    @pl.when(step == 0)
    def _():
        place(core_ref, list(zip(own, other)), total)
        at = 2 * k
        for j in range(k // p):
            cols = slice(j * p, (j + 1) * p)
            for i in range(j + 1):
                block = total[at:at + p]
                at += p
                if i == j:
                    a = lax.broadcasted_iota(jnp.int32, (p, p), 0)
                    b = lax.broadcasted_iota(jnp.int32, (p, p), 1)
                    block = block - jnp.where(a == b, 1.0, 0.0)
                high, low = split(block)
                rows = slice(i * p, (i + 1) * p)
                offh[rows, cols] = high
                offl[rows, cols] = low
                if i < j:
                    offh[cols, rows] = high.T
                    offl[cols, rows] = low.T
        for c in range(2):
            cols = slice(c * p, (c + 1) * p)
            coef = total[c * k:(c + 1) * k]
            b = coef.astype(BF16)
            b_ref[:, cols] = b
            after = (coef - wide(b)) - dot(offh[...], b) - dot(offl[...], b)
            if c == 0:
                sb = after.astype(BF16)
                sb_ref[...] = sb
                h_ref[...] = (after - wide(sb)) - dot(offh[...], sb) - dot(offl[...], sb)
            else:
                z_ref[...] = after
                b2_ref[...] = b
        acc[...] = jnp.zeros_like(acc)
        hl[...] = jnp.zeros_like(hl)

    t = dot(e_ref[...], b_ref[...])
    once = wide((wide(x_ref[:, :p]) - t[:, :p]).astype(BF16))
    u_ref[...] = wide(x_ref[:, p:]) - t[:, p:]
    high, low = split(once - dot(e_ref[...], sb_ref[...]))
    hi_ref[...] = high
    lo_ref[...] = low
    both = jnp.concatenate([high.T, low.T], axis=0)
    square = dot(both, high)
    acc[:p] += square[:p]
    hl[...] += square[p:]
    other_two = dot(both, x_ref[:, p:])
    acc[p:] += other_two[:p] + other_two[p:]

    @pl.when(step == pl.num_programs(0) - 1)
    def _():
        acc[:p] = acc[:p] + hl[...] + hl[...].T
        deal(core_ref, acc, scale, [send], [keep])


def second_kernel(parts, scale, core_ref, own, other, z_ref, h_ref, b2_ref, e_ref, u_ref, hi_ref, lo_ref, l_ref, *refs):
    q_ref, hi2_ref, lo2_ref, r_ref, x_ref = refs[:5]
    sends, keeps = refs[5:5 + parts], refs[5 + parts:5 + 2 * parts]
    total, m_ref, ih, il, db, ub, lb, acc, hl = refs[5 + 2 * parts:]
    p = r_ref.shape[0]
    step = pl.program_id(0)

    @pl.when(step == 0)
    def _():
        place(core_ref, [(own, other)], total)
        r_ref[...] = total[:p]
        factor(r_ref, m_ref)
        inv = m_ref[...]
        invt = inv.T
        high, low = split(invt)
        ih[...] = high
        il[...] = low
        d = full(inv, total[p:])
        d_b = d.astype(BF16)
        db[...] = d_b
        inv_s = split(inv)
        against = split(h_ref[...])
        at = split(h_ref[...].T)
        turned = split(dot(high, d_b) + dot(low, d_b))
        upper = (z_ref[...] - thrice(against, turned)).astype(BF16)
        ub[...] = upper
        lower = (d - wide(d_b)) - thrice(inv_s, split(dot(at[0], b2_ref[...]) + dot(at[1], b2_ref[...])))
        lower_b = lower.astype(BF16)
        lb[...] = lower_b
        x_ref[...] = (lower - wide(lower_b)) - thrice(inv_s, split(dot(at[0], upper) + dot(at[1], upper)))
        acc[...] = jnp.zeros_like(acc)
        hl[...] = jnp.zeros_like(hl)

    high, low = hi_ref[...], lo_ref[...]
    q = (dot(high, ih[...]) + dot(high, il[...]) + dot(low, ih[...])).astype(BF16)
    q_ref[...] = q
    once = wide((u_ref[...] - dot(q, db[...])).astype(BF16))
    high, low = split(once - dot(e_ref[...], ub[...]) - dot(q, lb[...]))
    hi2_ref[...] = high
    lo2_ref[...] = low
    qt = q.T
    left = jnp.concatenate([high.T, low.T, qt], axis=0)
    square = dot(left, high)
    acc[:p] += square[:p]
    hl[...] += square[p:2 * p]
    acc[p:2 * p] += square[2 * p:] + dot(qt, low)
    for c in range(2):
        mixed = dot(left, l_ref[:, c * p:(c + 1) * p])
        acc[(2 + c) * p:(3 + c) * p] += mixed[:p] + mixed[p:2 * p]
        acc[(4 + c) * p:(5 + c) * p] += mixed[2 * p:]

    @pl.when(step == pl.num_programs(0) - 1)
    def _():
        acc[:p] = acc[:p] + hl[...] + hl[...].T
        deal(core_ref, acc, scale, sends, keeps)


def last_kernel(parts, core_ref, *refs):
    own, other = refs[:parts], refs[parts:2 * parts]
    x_ref, r1_ref, q_ref, hi_ref, lo_ref, basis, factors, shift, total, r_ref, m_ref, ih, il, back = refs[2 * parts:]
    p = r_ref.shape[0]

    @pl.when(pl.program_id(0) == 0)
    def _():
        place(core_ref, list(zip(own, other)), total)
        res = total[p:2 * p]
        off = res - x_ref[...]
        off_b = off.astype(BF16)
        offt = off.T.astype(BF16)
        cut = dot(offt, res.astype(BF16))
        r_ref[...] = total[:p] - cut - cut.T + dot(offt, off_b)
        factor(r_ref, m_ref)
        inv = m_ref[...]
        invt = inv.T
        high, low = split(invt)
        ih[...] = high
        il[...] = low
        back[...] = dot(off_b, high).astype(BF16)
        inv_s = split(inv)
        factors[0] = r1_ref[...]
        factors[1] = r_ref[...]
        for c in range(2):
            cols = slice(c * p, (c + 1) * p)
            early = total[(4 + c) * p:(5 + c) * p]
            shift[:p, cols] = early
            late = total[(2 + c) * p:(3 + c) * p] - dot(offt, early.astype(BF16))
            shift[p:, cols] = thrice(inv_s, split(late))

    high, low = hi_ref[...], lo_ref[...]
    q = dot(high, ih[...]) + dot(high, il[...]) + dot(low, ih[...]) - dot(q_ref[...], back[...])
    basis[:, :p] = q_ref[...]
    basis[:, p:] = q.astype(BF16)


def exchange(x, axis, bit):
    size = lax.axis_size(axis)
    return lax.ppermute(x, axis, [(i, i ^ (1 << bit)) for i in range(size)])


def summed(sends, keeps, tail):
    bits = list(range(lax.axis_size("rows").bit_length() - 1))
    turn, last = bits[:-1], bits[-1:]
    orders = [turn[n % len(turn):] + turn[:n % len(turn)] + last for n in range(len(sends))]
    me = lax.axis_index("rows")
    parts = [keep + exchange(send, "grp", 0) for send, keep in zip(sends, keeps)]
    halving = len(bits) - tail
    for step in range(halving):
        for n, order in enumerate(orders):
            x, bit = parts[n], order[step]
            half = x.shape[0] // 2
            mine = (me >> bit) & 1
            send = lax.dynamic_slice_in_dim(x, (1 - mine) * half, half, 0)
            keep = lax.dynamic_slice_in_dim(x, mine * half, half, 0)
            parts[n] = keep + exchange(send, "rows", bit)
    for step in range(halving, len(bits)):
        for n, order in enumerate(orders):
            parts[n] = parts[n] + exchange(parts[n], "rows", order[step])
    for step in reversed(range(halving)):
        for n, order in enumerate(orders):
            x, bit = parts[n], order[step]
            other = exchange(x, "rows", bit)
            mine = ((me >> bit) & 1) == 1
            parts[n] = jnp.concatenate([jnp.where(mine, other, x), jnp.where(mine, x, other)], axis=0)
    return parts, [exchange(x, "grp", 0) for x in parts]


def summed_at_once(send, keep):
    size = lax.axis_size("rows")
    x = keep + exchange(send, "grp", 0)
    got = lax.all_to_all(x, "rows", 0, 0, tiled=True)
    mine = got.reshape(size, x.shape[0] // size, x.shape[1]).sum(0)
    same = jnp.broadcast_to(mine[None], (size,) + mine.shape).reshape(x.shape)
    x = lax.all_to_all(same, "rows", 0, 0, tiled=True)
    return x, exchange(x, "grp", 0)


def body(earlier, snapshots, later):
    n, k = earlier.shape
    p = snapshots.shape[1] // 2
    devices = lax.axis_size(AXES)
    scale = 1.0 / (n * devices)
    core = lax.axis_index("grp").astype(jnp.int32).reshape(1)
    blocks = k // p
    rows = (2 * blocks + blocks * (blocks + 1) // 2) * p
    unit = 2 * devices * 8
    parts = 3 if rows % (3 * unit) == 0 else 1
    tile = 1024 if n % 1024 == 0 else n

    def smem():
        return pl.BlockSpec(memory_space=pltpu.SMEM)

    def whole(*shape):
        return pl.BlockSpec(shape, lambda i: (0,) * len(shape))

    def tiled(cols):
        return pl.BlockSpec((tile, cols), lambda i: (i, 0))

    def shape(*dims, dtype=F32):
        return jax.ShapeDtypeStruct(dims, dtype)

    def call(kernel, name, room, ins, outs, scratch, flops, size, *args):
        return pl.pallas_call(
            kernel,
            grid=(n // tile,),
            in_specs=[s for s in ins],
            out_specs=[s for s, _ in outs],
            out_shape=[s for _, s in outs],
            scratch_shapes=scratch,
            name=name,
            cost_estimate=pl.CostEstimate(flops=flops, bytes_accessed=size, transcendentals=0),
            compiler_params=pltpu.CompilerParams(
                dimension_semantics=("arbitrary",), vmem_limit_bytes=room * MIB
            ),
        )(*args)

    half = rows // parts // 2
    halves = [(whole(half, p), shape(half, p))] * (2 * parts)
    got = call(
        lambda *r: cross_kernel(parts, scale, *r), "cross", 32,
        [smem(), tiled(k), tiled(2 * p)],
        halves,
        [pltpu.VMEM((rows, p), F32)],
        2 * n * rows * p, 2 * n * (k + 2 * p),
        core, earlier, snapshots,
    )
    own, other = summed(got[:parts], got[parts:], 1)

    u, hi, lo, z, h, b2, send, keep = call(
        lambda *r: first_kernel(parts, scale, *r), "first", 48,
        [smem()] + [whole(half, p)] * (2 * parts) + [tiled(k), tiled(2 * p)],
        [
            (tiled(p), shape(n, p)),
            (tiled(p), shape(n, p, dtype=BF16)),
            (tiled(p), shape(n, p, dtype=BF16)),
            (whole(k, p), shape(k, p)),
            (whole(k, p), shape(k, p)),
            (whole(k, p), shape(k, p, dtype=BF16)),
            (whole(p, p), shape(p, p)),
            (whole(p, p), shape(p, p)),
        ],
        [
            pltpu.VMEM((rows, p), F32),
            pltpu.VMEM((k, 2 * p), BF16),
            pltpu.VMEM((k, p), BF16),
            pltpu.VMEM((k, k), BF16),
            pltpu.VMEM((k, k), BF16),
            pltpu.VMEM((2 * p, p), F32),
            pltpu.VMEM((p, p), F32),
        ],
        2 * n * p * (3 * k + 4 * p) + 12 * k * k * p, n * (2 * k + 12 * p),
        core, *own, *other, earlier, snapshots,
    )
    own, other = summed_at_once(send, keep)

    got = call(
        lambda *r: second_kernel(3, scale, *r), "second", 44,
        [smem(), whole(p, p), whole(p, p), whole(k, p), whole(k, p), whole(k, p),
         tiled(k), tiled(p), tiled(p), tiled(p), tiled(2 * p)],
        [
            (tiled(p), shape(n, p, dtype=BF16)),
            (tiled(p), shape(n, p, dtype=BF16)),
            (tiled(p), shape(n, p, dtype=BF16)),
            (whole(p, p), shape(p, p)),
            (whole(p, p), shape(p, p)),
        ] + [(whole(p, p), shape(p, p))] * 6,
        [
            pltpu.VMEM((2 * p, p), F32),
            pltpu.VMEM((p, p), F32),
            pltpu.VMEM((p, p), BF16),
            pltpu.VMEM((p, p), BF16),
            pltpu.VMEM((p, p), BF16),
            pltpu.VMEM((k, p), BF16),
            pltpu.VMEM((p, p), BF16),
            pltpu.VMEM((6 * p, p), F32),
            pltpu.VMEM((p, p), F32),
        ],
        2 * n * p * (k + 15 * p), n * (2 * k + 18 * p),
        core, own, other, z, h, b2, earlier, u, hi, lo, later,
    )
    q_one, hi2, lo2, r_one, expected = got[:5]
    own, other = summed(got[5:8], got[8:], 2)

    return tuple(call(
        lambda *r: last_kernel(3, *r), "last", 30,
        [smem()] + [whole(p, p)] * 8 + [tiled(p)] * 3,
        [
            (tiled(2 * p), shape(n, 2 * p, dtype=BF16)),
            (whole(2, p, p), shape(2, p, p)),
            (whole(2 * p, 2 * p), shape(2 * p, 2 * p)),
        ],
        [
            pltpu.VMEM((6 * p, p), F32),
            pltpu.VMEM((p, p), F32),
            pltpu.VMEM((p, p), F32),
            pltpu.VMEM((p, p), BF16),
            pltpu.VMEM((p, p), BF16),
            pltpu.VMEM((p, p), BF16),
        ],
        2 * n * p * 4 * p, n * 10 * p,
        core, *own, *other, expected, r_one, q_one, hi2, lo2,
    ))


def solution(mesh):
    spec = P(("rows", "grp"), None)
    return jax.shard_map(
        body,
        mesh=mesh,
        in_specs=(spec, spec, spec),
        out_specs=(spec, P(), P()),
        check_vma=False,
    )
```

```python
import jax
import jax.numpy as jnp
from jax import lax
from jax.experimental import pallas as pl
from jax.experimental.pallas import tpu as pltpu
from jax.sharding import PartitionSpec as P

AXES = ("rows", "grp")
HIGHEST = lax.Precision.HIGHEST
BF16 = jnp.bfloat16
F32 = jnp.float32
MIB = 2**20


def dot(a, b):
    return jnp.dot(a, b, preferred_element_type=F32)


def full(a, b):
    return jnp.dot(a, b, precision=HIGHEST, preferred_element_type=F32)


def wide(x):
    return x.astype(F32)


def split(x):
    high = x.astype(BF16)
    return high, (x - wide(high)).astype(BF16)


def thrice(a, b):
    return dot(a[0], b[0]) + dot(a[0], b[1]) + dot(a[1], b[0])


def factor_tile(groups, emit):
    count = len(groups)
    lane = lax.broadcasted_iota(jnp.int32, (8, 128), 1)
    sub = lax.broadcasted_iota(jnp.int32, (8, 128), 0)
    rows = list(groups)
    for k in range(count):
        base = 8 * k
        strip = rows[k]
        inside = (lane >= base) & (lane < base + 8)
        eye = jnp.where(lane == base + sub, 1.0, 0.0).astype(F32)
        mixed = jnp.where(inside, eye, strip)
        cols = [jnp.broadcast_to(strip[:, base + j:base + j + 1], (8, 128)) for j in range(8)]
        entry = {}
        for j in range(8):
            for i in range(j, 8):
                entry[i, j] = jnp.broadcast_to(cols[j][i:i + 1, :], (8, 128))
        scale = []
        low = {}
        for j in range(8):
            r = lax.rsqrt(entry[j, j])
            scale.append(r)
            for i in range(j + 1, 8):
                low[i, j] = entry[i, j] * r
            for c in range(j + 1, 8):
                for i in range(c, 8):
                    entry[i, c] = entry[i, c] - low[i, j] * low[c, j]
        upper, both = [], []
        for j in range(8):
            u = jnp.broadcast_to(strip[j:j + 1, :], (8, 128))
            v = jnp.broadcast_to(mixed[j:j + 1, :], (8, 128))
            for i in range(j):
                u = u - low[j, i] * upper[i]
                v = v - low[j, i] * both[i]
            upper.append(u * scale[j])
            both.append(v * scale[j])
        out_r = upper[0]
        out_m = both[0]
        for j in range(1, 8):
            out_r = jnp.where(sub == j, upper[j], out_r)
            out_m = jnp.where(sub == j, both[j], out_m)
        emit(
            k,
            jnp.where(lane >= base + sub, out_r, 0.0),
            jnp.where(lane <= base + sub, out_m, 0.0),
        )
        for g in range(k + 1, count):
            w = rows[g]
            new = jnp.where(inside, 0.0, w)
            left = []
            for j in range(8):
                c = jnp.broadcast_to(w[:, base + j:base + j + 1], (8, 128))
                for i in range(j):
                    c = c - left[i] * low[j, i]
                c = c * scale[j]
                left.append(c)
                new = new - c * both[j]
            rows[g] = new


def factor(r_ref, m_ref):
    n = r_ref.shape[0]
    h = 128

    def step(t, carry):
        top = pl.multiple_of(t * h, h)
        groups = [r_ref[pl.ds(pl.multiple_of(top + 8 * g, 8), 8), pl.ds(top, h)] for g in range(h // 8)]

        def emit(k, r, m):
            at = pl.ds(pl.multiple_of(top + 8 * k, 8), 8)
            r_ref[at, pl.ds(top, h)] = r
            m_ref[at, pl.ds(top, h)] = m

        factor_tile(groups, emit)

        @pl.when(t == 0)
        def _():
            inv = m_ref[:h, :h]
            u = full(inv, r_ref[:h, h:])
            ut = u.T
            r_ref[:h, h:] = u
            r_ref[h:, h:] = r_ref[h:, h:] - full(ut, u)
            m_ref[h:, :h] = full(ut, inv)
            r_ref[h:, :h] = jnp.zeros((n - h, h), F32)
            m_ref[:h, h:] = jnp.zeros((h, n - h), F32)

        return carry

    lax.fori_loop(0, n // h, step, 0)
    m_ref[h:, :h] = -full(m_ref[h:, h:], m_ref[h:, :h])


def place(core_ref, sums, total_ref):
    mine = core_ref[0]
    at = 0
    for own, other in sums:
        h = own.shape[0]
        total_ref[pl.ds(pl.multiple_of(at + mine * h, 8), h)] = own[...]
        total_ref[pl.ds(pl.multiple_of(at + (1 - mine) * h, 8), h)] = other[...]
        at += 2 * h


def deal(core_ref, total_ref, scale, sends, keeps):
    mine = core_ref[0]
    at = 0
    for send, keep in zip(sends, keeps):
        h = send.shape[0]
        keep[...] = total_ref[pl.ds(pl.multiple_of(at + mine * h, 8), h)] * scale
        send[...] = total_ref[pl.ds(pl.multiple_of(at + (1 - mine) * h, 8), h)] * scale
        at += 2 * h


def cross_kernel(parts, scale, core_ref, e_ref, x_ref, *refs):
    sends, keeps, acc = refs[:parts], refs[parts:2 * parts], refs[-1]
    k = e_ref.shape[1]
    p = x_ref.shape[1] // 2
    step = pl.program_id(0)

    @pl.when(step == 0)
    def _():
        acc[...] = jnp.zeros_like(acc)

    et = e_ref[...].T
    at = 0
    for c in range(2):
        acc[at:at + k] += dot(et, x_ref[:, c * p:(c + 1) * p])
        at += k
    for j in range(k // p):
        m = (j + 1) * p
        acc[at:at + m] += dot(et[:m], e_ref[:, j * p:(j + 1) * p])
        at += m

    @pl.when(step == pl.num_programs(0) - 1)
    def _():
        deal(core_ref, acc, scale, sends, keeps)


def first_kernel(parts, scale, core_ref, *refs):
    own, other = refs[:parts], refs[parts:2 * parts]
    (e_ref, x_ref, u_ref, w_ref, z_ref, h_ref, b2_ref, send, keep,
     total, b_ref, offh, offl, acc, hl) = refs[2 * parts:]
    k = e_ref.shape[1]
    p = x_ref.shape[1] // 2
    step = pl.program_id(0)

    @pl.when(step == 0)
    def _():
        place(core_ref, list(zip(own, other)), total)
        at = 2 * k
        for j in range(k // p):
            cols = slice(j * p, (j + 1) * p)
            for i in range(j + 1):
                block = total[at:at + p]
                at += p
                if i == j:
                    a = lax.broadcasted_iota(jnp.int32, (p, p), 0)
                    b = lax.broadcasted_iota(jnp.int32, (p, p), 1)
                    block = block - jnp.where(a == b, 1.0, 0.0)
                high, low = split(block)
                rows = slice(i * p, (i + 1) * p)
                offh[rows, cols] = high
                offl[rows, cols] = low
                if i < j:
                    offh[cols, rows] = high.T
                    offl[cols, rows] = low.T
        for c in range(2):
            cols = slice(c * p, (c + 1) * p)
            coef = total[c * k:(c + 1) * k]
            b = coef.astype(BF16)
            b_ref[:, cols] = b
            after = (coef - wide(b)) - dot(offh[...], b) - dot(offl[...], b)
            if c == 0:
                sb = after.astype(BF16)
                b_ref[:, 2 * p:] = sb
                h_ref[...] = (after - wide(sb)) - dot(offh[...], sb) - dot(offl[...], sb)
            else:
                z_ref[...] = after
                b2_ref[...] = b
        acc[...] = jnp.zeros_like(acc)
        hl[...] = jnp.zeros_like(hl)

    t = dot(e_ref[...], b_ref[...])
    once = wide((wide(x_ref[:, :p]) - t[:, :p]).astype(BF16))
    u_ref[...] = wide(x_ref[:, p:]) - t[:, p:2 * p]
    high, low = split(once - t[:, 2 * p:])
    w_ref[:, :p] = high
    w_ref[:, p:] = low
    both = jnp.concatenate([high.T, low.T], axis=0)
    square = dot(both, high)
    acc[:p] += square[:p]
    hl[...] += square[p:]
    other_two = dot(both, x_ref[:, p:])
    acc[p:] += other_two[:p] + other_two[p:]

    @pl.when(step == pl.num_programs(0) - 1)
    def _():
        acc[:p] = acc[:p] + hl[...] + hl[...].T
        deal(core_ref, acc, scale, [send], [keep])


def second_kernel(parts, scale, core_ref, own, other, z_ref, h_ref, b2_ref, e_ref, u_ref, w_ref, l_ref, *refs):
    q_ref, w2_ref, r_ref, x_ref = refs[:4]
    sends, keeps = refs[4:4 + parts], refs[4 + parts:4 + 2 * parts]
    total, m_ref, ih, il, db, ub, lb, acc, hl = refs[4 + 2 * parts:]
    p = r_ref.shape[0]
    step = pl.program_id(0)

    @pl.when(step == 0)
    def _():
        place(core_ref, [(own, other)], total)
        r_ref[...] = total[:p]
        factor(r_ref, m_ref)
        inv = m_ref[...]
        invt = inv.T
        high, low = split(invt)
        ih[:p] = high
        ih[p:] = high
        il[...] = low
        d = full(inv, total[p:])
        d_b = d.astype(BF16)
        db[...] = d_b
        inv_s = split(inv)
        against = split(h_ref[...])
        at = split(h_ref[...].T)
        turned = split(dot(high, d_b) + dot(low, d_b))
        upper = (z_ref[...] - thrice(against, turned)).astype(BF16)
        ub[...] = upper
        lower = (d - wide(d_b)) - thrice(inv_s, split(dot(at[0], b2_ref[...]) + dot(at[1], b2_ref[...])))
        lower_b = lower.astype(BF16)
        lb[...] = lower_b
        x_ref[...] = (lower - wide(lower_b)) - thrice(inv_s, split(dot(at[0], upper) + dot(at[1], upper)))
        acc[...] = jnp.zeros_like(acc)
        hl[...] = jnp.zeros_like(hl)

    q = (dot(w_ref[...], ih[...]) + dot(w_ref[:, :p], il[...])).astype(BF16)
    q_ref[...] = q
    once = wide((u_ref[...] - dot(q, db[...])).astype(BF16))
    high, low = split(once - dot(e_ref[...], ub[...]) - dot(q, lb[...]))
    w2_ref[:, :p] = high
    w2_ref[:, p:] = low
    qt = q.T
    left = jnp.concatenate([high.T, low.T, qt], axis=0)
    square = dot(left, high)
    acc[:p] += square[:p]
    hl[...] += square[p:2 * p]
    acc[p:2 * p] += square[2 * p:] + dot(qt, low)
    for c in range(2):
        mixed = dot(left, l_ref[:, c * p:(c + 1) * p])
        acc[(2 + c) * p:(3 + c) * p] += mixed[:p] + mixed[p:2 * p]
        acc[(4 + c) * p:(5 + c) * p] += mixed[2 * p:]

    @pl.when(step == pl.num_programs(0) - 1)
    def _():
        acc[:p] = acc[:p] + hl[...] + hl[...].T
        deal(core_ref, acc, scale, sends, keeps)


def last_kernel(parts, core_ref, *refs):
    own, other = refs[:parts], refs[parts:2 * parts]
    x_ref, r1_ref, q_ref, w_ref, basis, factors, shift, total, r_ref, m_ref, ih, il, back = refs[2 * parts:]
    p = r_ref.shape[0]

    @pl.when(pl.program_id(0) == 0)
    def _():
        place(core_ref, list(zip(own, other)), total)
        res = total[p:2 * p]
        off = res - x_ref[...]
        off_b = off.astype(BF16)
        offt = off.T.astype(BF16)
        cut = dot(offt, res.astype(BF16))
        r_ref[...] = total[:p] - cut - cut.T + dot(offt, off_b)
        factor(r_ref, m_ref)
        inv = m_ref[...]
        invt = inv.T
        high, low = split(invt)
        ih[:p] = high
        ih[p:] = high
        il[...] = low
        back[...] = dot(off_b, high).astype(BF16)
        inv_s = split(inv)
        factors[0] = r1_ref[...]
        factors[1] = r_ref[...]
        for c in range(2):
            cols = slice(c * p, (c + 1) * p)
            early = total[(4 + c) * p:(5 + c) * p]
            shift[:p, cols] = early
            late = total[(2 + c) * p:(3 + c) * p] - dot(offt, early.astype(BF16))
            shift[p:, cols] = thrice(inv_s, split(late))

    q = dot(w_ref[...], ih[...]) + dot(w_ref[:, :p], il[...]) - dot(q_ref[...], back[...])
    basis[:, :p] = q_ref[...]
    basis[:, p:] = q.astype(BF16)


def exchange(x, axis, bit):
    size = lax.axis_size(axis)
    return lax.ppermute(x, axis, [(i, i ^ (1 << bit)) for i in range(size)])


def swap(x, mask):
    return lax.ppermute(x, "rows", [(i, i ^ mask) for i in range(lax.axis_size("rows"))])


def summed(sends, keeps, tail):
    bits = list(range(lax.axis_size("rows").bit_length() - 1))
    turn, last = bits[:-1], bits[-1:]
    orders = [turn[n % len(turn):] + turn[:n % len(turn)] + last for n in range(len(sends))]
    me = lax.axis_index("rows")
    parts = [keep + exchange(send, "grp", 0) for send, keep in zip(sends, keeps)]
    halving = len(bits) - tail
    for step in range(halving):
        for n, order in enumerate(orders):
            x, bit = parts[n], order[step]
            half = x.shape[0] // 2
            mine = (me >> bit) & 1
            send = lax.dynamic_slice_in_dim(x, (1 - mine) * half, half, 0)
            keep = lax.dynamic_slice_in_dim(x, mine * half, half, 0)
            parts[n] = keep + exchange(send, "rows", bit)
    for step in range(halving, len(bits)):
        for n, order in enumerate(orders):
            parts[n] = parts[n] + exchange(parts[n], "rows", order[step])
    for step in reversed(range(halving)):
        for n, order in enumerate(orders):
            x, bit = parts[n], order[step]
            other = exchange(x, "rows", bit)
            mine = ((me >> bit) & 1) == 1
            parts[n] = jnp.concatenate([jnp.where(mine, other, x), jnp.where(mine, x, other)], axis=0)
    return parts, [exchange(x, "grp", 0) for x in parts]


def summed_at_once(send, keep):
    bits = lax.axis_size("rows").bit_length() - 1
    me = lax.axis_index("rows")
    x = keep + exchange(send, "grp", 0)
    levels = [(at, min(2, bits - at)) for at in range(0, bits, 2)]
    for at, width in levels:
        count = 1 << width
        block = x.shape[0] // count
        mine = (me >> at) & (count - 1)

        def piece(m):
            return lax.dynamic_slice_in_dim(x, (mine ^ m) * block, block, 0)

        got = [piece(0)] + [swap(piece(m), m << at) for m in range(1, count)]
        while len(got) > 1:
            got = [a + b for a, b in zip(got[::2], got[1::2])]
        x = got[0]
    for at, width in reversed(levels):
        count = 1 << width
        mine = (me >> at) & (count - 1)
        got = [x] + [swap(x, m << at) for m in range(1, count)]
        order = []
        for place_at in range(count):
            pick = got[0]
            for m in range(1, count):
                pick = jnp.where((mine ^ m) == place_at, got[m], pick)
            order.append(pick)
        x = jnp.concatenate(order, axis=0)
    return x, exchange(x, "grp", 0)


def body(earlier, snapshots, later):
    n, k = earlier.shape
    p = snapshots.shape[1] // 2
    devices = lax.axis_size(AXES)
    scale = 1.0 / (n * devices)
    core = lax.axis_index("grp").astype(jnp.int32).reshape(1)
    blocks = k // p
    rows = (2 * blocks + blocks * (blocks + 1) // 2) * p
    unit = 2 * devices * 8
    parts = 3 if rows % (3 * unit) == 0 else 1
    tile = 1024 if n % 1024 == 0 else n

    def smem():
        return pl.BlockSpec(memory_space=pltpu.SMEM)

    def whole(*shape):
        return pl.BlockSpec(shape, lambda i: (0,) * len(shape))

    def tiled(cols):
        return pl.BlockSpec((tile, cols), lambda i: (i, 0))

    def shape(*dims, dtype=F32):
        return jax.ShapeDtypeStruct(dims, dtype)

    def near(*dims, dtype=F32):
        return pltpu.VMEM(dims, dtype)

    def far(*dims, dtype=F32):
        return pltpu.HBM(dims, dtype)

    earlier, snapshots, later = (pltpu.with_memory_space_constraint(a, pltpu.HBM) for a in (earlier, snapshots, later))

    def call(kernel, name, room, ins, outs, scratch, flops, size, *args):
        return pl.pallas_call(
            kernel,
            grid=(n // tile,),
            in_specs=[s for s in ins],
            out_specs=[s for s, _ in outs],
            out_shape=[s for _, s in outs],
            scratch_shapes=scratch,
            name=name,
            cost_estimate=pl.CostEstimate(flops=flops, bytes_accessed=size, transcendentals=0),
            compiler_params=pltpu.CompilerParams(
                dimension_semantics=("arbitrary",), vmem_limit_bytes=room * MIB
            ),
        )(*args)

    half = rows // parts // 2
    halves = [(whole(half, p), near(half, p))] * (2 * parts)
    got = call(
        lambda *r: cross_kernel(parts, scale, *r), "cross", 32,
        [smem(), tiled(k), tiled(2 * p)],
        halves,
        [pltpu.VMEM((rows, p), F32)],
        2 * n * rows * p, 2 * n * (k + 2 * p),
        core, earlier, snapshots,
    )
    own, other = summed(got[:parts], got[parts:], 1)

    u, w, z, h, b2, send, keep = call(
        lambda *r: first_kernel(parts, scale, *r), "first", 48,
        [smem()] + [whole(half, p)] * (2 * parts) + [tiled(k), tiled(2 * p)],
        [
            (tiled(p), far(n, p)),
            (tiled(2 * p), far(n, 2 * p, dtype=BF16)),
            (whole(k, p), near(k, p)),
            (whole(k, p), near(k, p)),
            (whole(k, p), near(k, p, dtype=BF16)),
            (whole(p, p), near(p, p)),
            (whole(p, p), near(p, p)),
        ],
        [
            pltpu.VMEM((rows, p), F32),
            pltpu.VMEM((k, 3 * p), BF16),
            pltpu.VMEM((k, k), BF16),
            pltpu.VMEM((k, k), BF16),
            pltpu.VMEM((2 * p, p), F32),
            pltpu.VMEM((p, p), F32),
        ],
        2 * n * p * (3 * k + 4 * p) + 12 * k * k * p, n * (2 * k + 12 * p),
        core, *own, *other, earlier, snapshots,
    )
    own, other = summed_at_once(send, keep)

    got = call(
        lambda *r: second_kernel(3, scale, *r), "second", 44,
        [smem(), whole(p, p), whole(p, p), whole(k, p), whole(k, p), whole(k, p),
         tiled(k), tiled(p), tiled(2 * p), tiled(2 * p)],
        [
            (tiled(p), far(n, p, dtype=BF16)),
            (tiled(2 * p), far(n, 2 * p, dtype=BF16)),
            (whole(p, p), near(p, p)),
            (whole(p, p), near(p, p)),
        ] + [(whole(p, p), near(p, p))] * 6,
        [
            pltpu.VMEM((2 * p, p), F32),
            pltpu.VMEM((p, p), F32),
            pltpu.VMEM((2 * p, p), BF16),
            pltpu.VMEM((p, p), BF16),
            pltpu.VMEM((p, p), BF16),
            pltpu.VMEM((k, p), BF16),
            pltpu.VMEM((p, p), BF16),
            pltpu.VMEM((6 * p, p), F32),
            pltpu.VMEM((p, p), F32),
        ],
        2 * n * p * (k + 15 * p), n * (2 * k + 18 * p),
        core, own, other, z, h, b2, earlier, u, w, later,
    )
    q_one, w2, r_one, expected = got[:4]
    own, other = summed(got[4:7], got[7:], 2)

    return tuple(call(
        lambda *r: last_kernel(3, *r), "last", 30,
        [smem()] + [whole(p, p)] * 8 + [tiled(p), tiled(2 * p)],
        [
            (tiled(2 * p), shape(n, 2 * p, dtype=BF16)),
            (whole(2, p, p), shape(2, p, p)),
            (whole(2 * p, 2 * p), shape(2 * p, 2 * p)),
        ],
        [
            pltpu.VMEM((6 * p, p), F32),
            pltpu.VMEM((p, p), F32),
            pltpu.VMEM((p, p), F32),
            pltpu.VMEM((2 * p, p), BF16),
            pltpu.VMEM((p, p), BF16),
            pltpu.VMEM((p, p), BF16),
        ],
        2 * n * p * 4 * p, n * 10 * p,
        core, *own, *other, expected, r_one, q_one, w2,
    ))


def solution(mesh):
    spec = P(("rows", "grp"), None)
    return jax.shard_map(
        body,
        mesh=mesh,
        in_specs=(spec, spec, spec),
        out_specs=(spec, P(), P()),
        check_vma=False,
    )
```

```python
import jax
import jax.numpy as jnp
from jax import lax
from jax.experimental import pallas as pl
from jax.experimental.pallas import tpu as pltpu
from jax.sharding import PartitionSpec as P

AXES = ("rows", "grp")
HIGHEST = lax.Precision.HIGHEST
BF16 = jnp.bfloat16
F32 = jnp.float32
MIB = 2**20


def dot(a, b):
    return jnp.dot(a, b, preferred_element_type=F32)


def full(a, b):
    return jnp.dot(a, b, precision=HIGHEST, preferred_element_type=F32)


def wide(x):
    return x.astype(F32)


def split(x):
    high = x.astype(BF16)
    return high, (x - wide(high)).astype(BF16)


def thrice(a, b):
    return dot(a[0], b[0]) + dot(a[0], b[1]) + dot(a[1], b[0])


def factor_tile(groups, emit):
    count = len(groups)
    lane = lax.broadcasted_iota(jnp.int32, (8, 128), 1)
    sub = lax.broadcasted_iota(jnp.int32, (8, 128), 0)
    rows = list(groups)
    for k in range(count):
        base = 8 * k
        strip = rows[k]
        inside = (lane >= base) & (lane < base + 8)
        eye = jnp.where(lane == base + sub, 1.0, 0.0).astype(F32)
        mixed = jnp.where(inside, eye, strip)
        cols = [jnp.broadcast_to(strip[:, base + j:base + j + 1], (8, 128)) for j in range(8)]
        entry = {}
        for j in range(8):
            for i in range(j, 8):
                entry[i, j] = jnp.broadcast_to(cols[j][i:i + 1, :], (8, 128))
        scale = []
        low = {}
        for j in range(8):
            r = lax.rsqrt(entry[j, j])
            scale.append(r)
            for i in range(j + 1, 8):
                low[i, j] = entry[i, j] * r
            for c in range(j + 1, 8):
                for i in range(c, 8):
                    entry[i, c] = entry[i, c] - low[i, j] * low[c, j]
        upper, both = [], []
        for j in range(8):
            u = jnp.broadcast_to(strip[j:j + 1, :], (8, 128))
            v = jnp.broadcast_to(mixed[j:j + 1, :], (8, 128))
            for i in range(j):
                u = u - low[j, i] * upper[i]
                v = v - low[j, i] * both[i]
            upper.append(u * scale[j])
            both.append(v * scale[j])
        out_r = upper[0]
        out_m = both[0]
        for j in range(1, 8):
            out_r = jnp.where(sub == j, upper[j], out_r)
            out_m = jnp.where(sub == j, both[j], out_m)
        emit(
            k,
            jnp.where(lane >= base + sub, out_r, 0.0),
            jnp.where(lane <= base + sub, out_m, 0.0),
        )
        for g in range(k + 1, count):
            w = rows[g]
            new = jnp.where(inside, 0.0, w)
            left = []
            for j in range(8):
                c = jnp.broadcast_to(w[:, base + j:base + j + 1], (8, 128))
                for i in range(j):
                    c = c - left[i] * low[j, i]
                c = c * scale[j]
                left.append(c)
                new = new - c * both[j]
            rows[g] = new


def factor(r_ref, m_ref):
    n = r_ref.shape[0]
    h = 128

    def step(t, carry):
        top = pl.multiple_of(t * h, h)
        groups = [r_ref[pl.ds(pl.multiple_of(top + 8 * g, 8), 8), pl.ds(top, h)] for g in range(h // 8)]

        def emit(k, r, m):
            at = pl.ds(pl.multiple_of(top + 8 * k, 8), 8)
            r_ref[at, pl.ds(top, h)] = r
            m_ref[at, pl.ds(top, h)] = m

        factor_tile(groups, emit)

        @pl.when(t == 0)
        def _():
            inv = m_ref[:h, :h]
            u = full(inv, r_ref[:h, h:])
            ut = u.T
            r_ref[:h, h:] = u
            r_ref[h:, h:] = r_ref[h:, h:] - full(ut, u)
            m_ref[h:, :h] = full(ut, inv)
            r_ref[h:, :h] = jnp.zeros((n - h, h), F32)
            m_ref[:h, h:] = jnp.zeros((h, n - h), F32)

        return carry

    lax.fori_loop(0, n // h, step, 0)
    m_ref[h:, :h] = -full(m_ref[h:, h:], m_ref[h:, :h])


def place(core_ref, sums, total_ref):
    mine = core_ref[0]
    at = 0
    for own, other in sums:
        h = own.shape[0]
        total_ref[pl.ds(pl.multiple_of(at + mine * h, 8), h)] = own[...]
        total_ref[pl.ds(pl.multiple_of(at + (1 - mine) * h, 8), h)] = other[...]
        at += 2 * h


def deal(core_ref, total_ref, scale, sends, keeps):
    mine = core_ref[0]
    at = 0
    for send, keep in zip(sends, keeps):
        h = send.shape[0]
        keep[...] = total_ref[pl.ds(pl.multiple_of(at + mine * h, 8), h)] * scale
        send[...] = total_ref[pl.ds(pl.multiple_of(at + (1 - mine) * h, 8), h)] * scale
        at += 2 * h


def cross_kernel(scale, core_ref, e_ref, x_ref, send, keep, acc):
    k = e_ref.shape[1]
    p = x_ref.shape[1] // 2
    step = pl.program_id(0)

    @pl.when(step == 0)
    def _():
        acc[...] = jnp.zeros_like(acc)

    et = e_ref[...].T
    for c in range(2):
        acc[c * k:(c + 1) * k] += dot(et, x_ref[:, c * p:(c + 1) * p])

    @pl.when(step == pl.num_programs(0) - 1)
    def _():
        deal(core_ref, acc, scale, [send], [keep])


def square_kernel(parts, scale, core_ref, e_ref, *refs):
    sends, keeps, acc = refs[:parts], refs[parts:2 * parts], refs[-1]
    k = e_ref.shape[1]
    p = acc.shape[1]
    step = pl.program_id(0)

    @pl.when(step == 0)
    def _():
        acc[...] = jnp.zeros_like(acc)

    et = e_ref[...].T
    at = 0
    for j in range(k // p):
        m = (j + 1) * p
        acc[at:at + m] += dot(et[:m], e_ref[:, j * p:(j + 1) * p])
        at += m

    @pl.when(step == pl.num_programs(0) - 1)
    def _():
        deal(core_ref, acc, scale, sends, keeps)


def once_kernel(core_ref, own, other, e_ref, x_ref, o_ref, u_ref, total, b_ref):
    k = e_ref.shape[1]
    p = o_ref.shape[1]

    @pl.when(pl.program_id(0) == 0)
    def _():
        place(core_ref, [(own, other)], total)
        for c in range(2):
            b_ref[:, c * p:(c + 1) * p] = total[c * k:(c + 1) * k].astype(BF16)

    t = dot(e_ref[...], b_ref[...])
    o_ref[...] = (wide(x_ref[:, :p]) - t[:, :p]).astype(BF16)
    u_ref[...] = wide(x_ref[:, p:]) - t[:, p:]


def first_kernel(parts, scale, core_ref, *refs):
    own, other = refs[:parts], refs[parts:2 * parts]
    (e_ref, x_ref, o_ref, w_ref, z_ref, h_ref, t_ref, send, keep,
     total, sb_ref, offh, offl, acc, hl) = refs[2 * parts:]
    k = e_ref.shape[1]
    p = o_ref.shape[1]
    step = pl.program_id(0)

    @pl.when(step == 0)
    def _():
        place(core_ref, list(zip(own, other)), total)
        at = 2 * k
        for j in range(k // p):
            cols = slice(j * p, (j + 1) * p)
            for i in range(j + 1):
                block = total[at:at + p]
                at += p
                if i == j:
                    a = lax.broadcasted_iota(jnp.int32, (p, p), 0)
                    b = lax.broadcasted_iota(jnp.int32, (p, p), 1)
                    block = block - jnp.where(a == b, 1.0, 0.0)
                high, low = split(block)
                rows = slice(i * p, (i + 1) * p)
                offh[rows, cols] = high
                offl[rows, cols] = low
                if i < j:
                    offh[cols, rows] = high.T
                    offl[cols, rows] = low.T
        coef = total[:k]
        b = coef.astype(BF16)
        after = (coef - wide(b)) - dot(offh[...], b) - dot(offl[...], b)
        sb = after.astype(BF16)
        sb_ref[...] = sb
        against = (after - wide(sb)) - dot(offh[...], sb) - dot(offl[...], sb)
        h_ref[...] = against
        coef = total[k:2 * k]
        b = coef.astype(BF16)
        z_ref[...] = (coef - wide(b)) - dot(offh[...], b) - dot(offl[...], b)
        high, low = split(against.T)
        t_ref[...] = dot(high, b) + dot(low, b)
        acc[...] = jnp.zeros_like(acc)
        hl[...] = jnp.zeros_like(hl)

    high, low = split(wide(o_ref[...]) - dot(e_ref[...], sb_ref[...]))
    w_ref[:, :p] = high
    w_ref[:, p:] = low
    both = jnp.concatenate([high.T, low.T], axis=0)
    square = dot(both, high)
    acc[:p] += square[:p]
    hl[...] += square[p:]
    other_two = dot(both, x_ref[...])
    acc[p:] += other_two[:p] + other_two[p:]

    @pl.when(step == pl.num_programs(0) - 1)
    def _():
        acc[:p] = acc[:p] + hl[...] + hl[...].T
        deal(core_ref, acc, scale, [send], [keep])


def second_kernel(parts, scale, core_ref, own, other, z_ref, h_ref, t_ref, e_ref, u_ref, w_ref, l_ref, *refs):
    q_ref, w2_ref, r_ref, x_ref = refs[:4]
    sends, keeps = refs[4:4 + parts], refs[4 + parts:4 + 2 * parts]
    total, m_ref, ih, il, db, ub, lb, acc, hl = refs[4 + 2 * parts:]
    p = r_ref.shape[0]
    step = pl.program_id(0)

    @pl.when(step == 0)
    def _():
        place(core_ref, [(own, other)], total)
        r_ref[...] = total[:p]
        factor(r_ref, m_ref)
        inv = m_ref[...]
        invt = inv.T
        high, low = split(invt)
        ih[:p] = high
        ih[p:] = high
        il[...] = low
        d = full(inv, total[p:])
        d_b = d.astype(BF16)
        db[...] = d_b
        inv_s = split(inv)
        against = split(h_ref[...])
        at = split(h_ref[...].T)
        turned = split(dot(high, d_b) + dot(low, d_b))
        upper = (z_ref[...] - thrice(against, turned)).astype(BF16)
        ub[...] = upper
        lower = (d - wide(d_b)) - thrice(inv_s, split(t_ref[...]))
        lower_b = lower.astype(BF16)
        lb[...] = lower_b
        x_ref[...] = (lower - wide(lower_b)) - thrice(inv_s, split(dot(at[0], upper) + dot(at[1], upper)))
        acc[...] = jnp.zeros_like(acc)
        hl[...] = jnp.zeros_like(hl)

    q = (dot(w_ref[...], ih[...]) + dot(w_ref[:, :p], il[...])).astype(BF16)
    q_ref[...] = q
    once = wide((u_ref[...] - dot(q, db[...])).astype(BF16))
    high, low = split(once - dot(e_ref[...], ub[...]) - dot(q, lb[...]))
    w2_ref[:, :p] = high
    w2_ref[:, p:] = low
    qt = q.T
    left = jnp.concatenate([high.T, low.T, qt], axis=0)
    square = dot(left, high)
    acc[:p] += square[:p]
    hl[...] += square[p:2 * p]
    acc[p:2 * p] += square[2 * p:] + dot(qt, low)
    for c in range(2):
        mixed = dot(left, l_ref[:, c * p:(c + 1) * p])
        acc[(2 + c) * p:(3 + c) * p] += mixed[:p] + mixed[p:2 * p]
        acc[(4 + c) * p:(5 + c) * p] += mixed[2 * p:]

    @pl.when(step == pl.num_programs(0) - 1)
    def _():
        acc[:p] = acc[:p] + hl[...] + hl[...].T
        deal(core_ref, acc, scale, sends, keeps)


def last_kernel(parts, core_ref, *refs):
    own, other = refs[:parts], refs[parts:2 * parts]
    x_ref, r1_ref, q_ref, w_ref, basis, factors, shift, total, r_ref, m_ref, ih, il, back = refs[2 * parts:]
    p = r_ref.shape[0]

    @pl.when(pl.program_id(0) == 0)
    def _():
        place(core_ref, list(zip(own, other)), total)
        res = total[p:2 * p]
        off = res - x_ref[...]
        off_b = off.astype(BF16)
        offt = off.T.astype(BF16)
        cut = dot(offt, res.astype(BF16))
        r_ref[...] = total[:p] - cut - cut.T + dot(offt, off_b)
        factor(r_ref, m_ref)
        inv = m_ref[...]
        invt = inv.T
        high, low = split(invt)
        ih[:p] = high
        ih[p:] = high
        il[...] = low
        back[...] = dot(off_b, high).astype(BF16)
        inv_s = split(inv)
        factors[0] = r1_ref[...]
        factors[1] = r_ref[...]
        for c in range(2):
            cols = slice(c * p, (c + 1) * p)
            early = total[(4 + c) * p:(5 + c) * p]
            shift[:p, cols] = early
            late = total[(2 + c) * p:(3 + c) * p] - dot(offt, early.astype(BF16))
            shift[p:, cols] = thrice(inv_s, split(late))

    q = dot(w_ref[...], ih[...]) + dot(w_ref[:, :p], il[...]) - dot(q_ref[...], back[...])
    basis[:, :p] = q_ref[...]
    basis[:, p:] = q.astype(BF16)


def exchange(x, axis, bit):
    size = lax.axis_size(axis)
    return lax.ppermute(x, axis, [(i, i ^ (1 << bit)) for i in range(size)])


def summed(sends, keeps, tail, orders):
    me = lax.axis_index("rows")
    parts = list(keeps)
    for n, order in enumerate(orders):
        x = keeps[n] + sends[n]
        halving = len(order) - tail
        for bit in order[:halving]:
            half = x.shape[0] // 2
            mine = (me >> bit) & 1
            send = lax.dynamic_slice_in_dim(x, (1 - mine) * half, half, 0)
            keep = lax.dynamic_slice_in_dim(x, mine * half, half, 0)
            x = keep + exchange(send, "rows", bit)
        for bit in order[halving:]:
            x = x + exchange(x, "rows", bit)
        for bit in reversed(order[:halving]):
            other = exchange(x, "rows", bit)
            mine = ((me >> bit) & 1) == 1
            x = jnp.concatenate([jnp.where(mine, other, x), jnp.where(mine, x, other)], axis=0)
        parts[n] = x
    return parts, [exchange(x, "grp", 0) for x in parts]


def turned(bits, n):
    most = bits[:-1]
    n = n % len(most)
    return most[n:] + most[:n] + bits[-1:]


def summed_at_once(send, keep):
    size = lax.axis_size("rows")
    x = keep + exchange(send, "grp", 0)
    got = lax.all_to_all(x, "rows", 0, 0, tiled=True)
    mine = got.reshape(size, x.shape[0] // size, x.shape[1]).sum(0)
    same = jnp.broadcast_to(mine[None], (size,) + mine.shape).reshape(x.shape)
    x = lax.all_to_all(same, "rows", 0, 0, tiled=True)
    return x, exchange(x, "grp", 0)


def body(earlier, snapshots, later):
    n, k = earlier.shape
    p = snapshots.shape[1] // 2
    devices = lax.axis_size(AXES)
    scale = 1.0 / (n * devices)
    core = lax.axis_index("grp").astype(jnp.int32).reshape(1)
    blocks = k // p
    parts = 2
    tile = 1024 if n % 1024 == 0 else n

    def smem():
        return pl.BlockSpec(memory_space=pltpu.SMEM)

    def whole(*shape):
        return pl.BlockSpec(shape, lambda i: (0,) * len(shape))

    def tiled(cols):
        return pl.BlockSpec((tile, cols), lambda i: (i, 0))

    def shape(*dims, dtype=F32):
        return jax.ShapeDtypeStruct(dims, dtype)

    def near(*dims, dtype=F32):
        return pltpu.VMEM(dims, dtype)

    def far(*dims, dtype=F32):
        return pltpu.HBM(dims, dtype)

    def fixed(x):
        return pltpu.with_memory_space_constraint(x, pltpu.HBM)

    earlier, snapshots, later = fixed(earlier), fixed(snapshots), fixed(later)

    def call(kernel, name, room, ins, outs, scratch, flops, size, *args):
        return pl.pallas_call(
            kernel,
            grid=(n // tile,),
            in_specs=[s for s in ins],
            out_specs=[s for s, _ in outs],
            out_shape=[s for _, s in outs],
            scratch_shapes=scratch,
            name=name,
            cost_estimate=pl.CostEstimate(flops=flops, bytes_accessed=size, transcendentals=0),
            compiler_params=pltpu.CompilerParams(
                dimension_semantics=("arbitrary",), vmem_limit_bytes=room * MIB
            ),
        )(*args)

    bits = list(range(lax.axis_size("rows").bit_length() - 1))
    send, keep = call(
        lambda *r: cross_kernel(scale, *r), "cross", 24,
        [smem(), tiled(k), tiled(2 * p)],
        [(whole(k, p), near(k, p))] * 2,
        [pltpu.VMEM((2 * k, p), F32)],
        4 * n * k * p, 2 * n * (k + 2 * p),
        core, earlier, snapshots,
    )
    got = exchange(send, "grp", 0)
    got, core_too = lax.optimization_barrier((got, core))
    (c_own,), (c_other,) = summed([got], [keep], 1, [turned(bits, 0)])

    rows = blocks * (blocks + 1) // 2 * p
    half = rows // parts // 2
    got = call(
        lambda *r: square_kernel(parts, scale, *r), "square", 28,
        [smem(), tiled(k)],
        [(whole(half, p), near(half, p))] * (2 * parts),
        [pltpu.VMEM((rows, p), F32)],
        2 * n * rows * p, 2 * n * k,
        core_too, earlier,
    )
    g_own, g_other = summed(
        [exchange(x, "grp", 0) for x in got[:parts]], got[parts:], 1,
        [turned(bits, t + 1) for t in range(parts)],
    )

    once, u = call(
        once_kernel, "once", 28,
        [smem(), whole(k, p), whole(k, p), tiled(k), tiled(2 * p)],
        [(tiled(p), far(n, p, dtype=BF16)), (tiled(p), far(n, p))],
        [pltpu.VMEM((2 * k, p), F32), pltpu.VMEM((k, 2 * p), BF16)],
        4 * n * k * p, 2 * n * (k + 5 * p),
        core, c_own, c_other, earlier, snapshots,
    )
    once, u = fixed(once), fixed(u)

    w, z, h, t, send, keep = call(
        lambda *r: first_kernel(1 + parts, scale, *r), "first", 36,
        [smem()] + ([whole(k, p)] + [whole(half, p)] * parts) * 2
        + [tiled(k), pl.BlockSpec((tile, p), lambda i: (i, 1)), tiled(p)],
        [
            (tiled(2 * p), far(n, 2 * p, dtype=BF16)),
            (whole(k, p), near(k, p)),
            (whole(k, p), near(k, p)),
            (whole(p, p), near(p, p)),
            (whole(p, p), near(p, p)),
            (whole(p, p), near(p, p)),
        ],
        [
            pltpu.VMEM((2 * k + rows, p), F32),
            pltpu.VMEM((k, p), BF16),
            pltpu.VMEM((k, k), BF16),
            pltpu.VMEM((k, k), BF16),
            pltpu.VMEM((2 * p, p), F32),
            pltpu.VMEM((p, p), F32),
        ],
        2 * n * p * (k + 4 * p) + 12 * k * k * p, n * (2 * k + 8 * p),
        core, c_own, *g_own, c_other, *g_other, earlier, snapshots, once,
    )
    w = fixed(w)
    own, other = summed_at_once(send, keep)

    got = call(
        lambda *r: second_kernel(3, scale, *r), "second", 32,
        [smem(), whole(p, p), whole(p, p), whole(k, p), whole(k, p), whole(p, p),
         tiled(k), tiled(p), tiled(2 * p), tiled(2 * p)],
        [
            (tiled(p), far(n, p, dtype=BF16)),
            (tiled(2 * p), far(n, 2 * p, dtype=BF16)),
            (whole(p, p), near(p, p)),
            (whole(p, p), near(p, p)),
        ] + [(whole(p, p), near(p, p))] * 6,
        [
            pltpu.VMEM((2 * p, p), F32),
            pltpu.VMEM((p, p), F32),
            pltpu.VMEM((2 * p, p), BF16),
            pltpu.VMEM((p, p), BF16),
            pltpu.VMEM((p, p), BF16),
            pltpu.VMEM((k, p), BF16),
            pltpu.VMEM((p, p), BF16),
            pltpu.VMEM((6 * p, p), F32),
            pltpu.VMEM((p, p), F32),
        ],
        2 * n * p * (k + 15 * p), n * (2 * k + 18 * p),
        core, own, other, z, h, t, earlier, u, w, later,
    )
    q_one, w2, r_one, expected = got[:4]
    q_one, w2 = fixed(q_one), fixed(w2)
    own, other = summed(
        [exchange(x, "grp", 0) for x in got[4:7]], got[7:], 2,
        [turned(bits, t) for t in range(3)],
    )

    return tuple(call(
        lambda *r: last_kernel(3, *r), "last", 28,
        [smem()] + [whole(p, p)] * 8 + [tiled(p), tiled(2 * p)],
        [
            (tiled(2 * p), shape(n, 2 * p, dtype=BF16)),
            (whole(2, p, p), shape(2, p, p)),
            (whole(2 * p, 2 * p), shape(2 * p, 2 * p)),
        ],
        [
            pltpu.VMEM((6 * p, p), F32),
            pltpu.VMEM((p, p), F32),
            pltpu.VMEM((p, p), F32),
            pltpu.VMEM((2 * p, p), BF16),
            pltpu.VMEM((p, p), BF16),
            pltpu.VMEM((p, p), BF16),
        ],
        2 * n * p * 4 * p, n * 10 * p,
        core, *own, *other, expected, r_one, q_one, w2,
    ))


def solution(mesh):
    spec = P(("rows", "grp"), None)
    return jax.shard_map(
        body,
        mesh=mesh,
        in_specs=(spec, spec, spec),
        out_specs=(spec, P(), P()),
        check_vma=False,
    )
```

```python
import jax
import jax.numpy as jnp
from jax import lax
from jax.experimental import pallas as pl
from jax.experimental.pallas import tpu as pltpu
from jax.sharding import PartitionSpec as P

AXES = ("rows", "grp")
HIGHEST = lax.Precision.HIGHEST
BF16 = jnp.bfloat16
F32 = jnp.float32
MIB = 2**20


def dot(a, b):
    return jnp.dot(a, b, preferred_element_type=F32)


def full(a, b):
    return jnp.dot(a, b, precision=HIGHEST, preferred_element_type=F32)


def wide(x):
    return x.astype(F32)


def split(x):
    high = x.astype(BF16)
    return high, (x - wide(high)).astype(BF16)


def thrice(a, b):
    return dot(a[0], b[0]) + dot(a[0], b[1]) + dot(a[1], b[0])


def factor_tile(groups, emit):
    count = len(groups)
    lane = lax.broadcasted_iota(jnp.int32, (8, 128), 1)
    sub = lax.broadcasted_iota(jnp.int32, (8, 128), 0)
    rows = list(groups)
    for k in range(count):
        base = 8 * k
        strip = rows[k]
        inside = (lane >= base) & (lane < base + 8)
        eye = jnp.where(lane == base + sub, 1.0, 0.0).astype(F32)
        mixed = jnp.where(inside, eye, strip)
        cols = [jnp.broadcast_to(strip[:, base + j:base + j + 1], (8, 128)) for j in range(8)]
        entry = {}
        for j in range(8):
            for i in range(j, 8):
                entry[i, j] = jnp.broadcast_to(cols[j][i:i + 1, :], (8, 128))
        scale = []
        low = {}
        for j in range(8):
            r = lax.rsqrt(entry[j, j])
            scale.append(r)
            for i in range(j + 1, 8):
                low[i, j] = entry[i, j] * r
            for c in range(j + 1, 8):
                for i in range(c, 8):
                    entry[i, c] = entry[i, c] - low[i, j] * low[c, j]
        upper, both = [], []
        for j in range(8):
            u = jnp.broadcast_to(strip[j:j + 1, :], (8, 128))
            v = jnp.broadcast_to(mixed[j:j + 1, :], (8, 128))
            for i in range(j):
                u = u - low[j, i] * upper[i]
                v = v - low[j, i] * both[i]
            upper.append(u * scale[j])
            both.append(v * scale[j])
        out_r = upper[0]
        out_m = both[0]
        for j in range(1, 8):
            out_r = jnp.where(sub == j, upper[j], out_r)
            out_m = jnp.where(sub == j, both[j], out_m)
        emit(
            k,
            jnp.where(lane >= base + sub, out_r, 0.0),
            jnp.where(lane <= base + sub, out_m, 0.0),
        )
        for g in range(k + 1, count):
            w = rows[g]
            new = jnp.where(inside, 0.0, w)
            left = []
            for j in range(8):
                c = jnp.broadcast_to(w[:, base + j:base + j + 1], (8, 128))
                for i in range(j):
                    c = c - left[i] * low[j, i]
                c = c * scale[j]
                left.append(c)
                new = new - c * both[j]
            rows[g] = new


def factor(r_ref, m_ref):
    n = r_ref.shape[0]
    h = 128

    def step(t, carry):
        top = pl.multiple_of(t * h, h)
        groups = [r_ref[pl.ds(pl.multiple_of(top + 8 * g, 8), 8), pl.ds(top, h)] for g in range(h // 8)]

        def emit(k, r, m):
            at = pl.ds(pl.multiple_of(top + 8 * k, 8), 8)
            r_ref[at, pl.ds(top, h)] = r
            m_ref[at, pl.ds(top, h)] = m

        factor_tile(groups, emit)

        @pl.when(t == 0)
        def _():
            inv = m_ref[:h, :h]
            u = full(inv, r_ref[:h, h:])
            ut = u.T
            r_ref[:h, h:] = u
            r_ref[h:, h:] = r_ref[h:, h:] - full(ut, u)
            m_ref[h:, :h] = full(ut, inv)
            r_ref[h:, :h] = jnp.zeros((n - h, h), F32)
            m_ref[:h, h:] = jnp.zeros((h, n - h), F32)

        return carry

    lax.fori_loop(0, n // h, step, 0)
    m_ref[h:, :h] = -full(m_ref[h:, h:], m_ref[h:, :h])


def begin(copies, sems):
    for n, (source, target) in enumerate(copies):
        pltpu.make_async_copy(source, target, sems.at[n]).start()


def finish(copies, sems):
    for n, (source, target) in enumerate(copies):
        pltpu.make_async_copy(source, target, sems.at[n]).wait()


def places(core_ref, own, other, total_ref):
    mine = core_ref[0]
    copies = []
    at = 0
    for a, b in zip(own, other):
        h = a.shape[0]
        copies.append((a, total_ref.at[pl.ds(pl.multiple_of(at + mine * h, 8), h)]))
        copies.append((b, total_ref.at[pl.ds(pl.multiple_of(at + (1 - mine) * h, 8), h)]))
        at += 2 * h
    return copies


def tile_rows(i, tile):
    return pl.ds(pl.multiple_of(i * tile, tile), tile)


def at_tile(pairs, i, tile):
    rows = tile_rows(i, tile)
    return [(a.at[rows], b.at[rows]) for a, b in pairs]


def deal(core_ref, total_ref, scale, sends, keeps):
    mine = core_ref[0]
    at = 0
    for send, keep in zip(sends, keeps):
        h = send.shape[0]
        keep[...] = total_ref[pl.ds(pl.multiple_of(at + mine * h, 8), h)] * scale
        send[...] = total_ref[pl.ds(pl.multiple_of(at + (1 - mine) * h, 8), h)] * scale
        at += 2 * h


def cross_kernel(parts, scale, core_ref, e_ref, x_ref, *refs):
    sends, keeps, acc = refs[:parts], refs[parts:2 * parts], refs[-1]
    k = e_ref.shape[1]
    p = x_ref.shape[1] // 2
    step = pl.program_id(0)

    @pl.when(step == 0)
    def _():
        acc[...] = jnp.zeros_like(acc)

    et = e_ref[...].T
    at = 0
    for c in range(2):
        acc[at:at + k] += dot(et, x_ref[:, c * p:(c + 1) * p])
        at += k
    for j in range(k // p):
        m = (j + 1) * p
        acc[at:at + m] += dot(et[:m], e_ref[:, j * p:(j + 1) * p])
        at += m

    @pl.when(step == pl.num_programs(0) - 1)
    def _():
        deal(core_ref, acc, scale, sends, keeps)


def first_kernel(parts, tile, scale, core_ref, *refs):
    own, other = refs[:parts], refs[parts:2 * parts]
    (e_in, x_in, u_out, w_out, z_out, h_out, t_ref, send, keep,
     total, e_ref, x_ref, u_ref, w_ref, z_ref, h_ref, b_ref, offh, offl, acc, hl,
     sum_sems, in_sems, out_sems, small_sems) = refs[2 * parts:]
    n, k = e_ref.shape
    p = u_ref.shape[1]
    tiles = n // tile
    sums = places(core_ref, own, other, total)
    inputs = [(e_in, e_ref), (x_in, x_ref)]
    outputs = [(u_ref, u_out), (w_ref, w_out)]
    small = [(z_ref, z_out), (h_ref, h_out)]
    begin(sums, sum_sems)
    for i in range(tiles):
        begin(at_tile(inputs, i, tile), in_sems.at[i])
    acc[...] = jnp.zeros_like(acc)
    hl[...] = jnp.zeros_like(hl)
    finish(sums, sum_sems)

    at = 2 * k
    for j in range(k // p):
        cols = slice(j * p, (j + 1) * p)
        for i in range(j + 1):
            block = total[at:at + p]
            at += p
            if i == j:
                a = lax.broadcasted_iota(jnp.int32, (p, p), 0)
                b = lax.broadcasted_iota(jnp.int32, (p, p), 1)
                block = block - jnp.where(a == b, 1.0, 0.0)
            high, low = split(block)
            rows = slice(i * p, (i + 1) * p)
            offh[rows, cols] = high
            offl[rows, cols] = low
            if i < j:
                offh[cols, rows] = high.T
                offl[cols, rows] = low.T
    for c in range(2):
        coef = total[c * k:(c + 1) * k]
        b = coef.astype(BF16)
        b_ref[:, c * p:(c + 1) * p] = b
        after = (coef - wide(b)) - dot(offh[...], b) - dot(offl[...], b)
        if c == 0:
            sb = after.astype(BF16)
            b_ref[:, 2 * p:] = sb
            against = (after - wide(sb)) - dot(offh[...], sb) - dot(offl[...], sb)
            h_ref[...] = against
        else:
            z_ref[...] = after
            high, low = split(against.T)
            t_ref[...] = dot(high, b) + dot(low, b)
    begin(small, small_sems)

    def step(i, carry):
        rows = tile_rows(i, tile)
        finish(at_tile(inputs, i, tile), in_sems.at[i])
        t = dot(e_ref[rows, :], b_ref[...])
        once = wide((wide(x_ref[rows, :p]) - t[:, :p]).astype(BF16))
        x_two = x_ref[rows, p:]
        u_ref[rows, :] = wide(x_two) - t[:, p:2 * p]
        high, low = split(once - t[:, 2 * p:])
        w_ref[rows, :p] = high
        w_ref[rows, p:] = low
        begin(at_tile(outputs, i, tile), out_sems.at[i])
        both = jnp.concatenate([high.T, low.T], axis=0)
        square = dot(both, high)
        acc[:p] += square[:p]
        hl[...] += square[p:]
        other_two = dot(both, x_two)
        acc[p:] += other_two[:p] + other_two[p:]
        return carry

    lax.fori_loop(0, tiles, step, 0)
    acc[:p] = acc[:p] + hl[...] + hl[...].T
    deal(core_ref, acc, scale, [send], [keep])
    for i in range(tiles):
        finish(at_tile(outputs, i, tile), out_sems.at[i])
    finish(small, small_sems)


def second_kernel(parts, tile, scale, core_ref, own, other, z_in, h_in, t_ref, e_in, u_in, w_in, l_in, *refs):
    q_out, w2_out, r_ref, x_ref = refs[:4]
    sends, keeps = refs[4:4 + parts], refs[4 + parts:4 + 2 * parts]
    (total, z_ref, h_ref, e_ref, u_ref, w_ref, l_ref, q_ref, w2_ref, m_ref, ih, il, db, ub, lb, acc, hl,
     sum_sems, small_sems, in_sems, out_sems) = refs[4 + 2 * parts:]
    p = r_ref.shape[0]
    n = e_ref.shape[0]
    tiles = n // tile
    sums = places(core_ref, [own], [other], total)
    small = [(z_in, z_ref), (h_in, h_ref)]
    inputs = [(e_in, e_ref), (u_in, u_ref), (w_in, w_ref), (l_in, l_ref)]
    outputs = [(q_ref, q_out), (w2_ref, w2_out)]
    begin(sums, sum_sems)
    begin(small, small_sems)
    for i in range(tiles):
        begin(at_tile(inputs, i, tile), in_sems.at[i])
    acc[...] = jnp.zeros_like(acc)
    hl[...] = jnp.zeros_like(hl)
    finish(sums, sum_sems)

    r_ref[...] = total[:p]
    factor(r_ref, m_ref)
    inv = m_ref[...]
    high, low = split(inv.T)
    ih[:p] = high
    ih[p:] = high
    il[...] = low
    d = full(inv, total[p:])
    d_b = d.astype(BF16)
    db[...] = d_b
    finish(small, small_sems)
    inv_s = split(inv)
    against = split(h_ref[...])
    at = split(h_ref[...].T)
    turned = split(dot(high, d_b) + dot(low, d_b))
    upper = (z_ref[...] - thrice(against, turned)).astype(BF16)
    ub[...] = upper
    lower = (d - wide(d_b)) - thrice(inv_s, split(t_ref[...]))
    lower_b = lower.astype(BF16)
    lb[...] = lower_b
    x_ref[...] = (lower - wide(lower_b)) - thrice(inv_s, split(dot(at[0], upper) + dot(at[1], upper)))

    def step(i, carry):
        rows = tile_rows(i, tile)
        finish(at_tile(inputs, i, tile), in_sems.at[i])
        q = (dot(w_ref[rows, :], ih[...]) + dot(w_ref[rows, :p], il[...])).astype(BF16)
        q_ref[rows, :] = q
        once = wide((u_ref[rows, :] - dot(q, db[...])).astype(BF16))
        high, low = split(once - dot(e_ref[rows, :], ub[...]) - dot(q, lb[...]))
        w2_ref[rows, :p] = high
        w2_ref[rows, p:] = low
        begin(at_tile(outputs, i, tile), out_sems.at[i])
        qt = q.T
        left = jnp.concatenate([high.T, low.T, qt], axis=0)
        square = dot(left, high)
        acc[:p] += square[:p]
        hl[...] += square[p:2 * p]
        acc[p:2 * p] += square[2 * p:] + dot(qt, low)
        for c in range(2):
            mixed = dot(left, l_ref[rows, c * p:(c + 1) * p])
            acc[(2 + c) * p:(3 + c) * p] += mixed[:p] + mixed[p:2 * p]
            acc[(4 + c) * p:(5 + c) * p] += mixed[2 * p:]
        return carry

    lax.fori_loop(0, tiles, step, 0)
    acc[:p] = acc[:p] + hl[...] + hl[...].T
    deal(core_ref, acc, scale, sends, keeps)
    for i in range(tiles):
        finish(at_tile(outputs, i, tile), out_sems.at[i])


def last_kernel(parts, tile, core_ref, *refs):
    own, other = refs[:parts], refs[parts:2 * parts]
    (x_ref, r1_ref, q_in, w_in, basis_out, factors, shift,
     total, q_ref, w_ref, basis, r_ref, m_ref, ih, il, back, sum_sems, in_sems, out_sems) = refs[2 * parts:]
    p = r_ref.shape[0]
    tiles = q_ref.shape[0] // tile
    sums = places(core_ref, own, other, total)
    inputs = [(q_in, q_ref), (w_in, w_ref)]
    outputs = [(basis, basis_out)]
    begin(sums, sum_sems)
    for i in range(tiles):
        begin(at_tile(inputs, i, tile), in_sems.at[i])
    finish(sums, sum_sems)

    res = total[p:2 * p]
    off = res - x_ref[...]
    off_b = off.astype(BF16)
    offt = off.T.astype(BF16)
    cut = dot(offt, res.astype(BF16))
    r_ref[...] = total[:p] - cut - cut.T + dot(offt, off_b)
    factor(r_ref, m_ref)
    inv = m_ref[...]
    high, low = split(inv.T)
    ih[:p] = high
    ih[p:] = high
    il[...] = low
    back[...] = dot(off_b, high).astype(BF16)

    def step(i, carry):
        rows = tile_rows(i, tile)
        finish(at_tile(inputs, i, tile), in_sems.at[i])
        q = dot(w_ref[rows, :], ih[...]) + dot(w_ref[rows, :p], il[...]) - dot(q_ref[rows, :], back[...])
        basis[rows, :p] = q_ref[rows, :]
        basis[rows, p:] = q.astype(BF16)
        begin(at_tile(outputs, i, tile), out_sems.at[i])
        return carry

    lax.fori_loop(0, tiles, step, 0)
    inv_s = split(m_ref[...])
    factors[0] = r1_ref[...]
    factors[1] = r_ref[...]
    for c in range(2):
        cols = slice(c * p, (c + 1) * p)
        early = total[(4 + c) * p:(5 + c) * p]
        shift[:p, cols] = early
        late = total[(2 + c) * p:(3 + c) * p] - dot(offt, early.astype(BF16))
        shift[p:, cols] = thrice(inv_s, split(late))
    for i in range(tiles):
        finish(at_tile(outputs, i, tile), out_sems.at[i])


def exchange(x, axis, bit):
    size = lax.axis_size(axis)
    return lax.ppermute(x, axis, [(i, i ^ (1 << bit)) for i in range(size)])


def summed(sends, keeps, tail):
    bits = list(range(lax.axis_size("rows").bit_length() - 1))
    turn, last = bits[:-1], bits[-1:]
    orders = [turn[n % len(turn):] + turn[:n % len(turn)] + last for n in range(len(sends))]
    me = lax.axis_index("rows")
    parts = [keep + exchange(send, "grp", 0) for send, keep in zip(sends, keeps)]
    halving = len(bits) - tail
    for step in range(halving):
        for n, order in enumerate(orders):
            x, bit = parts[n], order[step]
            half = x.shape[0] // 2
            mine = (me >> bit) & 1
            send = lax.dynamic_slice_in_dim(x, (1 - mine) * half, half, 0)
            keep = lax.dynamic_slice_in_dim(x, mine * half, half, 0)
            parts[n] = keep + exchange(send, "rows", bit)
    for step in range(halving, len(bits)):
        for n, order in enumerate(orders):
            parts[n] = parts[n] + exchange(parts[n], "rows", order[step])
    for step in reversed(range(halving)):
        for n, order in enumerate(orders):
            x, bit = parts[n], order[step]
            other = exchange(x, "rows", bit)
            mine = ((me >> bit) & 1) == 1
            parts[n] = jnp.concatenate([jnp.where(mine, other, x), jnp.where(mine, x, other)], axis=0)
    return parts, [exchange(x, "grp", 0) for x in parts]


def summed_at_once(send, keep):
    size = lax.axis_size("rows")
    x = keep + exchange(send, "grp", 0)
    got = lax.all_to_all(x, "rows", 0, 0, tiled=True)
    mine = got.reshape(size, x.shape[0] // size, x.shape[1]).sum(0)
    same = jnp.broadcast_to(mine[None], (size,) + mine.shape).reshape(x.shape)
    x = lax.all_to_all(same, "rows", 0, 0, tiled=True)
    return x, exchange(x, "grp", 0)


def body(earlier, snapshots, later):
    n, k = earlier.shape
    p = snapshots.shape[1] // 2
    devices = lax.axis_size(AXES)
    scale = 1.0 / (n * devices)
    core = lax.axis_index("grp").astype(jnp.int32).reshape(1)
    blocks = k // p
    rows = (2 * blocks + blocks * (blocks + 1) // 2) * p
    unit = 2 * devices * 8
    parts = 3 if rows % (3 * unit) == 0 else 1
    tile = 1024 if n % 1024 == 0 else n

    def smem():
        return pl.BlockSpec(memory_space=pltpu.SMEM)

    def whole(*shape):
        return pl.BlockSpec(shape, lambda i: (0,) * len(shape))

    def tiled(cols):
        return pl.BlockSpec((tile, cols), lambda i: (i, 0))

    def shape(*dims, dtype=F32):
        return jax.ShapeDtypeStruct(dims, dtype)

    def near(*dims, dtype=F32):
        return pltpu.VMEM(dims, dtype)

    def far(*dims, dtype=F32):
        return pltpu.HBM(dims, dtype)

    apart = pl.BlockSpec(memory_space=pl.ANY)
    inside = pl.BlockSpec(memory_space=pltpu.VMEM)

    def fixed(x):
        return pltpu.with_memory_space_constraint(x, pltpu.HBM)

    earlier, snapshots, later = fixed(earlier), fixed(snapshots), fixed(later)

    def call(kernel, name, room, ins, outs, scratch, flops, size, *args, grid=None):
        return pl.pallas_call(
            kernel,
            grid=(n // tile,) if grid is None else grid,
            in_specs=[s for s in ins],
            out_specs=[s for s, _ in outs],
            out_shape=[s for _, s in outs],
            scratch_shapes=scratch,
            name=name,
            cost_estimate=pl.CostEstimate(flops=flops, bytes_accessed=size, transcendentals=0),
            compiler_params=pltpu.CompilerParams(
                vmem_limit_bytes=room * MIB
            ),
        )(*args)

    half = rows // parts // 2
    halves = [(whole(half, p), near(half, p))] * (2 * parts)
    got = call(
        lambda *r: cross_kernel(parts, scale, *r), "cross", 32,
        [smem(), tiled(k), tiled(2 * p)],
        halves,
        [pltpu.VMEM((rows, p), F32)],
        2 * n * rows * p, 2 * n * (k + 2 * p),
        core, earlier, snapshots,
    )
    own, other = summed(got[:parts], got[parts:], 1)

    tiles = n // tile
    dma = pltpu.SemaphoreType.DMA

    def held(*dims, dtype=F32):
        return pltpu.VMEM(dims, dtype)

    u, w, z, h, t, send, keep = call(
        lambda *r: first_kernel(parts, tile, scale, *r), "first", 50,
        [smem()] + [apart] * (2 * parts + 2),
        [
            (apart, far(n, p)),
            (apart, far(n, 2 * p, dtype=BF16)),
            (apart, far(k, p)),
            (apart, far(k, p)),
            (inside, near(p, p)),
            (inside, near(p, p)),
            (inside, near(p, p)),
        ],
        [
            held(rows, p),
            held(n, k, dtype=BF16),
            held(n, 2 * p, dtype=BF16),
            held(n, p),
            held(n, 2 * p, dtype=BF16),
            held(k, p),
            held(k, p),
            held(k, 3 * p, dtype=BF16),
            held(k, k, dtype=BF16),
            held(k, k, dtype=BF16),
            held(2 * p, p),
            held(p, p),
            dma((2 * parts,)), dma((tiles, 2)), dma((tiles, 2)), dma((2,)),
        ],
        2 * n * p * (3 * k + 4 * p) + 12 * k * k * p, n * (2 * k + 12 * p),
        core, *own, *other, earlier, snapshots, grid=(),
    )
    own, other = summed_at_once(send, keep)

    got = call(
        lambda *r: second_kernel(3, tile, scale, *r), "second", 46,
        [smem()] + [apart] * 4 + [inside] + [apart] * 4,
        [
            (apart, far(n, p, dtype=BF16)),
            (apart, far(n, 2 * p, dtype=BF16)),
            (inside, near(p, p)),
            (inside, near(p, p)),
        ] + [(inside, near(p, p))] * 6,
        [
            held(2 * p, p),
            held(k, p),
            held(k, p),
            held(n, k, dtype=BF16),
            held(n, p),
            held(n, 2 * p, dtype=BF16),
            held(n, 2 * p, dtype=BF16),
            held(n, p, dtype=BF16),
            held(n, 2 * p, dtype=BF16),
            held(p, p),
            held(2 * p, p, dtype=BF16),
            held(p, p, dtype=BF16),
            held(p, p, dtype=BF16),
            held(k, p, dtype=BF16),
            held(p, p, dtype=BF16),
            held(6 * p, p),
            held(p, p),
            dma((2,)), dma((2,)), dma((tiles, 4)), dma((tiles, 2)),
        ],
        2 * n * p * (k + 15 * p), n * (2 * k + 18 * p),
        core, own, other, fixed(z), fixed(h), t, earlier, fixed(u), fixed(w), later, grid=(),
    )
    q_one, w2, r_one, expected = got[:4]
    own, other = summed(got[4:7], got[7:], 2)

    return tuple(call(
        lambda *r: last_kernel(3, tile, *r), "last", 26,
        [smem()] + [apart] * 6 + [inside] * 2 + [apart] * 2,
        [
            (apart, far(n, 2 * p, dtype=BF16)),
            (inside, shape(2, p, p)),
            (inside, shape(2 * p, 2 * p)),
        ],
        [
            held(6 * p, p),
            held(n, p, dtype=BF16),
            held(n, 2 * p, dtype=BF16),
            held(n, 2 * p, dtype=BF16),
            held(p, p),
            held(p, p),
            held(2 * p, p, dtype=BF16),
            held(p, p, dtype=BF16),
            held(p, p, dtype=BF16),
            dma((6,)), dma((tiles, 2)), dma((tiles, 1)),
        ],
        2 * n * p * 4 * p, n * 10 * p,
        core, *own, *other, expected, r_one, fixed(q_one), fixed(w2), grid=(),
    ))


def solution(mesh):
    spec = P(("rows", "grp"), None)
    return jax.shard_map(
        body,
        mesh=mesh,
        in_specs=(spec, spec, spec),
        out_specs=(spec, P(), P()),
        check_vma=False,
    )
```

```python
import jax
import jax.numpy as jnp
from jax import lax
from jax.experimental import pallas as pl
from jax.experimental.pallas import tpu as pltpu
from jax.sharding import PartitionSpec as P

AXES = ("rows", "grp")
HIGHEST = lax.Precision.HIGHEST
BF16 = jnp.bfloat16
F32 = jnp.float32
MIB = 2**20


def dot(a, b):
    return jnp.dot(a, b, preferred_element_type=F32)


def full(a, b):
    return jnp.dot(a, b, precision=HIGHEST, preferred_element_type=F32)


def wide(x):
    return x.astype(F32)


def split(x):
    high = x.astype(BF16)
    return high, (x - wide(high)).astype(BF16)


def thrice(a, b):
    return dot(a[0], b[0]) + dot(a[0], b[1]) + dot(a[1], b[0])


def factor_tile(groups, emit):
    count = len(groups)
    lane = lax.broadcasted_iota(jnp.int32, (8, 128), 1)
    sub = lax.broadcasted_iota(jnp.int32, (8, 128), 0)
    rows = list(groups)
    for k in range(count):
        base = 8 * k
        strip = rows[k]
        inside = (lane >= base) & (lane < base + 8)
        eye = jnp.where(lane == base + sub, 1.0, 0.0).astype(F32)
        mixed = jnp.where(inside, eye, strip)
        cols = [jnp.broadcast_to(strip[:, base + j:base + j + 1], (8, 128)) for j in range(8)]
        entry = {}
        for j in range(8):
            for i in range(j, 8):
                entry[i, j] = jnp.broadcast_to(cols[j][i:i + 1, :], (8, 128))
        scale = []
        low = {}
        for j in range(8):
            r = lax.rsqrt(entry[j, j])
            scale.append(r)
            for i in range(j + 1, 8):
                low[i, j] = entry[i, j] * r
            for c in range(j + 1, 8):
                for i in range(c, 8):
                    entry[i, c] = entry[i, c] - low[i, j] * low[c, j]
        upper, both = [], []
        for j in range(8):
            u = jnp.broadcast_to(strip[j:j + 1, :], (8, 128))
            v = jnp.broadcast_to(mixed[j:j + 1, :], (8, 128))
            for i in range(j):
                u = u - low[j, i] * upper[i]
                v = v - low[j, i] * both[i]
            upper.append(u * scale[j])
            both.append(v * scale[j])
        out_r = upper[0]
        out_m = both[0]
        for j in range(1, 8):
            out_r = jnp.where(sub == j, upper[j], out_r)
            out_m = jnp.where(sub == j, both[j], out_m)
        emit(
            k,
            jnp.where(lane >= base + sub, out_r, 0.0),
            jnp.where(lane <= base + sub, out_m, 0.0),
        )
        for g in range(k + 1, count):
            w = rows[g]
            new = jnp.where(inside, 0.0, w)
            left = []
            for j in range(8):
                c = jnp.broadcast_to(w[:, base + j:base + j + 1], (8, 128))
                for i in range(j):
                    c = c - left[i] * low[j, i]
                c = c * scale[j]
                left.append(c)
                new = new - c * both[j]
            rows[g] = new


def factor(r_ref, m_ref):
    n = r_ref.shape[0]
    h = 128

    def step(t, carry):
        top = pl.multiple_of(t * h, h)
        groups = [r_ref[pl.ds(pl.multiple_of(top + 8 * g, 8), 8), pl.ds(top, h)] for g in range(h // 8)]

        def emit(k, r, m):
            at = pl.ds(pl.multiple_of(top + 8 * k, 8), 8)
            r_ref[at, pl.ds(top, h)] = r
            m_ref[at, pl.ds(top, h)] = m

        factor_tile(groups, emit)

        @pl.when(t == 0)
        def _():
            inv = m_ref[:h, :h]
            u = full(inv, r_ref[:h, h:])
            ut = u.T
            r_ref[:h, h:] = u
            r_ref[h:, h:] = r_ref[h:, h:] - full(ut, u)
            m_ref[h:, :h] = full(ut, inv)
            r_ref[h:, :h] = jnp.zeros((n - h, h), F32)
            m_ref[:h, h:] = jnp.zeros((h, n - h), F32)

        return carry

    lax.fori_loop(0, n // h, step, 0)
    m_ref[h:, :h] = -full(m_ref[h:, h:], m_ref[h:, :h])


def begin(copies, sems):
    for n, (source, target) in enumerate(copies):
        pltpu.make_async_copy(source, target, sems.at[n]).start()


def finish(copies, sems):
    for n, (source, target) in enumerate(copies):
        pltpu.make_async_copy(source, target, sems.at[n]).wait()


def places(core_ref, own, other, total_ref):
    mine = core_ref[0]
    copies = []
    at = 0
    for a, b in zip(own, other):
        h = a.shape[0]
        copies.append((a, total_ref.at[pl.ds(pl.multiple_of(at + mine * h, 8), h)]))
        copies.append((b, total_ref.at[pl.ds(pl.multiple_of(at + (1 - mine) * h, 8), h)]))
        at += 2 * h
    return copies


def tile_rows(i, tile):
    return pl.ds(pl.multiple_of(i * tile, tile), tile)


def at_tile(pairs, i, tile):
    rows = tile_rows(i, tile)
    return [(a.at[rows], b.at[rows]) for a, b in pairs]


def deal(core_ref, total_ref, scale, sends, keeps):
    mine = core_ref[0]
    at = 0
    for send, keep in zip(sends, keeps):
        h = send.shape[0]
        keep[...] = total_ref[pl.ds(pl.multiple_of(at + mine * h, 8), h)] * scale
        send[...] = total_ref[pl.ds(pl.multiple_of(at + (1 - mine) * h, 8), h)] * scale
        at += 2 * h


def cross_kernel(parts, tile, core_ref, e_in, x_in, *refs):
    sends, keeps = refs[:parts], refs[parts:2 * parts]
    e_ref, x_ref, acc, in_sems, out_sems = refs[2 * parts:]
    n, k = e_ref.shape
    p = x_ref.shape[1] // 2
    tiles = n // tile
    inputs = [(e_in, e_ref), (x_in, x_ref)]
    outputs = []
    for n, (send, keep) in enumerate(zip(sends, keeps)):
        h = send.shape[0]
        first, last = core_ref[0] * h + 2 * n * h, (1 - core_ref[0]) * h + 2 * n * h
        outputs.append([
            (acc.at[pl.ds(pl.multiple_of(last, 8), h)], send),
            (acc.at[pl.ds(pl.multiple_of(first, 8), h)], keep),
        ])
    for i in range(tiles):
        begin(at_tile(inputs, i, tile), in_sems.at[i])
    sent = 0
    for i in range(tiles):
        finish(at_tile(inputs, i, tile), in_sems.at[i])
        rows = slice(i * tile, (i + 1) * tile)
        et = e_ref[rows, :].T
        jobs = [(k, x_ref, c) for c in range(2)] + [((j + 1) * p, e_ref, j) for j in range(k // p)]
        at = 0
        for m, right, c in jobs:
            got = dot(et[:m], right[rows, c * p:(c + 1) * p])
            acc[at:at + m] = got if i == 0 else acc[at:at + m] + got
            at += m
            while i == tiles - 1 and sent < parts and at >= 2 * (sent + 1) * sends[0].shape[0]:
                begin(outputs[sent], out_sems.at[sent])
                sent += 1
    for n in range(parts):
        finish(outputs[n], out_sems.at[n])


def first_kernel(parts, tile, scale, core_ref, *refs):
    own, other = refs[:parts], refs[parts:2 * parts]
    (e_in, x_in, u_out, w_out, z_out, h_out, t_ref, send, keep,
     total, e_ref, x_ref, u_ref, w_ref, z_ref, h_ref, b_ref, offh, offl, acc, hl,
     sum_sems, in_sems, out_sems, small_sems) = refs[2 * parts:]
    n, k = e_ref.shape
    p = u_ref.shape[1]
    tiles = n // tile
    sums = places(core_ref, own, other, total)
    inputs = [(e_in, e_ref), (x_in, x_ref)]
    outputs = [(u_ref, u_out), (w_ref, w_out)]
    small = [(z_ref, z_out), (h_ref, h_out)]
    begin(sums, sum_sems)
    for i in range(tiles):
        begin(at_tile(inputs, i, tile), in_sems.at[i])
    acc[...] = jnp.zeros_like(acc)
    hl[...] = jnp.zeros_like(hl)
    finish(sums, sum_sems)

    at = 2 * k
    for j in range(k // p):
        cols = slice(j * p, (j + 1) * p)
        for i in range(j + 1):
            block = total[at:at + p] * scale
            at += p
            if i == j:
                a = lax.broadcasted_iota(jnp.int32, (p, p), 0)
                b = lax.broadcasted_iota(jnp.int32, (p, p), 1)
                block = block - jnp.where(a == b, 1.0, 0.0)
            high, low = split(block)
            rows = slice(i * p, (i + 1) * p)
            offh[rows, cols] = high
            offl[rows, cols] = low
            if i < j:
                offh[cols, rows] = high.T
                offl[cols, rows] = low.T
    for c in range(2):
        coef = total[c * k:(c + 1) * k] * scale
        b = coef.astype(BF16)
        b_ref[:, c * p:(c + 1) * p] = b
        after = (coef - wide(b)) - dot(offh[...], b) - dot(offl[...], b)
        if c == 0:
            sb = after.astype(BF16)
            b_ref[:, 2 * p:] = sb
            against = (after - wide(sb)) - dot(offh[...], sb) - dot(offl[...], sb)
            h_ref[...] = against
        else:
            z_ref[...] = after
            high, low = split(against.T)
            t_ref[...] = dot(high, b) + dot(low, b)
    begin(small, small_sems)

    for i in range(tiles):
        finish(at_tile(inputs, i, tile), in_sems.at[i])
    for i in range(tiles):
        rows = slice(i * tile, (i + 1) * tile)
        t = dot(e_ref[rows, :], b_ref[...])
        once = wide((wide(x_ref[rows, :p]) - t[:, :p]).astype(BF16))
        x_two = x_ref[rows, p:]
        u_ref[rows, :] = wide(x_two) - t[:, p:2 * p]
        high, low = split(once - t[:, 2 * p:])
        w_ref[rows, :p] = high
        w_ref[rows, p:] = low
        begin(at_tile(outputs, i, tile), out_sems.at[i])
        both = jnp.concatenate([high.T, low.T], axis=0)
        square = dot(both, high)
        acc[:p] += square[:p]
        hl[...] += square[p:]
        other_two = dot(both, x_two)
        acc[p:] += other_two[:p] + other_two[p:]
    acc[:p] = acc[:p] + hl[...] + hl[...].T
    deal(core_ref, acc, scale, [send], [keep])
    for i in range(tiles):
        finish(at_tile(outputs, i, tile), out_sems.at[i])
    finish(small, small_sems)


def second_kernel(parts, tile, scale, core_ref, own, other, z_in, h_in, t_ref, e_in, u_in, w_in, l_in, *refs):
    q_out, w2_out, r_ref, x_ref = refs[:4]
    sends, keeps = refs[4:4 + parts], refs[4 + parts:4 + 2 * parts]
    (total, z_ref, h_ref, e_ref, u_ref, w_ref, l_ref, q_ref, w2_ref, m_ref, ih, il, db, ub, lb, acc, hl,
     sum_sems, small_sems, in_sems, out_sems) = refs[4 + 2 * parts:]
    p = r_ref.shape[0]
    n = e_ref.shape[0]
    tiles = n // tile
    sums = places(core_ref, [own], [other], total)
    small = [(z_in, z_ref), (h_in, h_ref)]
    inputs = [(e_in, e_ref), (u_in, u_ref), (w_in, w_ref), (l_in, l_ref)]
    outputs = [(q_ref, q_out), (w2_ref, w2_out)]
    begin(sums, sum_sems)
    begin(small, small_sems)
    for i in range(tiles):
        begin(at_tile(inputs, i, tile), in_sems.at[i])
    acc[...] = jnp.zeros_like(acc)
    hl[...] = jnp.zeros_like(hl)
    finish(sums, sum_sems)

    r_ref[...] = total[:p]
    factor(r_ref, m_ref)
    inv = m_ref[...]
    high, low = split(inv.T)
    ih[:p] = high
    ih[p:] = high
    il[...] = low
    d = full(inv, total[p:])
    d_b = d.astype(BF16)
    db[...] = d_b
    finish(small, small_sems)
    inv_s = split(inv)
    against = split(h_ref[...])
    at = split(h_ref[...].T)
    turned = split(dot(high, d_b) + dot(low, d_b))
    upper = (z_ref[...] - thrice(against, turned)).astype(BF16)
    ub[...] = upper
    lower = (d - wide(d_b)) - thrice(inv_s, split(t_ref[...]))
    lower_b = lower.astype(BF16)
    lb[...] = lower_b
    x_ref[...] = (lower - wide(lower_b)) - thrice(inv_s, split(dot(at[0], upper) + dot(at[1], upper)))

    for i in range(tiles):
        finish(at_tile(inputs, i, tile), in_sems.at[i])
    for i in range(tiles):
        rows = slice(i * tile, (i + 1) * tile)
        q = (dot(w_ref[rows, :], ih[...]) + dot(w_ref[rows, :p], il[...])).astype(BF16)
        q_ref[rows, :] = q
        once = wide((u_ref[rows, :] - dot(q, db[...])).astype(BF16))
        high, low = split(once - dot(e_ref[rows, :], ub[...]) - dot(q, lb[...]))
        w2_ref[rows, :p] = high
        w2_ref[rows, p:] = low
        begin(at_tile(outputs, i, tile), out_sems.at[i])
        qt = q.T
        left = jnp.concatenate([high.T, low.T, qt], axis=0)
        square = dot(left, high)
        acc[:p] += square[:p]
        hl[...] += square[p:2 * p]
        acc[p:2 * p] += square[2 * p:] + dot(qt, low)
        for c in range(2):
            mixed = dot(left, l_ref[rows, c * p:(c + 1) * p])
            acc[(2 + c) * p:(3 + c) * p] += mixed[:p] + mixed[p:2 * p]
            acc[(4 + c) * p:(5 + c) * p] += mixed[2 * p:]
    acc[:p] = acc[:p] + hl[...] + hl[...].T
    deal(core_ref, acc, scale, sends, keeps)
    for i in range(tiles):
        finish(at_tile(outputs, i, tile), out_sems.at[i])


def last_kernel(parts, tile, core_ref, *refs):
    own, other = refs[:parts], refs[parts:2 * parts]
    (x_ref, r1_ref, q_in, w_in, basis_out, factors, shift,
     total, q_ref, w_ref, basis, r_ref, m_ref, ih, il, back, sum_sems, in_sems, out_sems) = refs[2 * parts:]
    p = r_ref.shape[0]
    tiles = q_ref.shape[0] // tile
    sums = places(core_ref, own, other, total)
    inputs = [(q_in, q_ref), (w_in, w_ref)]
    outputs = [(basis, basis_out)]
    begin(sums, sum_sems)
    for i in range(tiles):
        begin(at_tile(inputs, i, tile), in_sems.at[i])
    finish(sums, sum_sems)

    res = total[p:2 * p]
    off = res - x_ref[...]
    off_b = off.astype(BF16)
    offt = off.T.astype(BF16)
    cut = dot(offt, res.astype(BF16))
    r_ref[...] = total[:p] - cut - cut.T + dot(offt, off_b)
    factor(r_ref, m_ref)
    inv = m_ref[...]
    high, low = split(inv.T)
    ih[:p] = high
    ih[p:] = high
    il[...] = low
    back[...] = dot(off_b, high).astype(BF16)

    def step(i, carry):
        rows = tile_rows(i, tile)
        finish(at_tile(inputs, i, tile), in_sems.at[i])
        q = dot(w_ref[rows, :], ih[...]) + dot(w_ref[rows, :p], il[...]) - dot(q_ref[rows, :], back[...])
        basis[rows, :p] = q_ref[rows, :]
        basis[rows, p:] = q.astype(BF16)
        begin(at_tile(outputs, i, tile), out_sems.at[i])
        return carry

    lax.fori_loop(0, tiles, step, 0)
    inv_s = split(m_ref[...])
    factors[0] = r1_ref[...]
    factors[1] = r_ref[...]
    for c in range(2):
        cols = slice(c * p, (c + 1) * p)
        early = total[(4 + c) * p:(5 + c) * p]
        shift[:p, cols] = early
        late = total[(2 + c) * p:(3 + c) * p] - dot(offt, early.astype(BF16))
        shift[p:, cols] = thrice(inv_s, split(late))
    for i in range(tiles):
        finish(at_tile(outputs, i, tile), out_sems.at[i])


def exchange(x, axis, bit):
    size = lax.axis_size(axis)
    return lax.ppermute(x, axis, [(i, i ^ (1 << bit)) for i in range(size)])


def summed(sends, keeps, tail):
    bits = list(range(lax.axis_size("rows").bit_length() - 1))
    turn, last = bits[:-1], bits[-1:]
    orders = [turn[n % len(turn):] + turn[:n % len(turn)] + last for n in range(len(sends))]
    me = lax.axis_index("rows")
    parts = [keep + exchange(send, "grp", 0) for send, keep in zip(sends, keeps)]
    halving = len(bits) - tail
    for step in range(halving):
        for n, order in enumerate(orders):
            x, bit = parts[n], order[step]
            half = x.shape[0] // 2
            mine = (me >> bit) & 1
            send = lax.dynamic_slice_in_dim(x, (1 - mine) * half, half, 0)
            keep = lax.dynamic_slice_in_dim(x, mine * half, half, 0)
            parts[n] = keep + exchange(send, "rows", bit)
    for step in range(halving, len(bits)):
        for n, order in enumerate(orders):
            parts[n] = parts[n] + exchange(parts[n], "rows", order[step])
    for step in reversed(range(halving)):
        for n, order in enumerate(orders):
            x, bit = parts[n], order[step]
            other = exchange(x, "rows", bit)
            mine = ((me >> bit) & 1) == 1
            parts[n] = jnp.concatenate([jnp.where(mine, other, x), jnp.where(mine, x, other)], axis=0)
    return parts, [exchange(x, "grp", 0) for x in parts]


def summed_at_once(send, keep):
    size = lax.axis_size("rows")
    x = keep + exchange(send, "grp", 0)
    got = lax.all_to_all(x, "rows", 0, 0, tiled=True)
    mine = got.reshape(size, x.shape[0] // size, x.shape[1]).sum(0)
    same = jnp.broadcast_to(mine[None], (size,) + mine.shape).reshape(x.shape)
    x = lax.all_to_all(same, "rows", 0, 0, tiled=True)
    return x, exchange(x, "grp", 0)


def body(earlier, snapshots, later):
    n, k = earlier.shape
    p = snapshots.shape[1] // 2
    devices = lax.axis_size(AXES)
    scale = 1.0 / (n * devices)
    core = lax.axis_index("grp").astype(jnp.int32).reshape(1)
    blocks = k // p
    rows = (2 * blocks + blocks * (blocks + 1) // 2) * p
    unit = 2 * devices * 8
    parts = 3 if rows % (3 * unit) == 0 else 1
    tile = 1024 if n % 1024 == 0 else n

    def smem():
        return pl.BlockSpec(memory_space=pltpu.SMEM)

    def whole(*shape):
        return pl.BlockSpec(shape, lambda i: (0,) * len(shape))

    def tiled(cols):
        return pl.BlockSpec((tile, cols), lambda i: (i, 0))

    def shape(*dims, dtype=F32):
        return jax.ShapeDtypeStruct(dims, dtype)

    def near(*dims, dtype=F32):
        return pltpu.VMEM(dims, dtype)

    def far(*dims, dtype=F32):
        return pltpu.HBM(dims, dtype)

    apart = pl.BlockSpec(memory_space=pl.ANY)
    inside = pl.BlockSpec(memory_space=pltpu.VMEM)

    def fixed(x):
        return pltpu.with_memory_space_constraint(x, pltpu.HBM)

    earlier, snapshots, later = fixed(earlier), fixed(snapshots), fixed(later)

    def call(kernel, name, room, ins, outs, scratch, flops, size, *args, grid=None):
        return pl.pallas_call(
            kernel,
            grid=(n // tile,) if grid is None else grid,
            in_specs=[s for s in ins],
            out_specs=[s for s, _ in outs],
            out_shape=[s for _, s in outs],
            scratch_shapes=scratch,
            name=name,
            cost_estimate=pl.CostEstimate(flops=flops, bytes_accessed=size, transcendentals=0),
            compiler_params=pltpu.CompilerParams(
                vmem_limit_bytes=room * MIB
            ),
        )(*args)

    tiles = n // tile
    dma = pltpu.SemaphoreType.DMA

    def held(*dims, dtype=F32):
        return pltpu.VMEM(dims, dtype)

    half = rows // parts // 2
    got = call(
        lambda *r: cross_kernel(parts, tile, *r), "cross", 32,
        [smem(), apart, apart],
        [(apart, near(half, p))] * (2 * parts),
        [
            held(n, k, dtype=BF16),
            held(n, 2 * p, dtype=BF16),
            held(rows, p),
            dma((tiles, 2)), dma((parts, 2)),
        ],
        2 * n * rows * p, 2 * n * (k + 2 * p),
        core, earlier, snapshots, grid=(),
    )
    own, other = summed(got[:parts], got[parts:], 1)

    u, w, z, h, t, send, keep = call(
        lambda *r: first_kernel(parts, tile, scale, *r), "first", 50,
        [smem()] + [apart] * (2 * parts + 2),
        [
            (apart, far(n, p)),
            (apart, far(n, 2 * p, dtype=BF16)),
            (apart, far(k, p)),
            (apart, far(k, p)),
            (inside, near(p, p)),
            (inside, near(p, p)),
            (inside, near(p, p)),
        ],
        [
            held(rows, p),
            held(n, k, dtype=BF16),
            held(n, 2 * p, dtype=BF16),
            held(n, p),
            held(n, 2 * p, dtype=BF16),
            held(k, p),
            held(k, p),
            held(k, 3 * p, dtype=BF16),
            held(k, k, dtype=BF16),
            held(k, k, dtype=BF16),
            held(2 * p, p),
            held(p, p),
            dma((2 * parts,)), dma((tiles, 2)), dma((tiles, 2)), dma((2,)),
        ],
        2 * n * p * (3 * k + 4 * p) + 12 * k * k * p, n * (2 * k + 12 * p),
        core, *own, *other, earlier, snapshots, grid=(),
    )
    own, other = summed_at_once(send, keep)

    got = call(
        lambda *r: second_kernel(3, tile, scale, *r), "second", 46,
        [smem()] + [apart] * 4 + [inside] + [apart] * 4,
        [
            (apart, far(n, p, dtype=BF16)),
            (apart, far(n, 2 * p, dtype=BF16)),
            (inside, near(p, p)),
            (inside, near(p, p)),
        ] + [(inside, near(p, p))] * 6,
        [
            held(2 * p, p),
            held(k, p),
            held(k, p),
            held(n, k, dtype=BF16),
            held(n, p),
            held(n, 2 * p, dtype=BF16),
            held(n, 2 * p, dtype=BF16),
            held(n, p, dtype=BF16),
            held(n, 2 * p, dtype=BF16),
            held(p, p),
            held(2 * p, p, dtype=BF16),
            held(p, p, dtype=BF16),
            held(p, p, dtype=BF16),
            held(k, p, dtype=BF16),
            held(p, p, dtype=BF16),
            held(6 * p, p),
            held(p, p),
            dma((2,)), dma((2,)), dma((tiles, 4)), dma((tiles, 2)),
        ],
        2 * n * p * (k + 15 * p), n * (2 * k + 18 * p),
        core, own, other, fixed(z), fixed(h), t, earlier, fixed(u), fixed(w), later, grid=(),
    )
    q_one, w2, r_one, expected = got[:4]
    own, other = summed(got[4:7], got[7:], 2)

    return tuple(call(
        lambda *r: last_kernel(3, tile, *r), "last", 26,
        [smem()] + [apart] * 6 + [inside] * 2 + [apart] * 2,
        [
            (apart, far(n, 2 * p, dtype=BF16)),
            (inside, shape(2, p, p)),
            (inside, shape(2 * p, 2 * p)),
        ],
        [
            held(6 * p, p),
            held(n, p, dtype=BF16),
            held(n, 2 * p, dtype=BF16),
            held(n, 2 * p, dtype=BF16),
            held(p, p),
            held(p, p),
            held(2 * p, p, dtype=BF16),
            held(p, p, dtype=BF16),
            held(p, p, dtype=BF16),
            dma((6,)), dma((tiles, 2)), dma((tiles, 1)),
        ],
        2 * n * p * 4 * p, n * 10 * p,
        core, *own, *other, expected, r_one, fixed(q_one), fixed(w2), grid=(),
    ))


def solution(mesh):
    spec = P(("rows", "grp"), None)
    return jax.shard_map(
        body,
        mesh=mesh,
        in_specs=(spec, spec, spec),
        out_specs=(spec, P(), P()),
        check_vma=False,
    )
```

```python
import jax
import jax.numpy as jnp
from jax import lax
from jax.experimental import pallas as pl
from jax.experimental.pallas import tpu as pltpu
from jax.sharding import PartitionSpec as P

AXES = ("rows", "grp")
HIGHEST = lax.Precision.HIGHEST
BF16 = jnp.bfloat16
F32 = jnp.float32
MIB = 2**20


def dot(a, b):
    return jnp.dot(a, b, preferred_element_type=F32)


def full(a, b):
    return jnp.dot(a, b, precision=HIGHEST, preferred_element_type=F32)


def wide(x):
    return x.astype(F32)


def split(x):
    high = x.astype(BF16)
    return high, (x - wide(high)).astype(BF16)


def thrice(a, b):
    return dot(a[0], b[0]) + dot(a[0], b[1]) + dot(a[1], b[0])


def factor_tile(groups, emit):
    count = len(groups)
    lane = lax.broadcasted_iota(jnp.int32, (8, 128), 1)
    sub = lax.broadcasted_iota(jnp.int32, (8, 128), 0)
    rows = list(groups)
    for k in range(count):
        base = 8 * k
        strip = rows[k]
        inside = (lane >= base) & (lane < base + 8)
        eye = jnp.where(lane == base + sub, 1.0, 0.0).astype(F32)
        mixed = jnp.where(inside, eye, strip)
        cols = [jnp.broadcast_to(strip[:, base + j:base + j + 1], (8, 128)) for j in range(8)]
        entry = {}
        for j in range(8):
            for i in range(j, 8):
                entry[i, j] = jnp.broadcast_to(cols[j][i:i + 1, :], (8, 128))
        scale = []
        low = {}
        for j in range(8):
            r = lax.rsqrt(entry[j, j])
            scale.append(r)
            for i in range(j + 1, 8):
                low[i, j] = entry[i, j] * r
            for c in range(j + 1, 8):
                for i in range(c, 8):
                    entry[i, c] = entry[i, c] - low[i, j] * low[c, j]
        upper, both = [], []
        for j in range(8):
            u = jnp.broadcast_to(strip[j:j + 1, :], (8, 128))
            v = jnp.broadcast_to(mixed[j:j + 1, :], (8, 128))
            for i in range(j):
                u = u - low[j, i] * upper[i]
                v = v - low[j, i] * both[i]
            upper.append(u * scale[j])
            both.append(v * scale[j])
        out_r = upper[0]
        out_m = both[0]
        for j in range(1, 8):
            out_r = jnp.where(sub == j, upper[j], out_r)
            out_m = jnp.where(sub == j, both[j], out_m)
        emit(
            k,
            jnp.where(lane >= base + sub, out_r, 0.0),
            jnp.where(lane <= base + sub, out_m, 0.0),
        )
        for g in range(k + 1, count):
            w = rows[g]
            new = jnp.where(inside, 0.0, w)
            left = []
            for j in range(8):
                c = jnp.broadcast_to(w[:, base + j:base + j + 1], (8, 128))
                for i in range(j):
                    c = c - left[i] * low[j, i]
                c = c * scale[j]
                left.append(c)
                new = new - c * both[j]
            rows[g] = new


def factor(r_ref, m_ref):
    n = r_ref.shape[0]
    h = 128

    def step(t, carry):
        top = pl.multiple_of(t * h, h)
        groups = [r_ref[pl.ds(pl.multiple_of(top + 8 * g, 8), 8), pl.ds(top, h)] for g in range(h // 8)]

        def emit(k, r, m):
            at = pl.ds(pl.multiple_of(top + 8 * k, 8), 8)
            r_ref[at, pl.ds(top, h)] = r
            m_ref[at, pl.ds(top, h)] = m

        factor_tile(groups, emit)

        @pl.when(t == 0)
        def _():
            inv = m_ref[:h, :h]
            u = full(inv, r_ref[:h, h:])
            ut = u.T
            r_ref[:h, h:] = u
            r_ref[h:, h:] = r_ref[h:, h:] - full(ut, u)
            m_ref[h:, :h] = full(ut, inv)
            r_ref[h:, :h] = jnp.zeros((n - h, h), F32)
            m_ref[:h, h:] = jnp.zeros((h, n - h), F32)

        return carry

    lax.fori_loop(0, n // h, step, 0)
    m_ref[h:, :h] = -full(m_ref[h:, h:], m_ref[h:, :h])


def begin(copies, sems):
    for n, (source, target) in enumerate(copies):
        pltpu.make_async_copy(source, target, sems.at[n]).start()


def finish(copies, sems):
    for n, (source, target) in enumerate(copies):
        pltpu.make_async_copy(source, target, sems.at[n]).wait()


def places(core_ref, own, other, total_ref):
    mine = core_ref[0]
    copies = []
    at = 0
    for a, b in zip(own, other):
        h = a.shape[0]
        copies.append((a, total_ref.at[pl.ds(pl.multiple_of(at + mine * h, 8), h)]))
        copies.append((b, total_ref.at[pl.ds(pl.multiple_of(at + (1 - mine) * h, 8), h)]))
        at += 2 * h
    return copies


def tile_rows(i, tile):
    return pl.ds(pl.multiple_of(i * tile, tile), tile)


def at_tile(pairs, i, tile):
    rows = tile_rows(i, tile)
    return [(a.at[rows], b.at[rows]) for a, b in pairs]


def deal(core_ref, total_ref, scale, sends, keeps):
    mine = core_ref[0]
    at = 0
    for send, keep in zip(sends, keeps):
        h = send.shape[0]
        keep[...] = total_ref[pl.ds(pl.multiple_of(at + mine * h, 8), h)] * scale
        send[...] = total_ref[pl.ds(pl.multiple_of(at + (1 - mine) * h, 8), h)] * scale
        at += 2 * h


def cross_kernel(parts, scale, core_ref, e_ref, x_ref, *refs):
    sends, keeps, acc = refs[:parts], refs[parts:2 * parts], refs[-1]
    k = e_ref.shape[1]
    p = x_ref.shape[1] // 2
    step = pl.program_id(0)

    @pl.when(step == 0)
    def _():
        acc[...] = jnp.zeros_like(acc)

    et = e_ref[...].T
    at = 0
    for c in range(2):
        acc[at:at + k] += dot(et, x_ref[:, c * p:(c + 1) * p])
        at += k
    for j in range(k // p):
        m = (j + 1) * p
        acc[at:at + m] += dot(et[:m], e_ref[:, j * p:(j + 1) * p])
        at += m

    @pl.when(step == pl.num_programs(0) - 1)
    def _():
        deal(core_ref, acc, scale, sends, keeps)


def first_kernel(parts, tile, scale, core_ref, *refs):
    own, other = refs[:parts], refs[parts:2 * parts]
    (e_in, x_in, u_out, w_out, z_out, h_out, t_ref, send, keep,
     total, e_ref, x_ref, u_ref, w_ref, z_ref, h_ref, b_ref, offh, offl, acc, hl,
     sum_sems, in_sems, out_sems, small_sems) = refs[2 * parts:]
    n, k = e_ref.shape
    p = u_ref.shape[1]
    tiles = n // tile
    sums = places(core_ref, own, other, total)
    inputs = [(e_in, e_ref), (x_in, x_ref)]
    outputs = [(u_ref, u_out), (w_ref, w_out)]
    small = [(z_ref, z_out), (h_ref, h_out)]
    begin(sums, sum_sems)
    acc[...] = jnp.zeros_like(acc)
    hl[...] = jnp.zeros_like(hl)
    finish(sums, sum_sems)
    for i in range(tiles):
        begin(at_tile(inputs, i, tile), in_sems.at[i])

    at = 2 * k
    for j in range(k // p):
        cols = slice(j * p, (j + 1) * p)
        for i in range(j + 1):
            block = total[at:at + p]
            at += p
            if i == j:
                a = lax.broadcasted_iota(jnp.int32, (p, p), 0)
                b = lax.broadcasted_iota(jnp.int32, (p, p), 1)
                block = block - jnp.where(a == b, 1.0, 0.0)
            high, low = split(block)
            rows = slice(i * p, (i + 1) * p)
            offh[rows, cols] = high
            offl[rows, cols] = low
            if i < j:
                offh[cols, rows] = high.T
                offl[cols, rows] = low.T
    for c in range(2):
        coef = total[c * k:(c + 1) * k]
        b = coef.astype(BF16)
        b_ref[:, c * p:(c + 1) * p] = b
        after = (coef - wide(b)) - dot(offh[...], b) - dot(offl[...], b)
        if c == 0:
            sb = after.astype(BF16)
            b_ref[:, 2 * p:] = sb
            against = (after - wide(sb)) - dot(offh[...], sb) - dot(offl[...], sb)
            h_ref[...] = against
        else:
            z_ref[...] = after
            high, low = split(against.T)
            t_ref[...] = dot(high, b) + dot(low, b)
    begin(small, small_sems)

    for i in range(tiles):
        finish(at_tile(inputs, i, tile), in_sems.at[i])

    def project(i):
        rows = tile_rows(i, tile)
        t = dot(e_ref[rows, :], b_ref[...])
        once = wide((wide(x_ref[rows, :p]) - t[:, :p]).astype(BF16))
        u_ref[rows, :] = wide(x_ref[rows, p:]) - t[:, p:2 * p]
        high, low = split(once - t[:, 2 * p:])
        w_ref[rows, :p] = high
        w_ref[rows, p:] = low

    def gather(i):
        rows = tile_rows(i, tile)
        high = w_ref[rows, :p]
        both = jnp.concatenate([high.T, w_ref[rows, p:].T], axis=0)
        square = dot(both, high)
        acc[:p] += square[:p]
        hl[...] += square[p:]
        other_two = dot(both, x_ref[rows, p:])
        acc[p:] += other_two[:p] + other_two[p:]

    def step(i, carry):
        gather(i)
        project(i + 1)
        begin(at_tile(outputs, i + 1, tile), out_sems.at[i + 1])
        return carry

    project(0)
    begin(at_tile(outputs, 0, tile), out_sems.at[0])
    lax.fori_loop(0, tiles - 1, step, 0)
    gather(tiles - 1)
    acc[:p] = acc[:p] + hl[...] + hl[...].T
    deal(core_ref, acc, scale, [send], [keep])
    for i in range(tiles):
        finish(at_tile(outputs, i, tile), out_sems.at[i])
    finish(small, small_sems)


def second_kernel(parts, tile, scale, core_ref, own, other, z_in, h_in, t_ref, e_in, u_in, w_in, l_in, *refs):
    q_out, w2_out, r_ref, x_ref = refs[:4]
    sends, keeps = refs[4:4 + parts], refs[4 + parts:4 + 2 * parts]
    (total, z_ref, h_ref, e_ref, u_ref, w_ref, l_ref, q_ref, w2_ref, m_ref, ih, il, db, ub, lb, acc, hl,
     sum_sems, small_sems, in_sems, out_sems) = refs[4 + 2 * parts:]
    p = r_ref.shape[0]
    n = e_ref.shape[0]
    tiles = n // tile
    sums = places(core_ref, [own], [other], total)
    small = [(z_in, z_ref), (h_in, h_ref)]
    inputs = [(e_in, e_ref), (u_in, u_ref), (w_in, w_ref), (l_in, l_ref)]
    outputs = [(q_ref, q_out), (w2_ref, w2_out)]
    begin(sums, sum_sems)
    acc[...] = jnp.zeros_like(acc)
    hl[...] = jnp.zeros_like(hl)
    finish(sums, sum_sems)
    begin(small, small_sems)
    for i in range(tiles):
        begin(at_tile(inputs, i, tile), in_sems.at[i])

    r_ref[...] = total[:p]
    factor(r_ref, m_ref)
    inv = m_ref[...]
    high, low = split(inv.T)
    ih[:p] = high
    ih[p:] = high
    il[...] = low
    d = full(inv, total[p:])
    d_b = d.astype(BF16)
    db[...] = d_b
    finish(small, small_sems)
    inv_s = split(inv)
    against = split(h_ref[...])
    at = split(h_ref[...].T)
    turned = split(dot(high, d_b) + dot(low, d_b))
    upper = (z_ref[...] - thrice(against, turned)).astype(BF16)
    ub[...] = upper
    lower = (d - wide(d_b)) - thrice(inv_s, split(t_ref[...]))
    lower_b = lower.astype(BF16)
    lb[...] = lower_b
    x_ref[...] = (lower - wide(lower_b)) - thrice(inv_s, split(dot(at[0], upper) + dot(at[1], upper)))

    for i in range(tiles):
        finish(at_tile(inputs, i, tile), in_sems.at[i])

    def project(i):
        rows = tile_rows(i, tile)
        q = (dot(w_ref[rows, :], ih[...]) + dot(w_ref[rows, :p], il[...])).astype(BF16)
        q_ref[rows, :] = q
        once = wide((u_ref[rows, :] - dot(q, db[...])).astype(BF16))
        high, low = split(once - dot(e_ref[rows, :], ub[...]) - dot(q, lb[...]))
        w2_ref[rows, :p] = high
        w2_ref[rows, p:] = low

    def gather(i):
        rows = tile_rows(i, tile)
        high, low = w2_ref[rows, :p], w2_ref[rows, p:]
        qt = q_ref[rows, :].T
        left = jnp.concatenate([high.T, low.T, qt], axis=0)
        square = dot(left, high)
        acc[:p] += square[:p]
        hl[...] += square[p:2 * p]
        acc[p:2 * p] += square[2 * p:] + dot(qt, low)
        for c in range(2):
            mixed = dot(left, l_ref[rows, c * p:(c + 1) * p])
            acc[(2 + c) * p:(3 + c) * p] += mixed[:p] + mixed[p:2 * p]
            acc[(4 + c) * p:(5 + c) * p] += mixed[2 * p:]

    def step(i, carry):
        gather(i)
        project(i + 1)
        begin(at_tile(outputs, i + 1, tile), out_sems.at[i + 1])
        return carry

    project(0)
    begin(at_tile(outputs, 0, tile), out_sems.at[0])
    lax.fori_loop(0, tiles - 1, step, 0)
    gather(tiles - 1)
    acc[:p] = acc[:p] + hl[...] + hl[...].T
    deal(core_ref, acc, scale, sends, keeps)
    for i in range(tiles):
        finish(at_tile(outputs, i, tile), out_sems.at[i])


def last_kernel(parts, tile, core_ref, *refs):
    own, other = refs[:parts], refs[parts:2 * parts]
    (x_ref, r1_ref, q_in, w_in, basis_out, factors, shift,
     total, q_ref, w_ref, basis, r_ref, m_ref, ih, il, back, sum_sems, in_sems, out_sems) = refs[2 * parts:]
    p = r_ref.shape[0]
    tiles = q_ref.shape[0] // tile
    sums = places(core_ref, own, other, total)
    inputs = [(q_in, q_ref), (w_in, w_ref)]
    outputs = [(basis, basis_out)]
    begin(sums, sum_sems)
    finish(sums, sum_sems)
    for i in range(tiles):
        begin(at_tile(inputs, i, tile), in_sems.at[i])

    res = total[p:2 * p]
    off = res - x_ref[...]
    off_b = off.astype(BF16)
    offt = off.T.astype(BF16)
    cut = dot(offt, res.astype(BF16))
    r_ref[...] = total[:p] - cut - cut.T + dot(offt, off_b)
    factor(r_ref, m_ref)
    inv = m_ref[...]
    high, low = split(inv.T)
    ih[:p] = high
    ih[p:] = high
    il[...] = low
    back[...] = dot(off_b, high).astype(BF16)

    def step(i, carry):
        rows = tile_rows(i, tile)
        finish(at_tile(inputs, i, tile), in_sems.at[i])
        q = dot(w_ref[rows, :], ih[...]) + dot(w_ref[rows, :p], il[...]) - dot(q_ref[rows, :], back[...])
        basis[rows, :p] = q_ref[rows, :]
        basis[rows, p:] = q.astype(BF16)
        begin(at_tile(outputs, i, tile), out_sems.at[i])
        return carry

    lax.fori_loop(0, tiles, step, 0)
    inv_s = split(m_ref[...])
    factors[0] = r1_ref[...]
    factors[1] = r_ref[...]
    for c in range(2):
        cols = slice(c * p, (c + 1) * p)
        early = total[(4 + c) * p:(5 + c) * p]
        shift[:p, cols] = early
        late = total[(2 + c) * p:(3 + c) * p] - dot(offt, early.astype(BF16))
        shift[p:, cols] = thrice(inv_s, split(late))
    for i in range(tiles):
        finish(at_tile(outputs, i, tile), out_sems.at[i])


def exchange(x, axis, bit):
    size = lax.axis_size(axis)
    return lax.ppermute(x, axis, [(i, i ^ (1 << bit)) for i in range(size)])


def summed(sends, keeps, tail):
    bits = list(range(lax.axis_size("rows").bit_length() - 1))
    turn, last = bits[:-1], bits[-1:]
    orders = [turn[n % len(turn):] + turn[:n % len(turn)] + last for n in range(len(sends))]
    me = lax.axis_index("rows")
    parts = [keep + exchange(send, "grp", 0) for send, keep in zip(sends, keeps)]
    halving = len(bits) - tail
    for step in range(halving):
        for n, order in enumerate(orders):
            x, bit = parts[n], order[step]
            half = x.shape[0] // 2
            mine = (me >> bit) & 1
            send = lax.dynamic_slice_in_dim(x, (1 - mine) * half, half, 0)
            keep = lax.dynamic_slice_in_dim(x, mine * half, half, 0)
            parts[n] = keep + exchange(send, "rows", bit)
    for step in range(halving, len(bits)):
        for n, order in enumerate(orders):
            parts[n] = parts[n] + exchange(parts[n], "rows", order[step])
    for step in reversed(range(halving)):
        for n, order in enumerate(orders):
            x, bit = parts[n], order[step]
            other = exchange(x, "rows", bit)
            mine = ((me >> bit) & 1) == 1
            parts[n] = jnp.concatenate([jnp.where(mine, other, x), jnp.where(mine, x, other)], axis=0)
    return parts, [exchange(x, "grp", 0) for x in parts]


def summed_at_once(send, keep):
    size = lax.axis_size("rows")
    x = keep + exchange(send, "grp", 0)
    got = lax.all_to_all(x, "rows", 0, 0, tiled=True)
    mine = got.reshape(size, x.shape[0] // size, x.shape[1]).sum(0)
    same = jnp.broadcast_to(mine[None], (size,) + mine.shape).reshape(x.shape)
    x = lax.all_to_all(same, "rows", 0, 0, tiled=True)
    return x, exchange(x, "grp", 0)


def body(earlier, snapshots, later):
    n, k = earlier.shape
    p = snapshots.shape[1] // 2
    devices = lax.axis_size(AXES)
    scale = 1.0 / (n * devices)
    core = lax.axis_index("grp").astype(jnp.int32).reshape(1)
    blocks = k // p
    rows = (2 * blocks + blocks * (blocks + 1) // 2) * p
    unit = 2 * devices * 8
    parts = 3 if rows % (3 * unit) == 0 else 1
    tile = 1024 if n % 1024 == 0 else n

    def smem():
        return pl.BlockSpec(memory_space=pltpu.SMEM)

    def whole(*shape):
        return pl.BlockSpec(shape, lambda i: (0,) * len(shape))

    def tiled(cols):
        return pl.BlockSpec((tile, cols), lambda i: (i, 0))

    def shape(*dims, dtype=F32):
        return jax.ShapeDtypeStruct(dims, dtype)

    def near(*dims, dtype=F32):
        return pltpu.VMEM(dims, dtype)

    def far(*dims, dtype=F32):
        return pltpu.HBM(dims, dtype)

    apart = pl.BlockSpec(memory_space=pl.ANY)
    inside = pl.BlockSpec(memory_space=pltpu.VMEM)

    def fixed(x):
        return pltpu.with_memory_space_constraint(x, pltpu.HBM)

    earlier, snapshots, later = fixed(earlier), fixed(snapshots), fixed(later)

    def call(kernel, name, room, ins, outs, scratch, flops, size, *args, grid=None):
        return pl.pallas_call(
            kernel,
            grid=(n // tile,) if grid is None else grid,
            in_specs=[s for s in ins],
            out_specs=[s for s, _ in outs],
            out_shape=[s for _, s in outs],
            scratch_shapes=scratch,
            name=name,
            cost_estimate=pl.CostEstimate(flops=flops, bytes_accessed=size, transcendentals=0),
            compiler_params=pltpu.CompilerParams(
                vmem_limit_bytes=room * MIB
            ),
        )(*args)

    short = 512 if n % 512 == 0 else n
    tiles = n // short
    dma = pltpu.SemaphoreType.DMA

    def held(*dims, dtype=F32):
        return pltpu.VMEM(dims, dtype)

    half = rows // parts // 2
    halves = [(whole(half, p), near(half, p))] * (2 * parts)
    got = call(
        lambda *r: cross_kernel(parts, scale, *r), "cross", 32,
        [smem(), tiled(k), tiled(2 * p)],
        halves,
        [pltpu.VMEM((rows, p), F32)],
        2 * n * rows * p, 2 * n * (k + 2 * p),
        core, earlier, snapshots,
    )
    own, other = summed(got[:parts], got[parts:], 1)

    short = 512 if n % 512 == 0 else n
    tiles = n // short
    dma = pltpu.SemaphoreType.DMA

    def held(*dims, dtype=F32):
        return pltpu.VMEM(dims, dtype)

    u, w, z, h, t, send, keep = call(
        lambda *r: first_kernel(parts, short, scale, *r), "first", 50,
        [smem()] + [apart] * (2 * parts + 2),
        [
            (apart, far(n, p)),
            (apart, far(n, 2 * p, dtype=BF16)),
            (apart, far(k, p)),
            (apart, far(k, p)),
            (inside, near(p, p)),
            (inside, near(p, p)),
            (inside, near(p, p)),
        ],
        [
            held(rows, p),
            held(n, k, dtype=BF16),
            held(n, 2 * p, dtype=BF16),
            held(n, p),
            held(n, 2 * p, dtype=BF16),
            held(k, p),
            held(k, p),
            held(k, 3 * p, dtype=BF16),
            held(k, k, dtype=BF16),
            held(k, k, dtype=BF16),
            held(2 * p, p),
            held(p, p),
            dma((2 * parts,)), dma((tiles, 2)), dma((tiles, 2)), dma((2,)),
        ],
        2 * n * p * (3 * k + 4 * p) + 12 * k * k * p, n * (2 * k + 12 * p),
        core, *own, *other, earlier, snapshots, grid=(),
    )
    own, other = summed_at_once(send, keep)

    got = call(
        lambda *r: second_kernel(3, short, scale, *r), "second", 46,
        [smem()] + [apart] * 4 + [inside] + [apart] * 4,
        [
            (apart, far(n, p, dtype=BF16)),
            (apart, far(n, 2 * p, dtype=BF16)),
            (inside, near(p, p)),
            (inside, near(p, p)),
        ] + [(inside, near(p, p))] * 6,
        [
            held(2 * p, p),
            held(k, p),
            held(k, p),
            held(n, k, dtype=BF16),
            held(n, p),
            held(n, 2 * p, dtype=BF16),
            held(n, 2 * p, dtype=BF16),
            held(n, p, dtype=BF16),
            held(n, 2 * p, dtype=BF16),
            held(p, p),
            held(2 * p, p, dtype=BF16),
            held(p, p, dtype=BF16),
            held(p, p, dtype=BF16),
            held(k, p, dtype=BF16),
            held(p, p, dtype=BF16),
            held(6 * p, p),
            held(p, p),
            dma((2,)), dma((2,)), dma((tiles, 4)), dma((tiles, 2)),
        ],
        2 * n * p * (k + 15 * p), n * (2 * k + 18 * p),
        core, own, other, fixed(z), fixed(h), t, earlier, fixed(u), fixed(w), later, grid=(),
    )
    q_one, w2, r_one, expected = got[:4]
    own, other = summed(got[4:7], got[7:], 2)

    return tuple(call(
        lambda *r: last_kernel(3, short, *r), "last", 26,
        [smem()] + [apart] * 6 + [inside] * 2 + [apart] * 2,
        [
            (apart, far(n, 2 * p, dtype=BF16)),
            (inside, shape(2, p, p)),
            (inside, shape(2 * p, 2 * p)),
        ],
        [
            held(6 * p, p),
            held(n, p, dtype=BF16),
            held(n, 2 * p, dtype=BF16),
            held(n, 2 * p, dtype=BF16),
            held(p, p),
            held(p, p),
            held(2 * p, p, dtype=BF16),
            held(p, p, dtype=BF16),
            held(p, p, dtype=BF16),
            dma((6,)), dma((tiles, 2)), dma((tiles, 1)),
        ],
        2 * n * p * 4 * p, n * 10 * p,
        core, *own, *other, expected, r_one, fixed(q_one), fixed(w2), grid=(),
    ))


def solution(mesh):
    spec = P(("rows", "grp"), None)
    return jax.shard_map(
        body,
        mesh=mesh,
        in_specs=(spec, spec, spec),
        out_specs=(spec, P(), P()),
        check_vma=False,
    )
```

```python
import jax
import jax.numpy as jnp
from jax import lax
from jax.experimental import pallas as pl
from jax.experimental.pallas import tpu as pltpu
from jax.sharding import PartitionSpec as P

AXES = ("rows", "grp")
HIGHEST = lax.Precision.HIGHEST
BF16 = jnp.bfloat16
F32 = jnp.float32
MIB = 2**20


def dot(a, b):
    return jnp.dot(a, b, preferred_element_type=F32)


def full(a, b):
    return jnp.dot(a, b, precision=HIGHEST, preferred_element_type=F32)


def wide(x):
    return x.astype(F32)


def split(x):
    high = x.astype(BF16)
    return high, (x - wide(high)).astype(BF16)


def thrice(a, b):
    return dot(a[0], b[0]) + dot(a[0], b[1]) + dot(a[1], b[0])


def factor_tile(groups, emit):
    count = len(groups)
    lane = lax.broadcasted_iota(jnp.int32, (8, 128), 1)
    sub = lax.broadcasted_iota(jnp.int32, (8, 128), 0)
    rows = list(groups)

    def column(w, at):
        return jnp.broadcast_to(w[:, at:at + 1], (8, 128))

    def row(w, at):
        return jnp.broadcast_to(w[at:at + 1, :], (8, 128))

    def entries(w, base):
        cols = [column(w, base + j) for j in range(8)]
        return {(i, j): row(cols[j], i) for j in range(8) for i in range(j, 8)}

    later = entries(rows[0], 0)
    for k in range(count):
        base = 8 * k
        strip = rows[k]
        inside = (lane >= base) & (lane < base + 8)
        eye = jnp.where(lane == base + sub, 1.0, 0.0).astype(F32)
        mixed = jnp.where(inside, eye, strip)
        entry = later
        if k + 1 < count:
            later = entries(rows[k + 1], base + 8)
        scale = []
        low = {}
        for j in range(8):
            r = lax.rsqrt(entry[j, j])
            scale.append(r)
            for i in range(j + 1, 8):
                low[i, j] = entry[i, j] * r
            for c in range(j + 1, 8):
                for i in range(c, 8):
                    entry[i, c] = entry[i, c] - low[i, j] * low[c, j]
        lefts = {}
        for g in range(k + 1, count):
            left = []
            for j in range(8):
                c = column(rows[g], base + j)
                for i in range(j):
                    c = c - left[i] * low[j, i]
                left.append(c * scale[j])
            lefts[g] = left
            if g == k + 1:
                for j in range(8):
                    spread = [row(left[j], i) for i in range(8)]
                    for c in range(8):
                        for i in range(c, 8):
                            later[i, c] = later[i, c] - spread[i] * spread[c]
        upper, both = [], []
        for j in range(8):
            u = row(strip, j)
            v = row(mixed, j)
            for i in range(j):
                u = u - low[j, i] * upper[i]
                v = v - low[j, i] * both[i]
            upper.append(u * scale[j])
            both.append(v * scale[j])
        out_r = upper[0]
        out_m = both[0]
        for j in range(1, 8):
            out_r = jnp.where(sub == j, upper[j], out_r)
            out_m = jnp.where(sub == j, both[j], out_m)
        emit(
            k,
            jnp.where(lane >= base + sub, out_r, 0.0),
            jnp.where(lane <= base + sub, out_m, 0.0),
        )
        for g in range(k + 1, count):
            new = jnp.where(inside, 0.0, rows[g])
            for j in range(8):
                new = new - lefts[g][j] * both[j]
            rows[g] = new


def factor(r_ref, m_ref):
    n = r_ref.shape[0]
    h = 128

    def step(t, carry):
        top = pl.multiple_of(t * h, h)
        groups = [r_ref[pl.ds(pl.multiple_of(top + 8 * g, 8), 8), pl.ds(top, h)] for g in range(h // 8)]

        def emit(k, r, m):
            at = pl.ds(pl.multiple_of(top + 8 * k, 8), 8)
            r_ref[at, pl.ds(top, h)] = r
            m_ref[at, pl.ds(top, h)] = m

        factor_tile(groups, emit)

        @pl.when(t == 0)
        def _():
            inv = m_ref[:h, :h]
            u = full(inv, r_ref[:h, h:])
            ut = u.T
            r_ref[:h, h:] = u
            r_ref[h:, h:] = r_ref[h:, h:] - full(ut, u)
            m_ref[h:, :h] = full(ut, inv)
            r_ref[h:, :h] = jnp.zeros((n - h, h), F32)
            m_ref[:h, h:] = jnp.zeros((h, n - h), F32)

        return carry

    lax.fori_loop(0, n // h, step, 0)
    m_ref[h:, :h] = -full(m_ref[h:, h:], m_ref[h:, :h])


def begin(copies, sems):
    for n, (source, target) in enumerate(copies):
        pltpu.make_async_copy(source, target, sems.at[n]).start()


def finish(copies, sems):
    for n, (source, target) in enumerate(copies):
        pltpu.make_async_copy(source, target, sems.at[n]).wait()


def places(core_ref, own, other, total_ref):
    mine = core_ref[0]
    copies = []
    at = 0
    for a, b in zip(own, other):
        h = a.shape[0]
        copies.append((a, total_ref.at[pl.ds(pl.multiple_of(at + mine * h, 8), h)]))
        copies.append((b, total_ref.at[pl.ds(pl.multiple_of(at + (1 - mine) * h, 8), h)]))
        at += 2 * h
    return copies


def tile_rows(i, tile):
    return pl.ds(pl.multiple_of(i * tile, tile), tile)


def at_tile(pairs, i, tile):
    rows = tile_rows(i, tile)
    return [(a.at[rows], b.at[rows]) for a, b in pairs]


def deal(core_ref, total_ref, scale, sends, keeps):
    mine = core_ref[0]
    at = 0
    for send, keep in zip(sends, keeps):
        h = send.shape[0]
        keep[...] = total_ref[pl.ds(pl.multiple_of(at + mine * h, 8), h)] * scale
        send[...] = total_ref[pl.ds(pl.multiple_of(at + (1 - mine) * h, 8), h)] * scale
        at += 2 * h


def cross_kernel(parts, tile, core_ref, e_in, x_in, *refs):
    sends, keeps = refs[:parts], refs[parts:2 * parts]
    e_ref, x_ref, even, odd, acc, in_sems, out_sems = refs[2 * parts:]
    k = e_ref.shape[1]
    p = x_ref.shape[1] // 2
    tiles = e_ref.shape[0] // tile
    ahead = min(3, tiles)
    inputs = [(e_in, e_ref), (x_in, x_ref)]
    h = sends[0].shape[0]
    outputs = []
    for n in range(parts):
        away, stay = (2 * n + 1 - core_ref[0]) * h, (2 * n + core_ref[0]) * h
        outputs.append([
            (acc.at[pl.ds(pl.multiple_of(away, 8), h)], sends[n]),
            (acc.at[pl.ds(pl.multiple_of(stay, 8), h)], keeps[n]),
        ])
    jobs = [(k, x_ref, c) for c in range(2)] + [((j + 1) * p, e_ref, j) for j in range(k // p)]

    def turn(i, target):
        target[...] = e_ref[tile_rows(i, tile), :].T

    def products(i, left):
        rows = tile_rows(i, tile)
        at = 0
        for m, right, c in jobs:
            acc[at:at + m] += dot(left[:m], right[rows, c * p:(c + 1) * p])
            at += m

    def arrive(i):
        finish(at_tile(inputs, i, tile), in_sems.at[i])

        @pl.when(i + ahead < tiles)
        def _():
            begin(at_tile(inputs, i + ahead, tile), in_sems.at[i + ahead])

    for i in range(ahead):
        begin(at_tile(inputs, i, tile), in_sems.at[i])
    acc[...] = jnp.zeros_like(acc)
    arrive(0)
    turn(0, even)

    def step(t, carry):
        i = 2 * t
        arrive(i + 1)

        @pl.when(i + 2 < tiles)
        def _():
            arrive(i + 2)

        products(i, even)
        turn(i + 1, odd)
        products(i + 1, odd)
        turn(jnp.minimum(i + 2, tiles - 1), even)
        return carry

    lax.fori_loop(0, tiles // 2, step, 0)
    if tiles % 2:
        products(tiles - 1, even)
    for n in range(parts):
        begin(outputs[n], out_sems.at[n])
    for n in range(parts):
        finish(outputs[n], out_sems.at[n])


def first_kernel(parts, tile, scale, core_ref, *refs):
    own, other = refs[:parts], refs[parts:2 * parts]
    (e_in, x_in, u_out, w_out, z_out, h_out, t_ref, send, keep,
     total, e_ref, x_ref, u_ref, w_ref, z_ref, h_ref, b_ref, offh, offl, acc, hl,
     sum_sems, in_sems, out_sems, small_sems) = refs[2 * parts:]
    n, k = e_ref.shape
    p = u_ref.shape[1]
    tiles = n // tile
    sums = places(core_ref, own, other, total)
    inputs = [(e_in, e_ref), (x_in, x_ref)]
    outputs = [(u_ref, u_out), (w_ref, w_out)]
    small = [(z_ref, z_out), (h_ref, h_out)]
    begin(sums, sum_sems)
    acc[...] = jnp.zeros_like(acc)
    hl[...] = jnp.zeros_like(hl)
    finish(sums, sum_sems)
    for i in range(tiles):
        begin(at_tile(inputs, i, tile), in_sems.at[i])

    at = 2 * k
    for j in range(k // p):
        cols = slice(j * p, (j + 1) * p)
        for i in range(j + 1):
            block = total[at:at + p] * scale
            at += p
            if i == j:
                a = lax.broadcasted_iota(jnp.int32, (p, p), 0)
                b = lax.broadcasted_iota(jnp.int32, (p, p), 1)
                block = block - jnp.where(a == b, 1.0, 0.0)
            high, low = split(block)
            rows = slice(i * p, (i + 1) * p)
            offh[rows, cols] = high
            offl[rows, cols] = low
            if i < j:
                offh[cols, rows] = high.T
                offl[cols, rows] = low.T
    for c in range(2):
        coef = total[c * k:(c + 1) * k] * scale
        b = coef.astype(BF16)
        b_ref[:, c * p:(c + 1) * p] = b
        after = (coef - wide(b)) - dot(offh[...], b) - dot(offl[...], b)
        if c == 0:
            sb = after.astype(BF16)
            b_ref[:, 2 * p:] = sb
            against = (after - wide(sb)) - dot(offh[...], sb) - dot(offl[...], sb)
            h_ref[...] = against
        else:
            z_ref[...] = after
            high, low = split(against.T)
            t_ref[...] = dot(high, b) + dot(low, b)
    begin(small, small_sems)

    for i in range(tiles):
        finish(at_tile(inputs, i, tile), in_sems.at[i])

    def project(i):
        rows = tile_rows(i, tile)
        t = dot(e_ref[rows, :], b_ref[...])
        once = wide((wide(x_ref[rows, :p]) - t[:, :p]).astype(BF16))
        u_ref[rows, :] = wide(x_ref[rows, p:]) - t[:, p:2 * p]
        high, low = split(once - t[:, 2 * p:])
        w_ref[rows, :p] = high
        w_ref[rows, p:] = low

    def gather(i):
        rows = tile_rows(i, tile)
        high = w_ref[rows, :p]
        both = jnp.concatenate([high.T, w_ref[rows, p:].T], axis=0)
        square = dot(both, high)
        acc[:p] += square[:p]
        hl[...] += square[p:]
        other_two = dot(both, x_ref[rows, p:])
        acc[p:] += other_two[:p] + other_two[p:]

    def step(i, carry):
        gather(i)
        project(i + 1)
        begin(at_tile(outputs, i + 1, tile), out_sems.at[i + 1])
        return carry

    project(0)
    begin(at_tile(outputs, 0, tile), out_sems.at[0])
    lax.fori_loop(0, tiles - 1, step, 0)
    gather(tiles - 1)
    acc[:p] = acc[:p] + hl[...] + hl[...].T
    deal(core_ref, acc, scale, [send], [keep])
    for i in range(tiles):
        finish(at_tile(outputs, i, tile), out_sems.at[i])
    finish(small, small_sems)


def second_kernel(parts, tile, scale, core_ref, own, other, z_in, h_in, t_ref, e_in, u_in, w_in, l_in, *refs):
    q_out, w2_out, r_ref, x_ref = refs[:4]
    sends, keeps = refs[4:4 + parts], refs[4 + parts:4 + 2 * parts]
    (total, z_ref, h_ref, e_ref, u_ref, w_ref, l_ref, q_ref, w2_ref, m_ref, ih, il, db, ub, lb, acc, hl,
     sum_sems, small_sems, in_sems, out_sems) = refs[4 + 2 * parts:]
    p = r_ref.shape[0]
    n = e_ref.shape[0]
    tiles = n // tile
    sums = places(core_ref, [own], [other], total)
    small = [(z_in, z_ref), (h_in, h_ref)]
    inputs = [(e_in, e_ref), (u_in, u_ref), (w_in, w_ref), (l_in, l_ref)]
    outputs = [(q_ref, q_out), (w2_ref, w2_out)]
    begin(sums, sum_sems)
    acc[...] = jnp.zeros_like(acc)
    hl[...] = jnp.zeros_like(hl)
    finish(sums, sum_sems)
    begin(small, small_sems)
    for i in range(tiles):
        begin(at_tile(inputs, i, tile), in_sems.at[i])

    r_ref[...] = total[:p]
    factor(r_ref, m_ref)
    inv = m_ref[...]
    high, low = split(inv.T)
    ih[:p] = high
    ih[p:] = high
    il[...] = low
    d = full(inv, total[p:])
    d_b = d.astype(BF16)
    db[...] = d_b
    finish(small, small_sems)
    inv_s = split(inv)
    against = split(h_ref[...])
    at = split(h_ref[...].T)
    turned = split(dot(high, d_b) + dot(low, d_b))
    upper = (z_ref[...] - thrice(against, turned)).astype(BF16)
    ub[...] = upper
    lower = (d - wide(d_b)) - thrice(inv_s, split(t_ref[...]))
    lower_b = lower.astype(BF16)
    lb[...] = lower_b
    x_ref[...] = (lower - wide(lower_b)) - thrice(inv_s, split(dot(at[0], upper) + dot(at[1], upper)))

    for i in range(tiles):
        finish(at_tile(inputs, i, tile), in_sems.at[i])

    def project(i):
        rows = tile_rows(i, tile)
        q = (dot(w_ref[rows, :], ih[...]) + dot(w_ref[rows, :p], il[...])).astype(BF16)
        q_ref[rows, :] = q
        once = wide((u_ref[rows, :] - dot(q, db[...])).astype(BF16))
        high, low = split(once - dot(e_ref[rows, :], ub[...]) - dot(q, lb[...]))
        w2_ref[rows, :p] = high
        w2_ref[rows, p:] = low

    def gather(i):
        rows = tile_rows(i, tile)
        high, low = w2_ref[rows, :p], w2_ref[rows, p:]
        qt = q_ref[rows, :].T
        left = jnp.concatenate([high.T, low.T, qt], axis=0)
        square = dot(left, high)
        acc[:p] += square[:p]
        hl[...] += square[p:2 * p]
        acc[p:2 * p] += square[2 * p:] + dot(qt, low)
        for c in range(2):
            mixed = dot(left, l_ref[rows, c * p:(c + 1) * p])
            acc[(2 + c) * p:(3 + c) * p] += mixed[:p] + mixed[p:2 * p]
            acc[(4 + c) * p:(5 + c) * p] += mixed[2 * p:]

    def step(i, carry):
        gather(i)
        project(i + 1)
        begin(at_tile(outputs, i + 1, tile), out_sems.at[i + 1])
        return carry

    project(0)
    begin(at_tile(outputs, 0, tile), out_sems.at[0])
    lax.fori_loop(0, tiles - 1, step, 0)
    gather(tiles - 1)
    acc[:p] = acc[:p] + hl[...] + hl[...].T
    deal(core_ref, acc, scale, sends, keeps)
    for i in range(tiles):
        finish(at_tile(outputs, i, tile), out_sems.at[i])


def last_kernel(parts, tile, core_ref, *refs):
    own, other = refs[:parts], refs[parts:2 * parts]
    (x_ref, r1_ref, q_in, w_in, basis_out, factors, shift,
     total, q_ref, w_ref, basis, r_ref, m_ref, ih, il, back, sum_sems, in_sems, out_sems) = refs[2 * parts:]
    p = r_ref.shape[0]
    tiles = q_ref.shape[0] // tile
    sums = places(core_ref, own, other, total)
    inputs = [(q_in, q_ref), (w_in, w_ref)]
    outputs = [(basis, basis_out)]
    begin(sums, sum_sems)
    finish(sums, sum_sems)
    for i in range(tiles):
        begin(at_tile(inputs, i, tile), in_sems.at[i])

    res = total[p:2 * p]
    off = res - x_ref[...]
    off_b = off.astype(BF16)
    offt = off.T.astype(BF16)
    cut = dot(offt, res.astype(BF16))
    r_ref[...] = total[:p] - cut - cut.T + dot(offt, off_b)
    factor(r_ref, m_ref)
    inv = m_ref[...]
    high, low = split(inv.T)
    ih[:p] = high
    ih[p:] = high
    il[...] = low
    back[...] = dot(off_b, high).astype(BF16)

    def step(i, carry):
        rows = tile_rows(i, tile)
        finish(at_tile(inputs, i, tile), in_sems.at[i])
        q = dot(w_ref[rows, :], ih[...]) + dot(w_ref[rows, :p], il[...]) - dot(q_ref[rows, :], back[...])
        basis[rows, :p] = q_ref[rows, :]
        basis[rows, p:] = q.astype(BF16)
        begin(at_tile(outputs, i, tile), out_sems.at[i])
        return carry

    lax.fori_loop(0, tiles, step, 0)
    inv_s = split(m_ref[...])
    factors[0] = r1_ref[...]
    factors[1] = r_ref[...]
    for c in range(2):
        cols = slice(c * p, (c + 1) * p)
        early = total[(4 + c) * p:(5 + c) * p]
        shift[:p, cols] = early
        late = total[(2 + c) * p:(3 + c) * p] - dot(offt, early.astype(BF16))
        shift[p:, cols] = thrice(inv_s, split(late))
    for i in range(tiles):
        finish(at_tile(outputs, i, tile), out_sems.at[i])


def exchange(x, axis, bit):
    size = lax.axis_size(axis)
    return lax.ppermute(x, axis, [(i, i ^ (1 << bit)) for i in range(size)])


def summed(sends, keeps, tail):
    bits = list(range(lax.axis_size("rows").bit_length() - 1))
    turn, last = bits[:-1], bits[-1:]
    orders = [turn[n % len(turn):] + turn[:n % len(turn)] + last for n in range(len(sends))]
    me = lax.axis_index("rows")
    parts = [keep + exchange(send, "grp", 0) for send, keep in zip(sends, keeps)]
    halving = len(bits) - tail
    for step in range(halving):
        for n, order in enumerate(orders):
            x, bit = parts[n], order[step]
            half = x.shape[0] // 2
            mine = (me >> bit) & 1
            send = lax.dynamic_slice_in_dim(x, (1 - mine) * half, half, 0)
            keep = lax.dynamic_slice_in_dim(x, mine * half, half, 0)
            parts[n] = keep + exchange(send, "rows", bit)
    for step in range(halving, len(bits)):
        for n, order in enumerate(orders):
            parts[n] = parts[n] + exchange(parts[n], "rows", order[step])
    for step in reversed(range(halving)):
        for n, order in enumerate(orders):
            x, bit = parts[n], order[step]
            other = exchange(x, "rows", bit)
            mine = ((me >> bit) & 1) == 1
            parts[n] = jnp.concatenate([jnp.where(mine, other, x), jnp.where(mine, x, other)], axis=0)
    return parts, [exchange(x, "grp", 0) for x in parts]


def summed_at_once(send, keep):
    size = lax.axis_size("rows")
    x = keep + exchange(send, "grp", 0)
    got = lax.all_to_all(x, "rows", 0, 0, tiled=True)
    mine = got.reshape(size, x.shape[0] // size, x.shape[1]).sum(0)
    same = jnp.broadcast_to(mine[None], (size,) + mine.shape).reshape(x.shape)
    x = lax.all_to_all(same, "rows", 0, 0, tiled=True)
    return x, exchange(x, "grp", 0)


def body(earlier, snapshots, later):
    n, k = earlier.shape
    p = snapshots.shape[1] // 2
    devices = lax.axis_size(AXES)
    scale = 1.0 / (n * devices)
    core = lax.axis_index("grp").astype(jnp.int32).reshape(1)
    blocks = k // p
    rows = (2 * blocks + blocks * (blocks + 1) // 2) * p
    unit = 2 * devices * 8
    parts = 3 if rows % (3 * unit) == 0 else 1

    def smem():
        return pl.BlockSpec(memory_space=pltpu.SMEM)

    def shape(*dims, dtype=F32):
        return jax.ShapeDtypeStruct(dims, dtype)

    def near(*dims, dtype=F32):
        return pltpu.VMEM(dims, dtype)

    def far(*dims, dtype=F32):
        return pltpu.HBM(dims, dtype)

    apart = pl.BlockSpec(memory_space=pl.ANY)
    inside = pl.BlockSpec(memory_space=pltpu.VMEM)

    def fixed(x):
        return pltpu.with_memory_space_constraint(x, pltpu.HBM)

    earlier, snapshots, later = fixed(earlier), fixed(snapshots), fixed(later)

    def call(kernel, name, room, ins, outs, scratch, flops, size, *args):
        return pl.pallas_call(
            kernel,
            in_specs=[s for s in ins],
            out_specs=[s for s, _ in outs],
            out_shape=[s for _, s in outs],
            scratch_shapes=scratch,
            name=name,
            cost_estimate=pl.CostEstimate(flops=flops, bytes_accessed=size, transcendentals=0),
            compiler_params=pltpu.CompilerParams(
                vmem_limit_bytes=room * MIB
            ),
        )(*args)

    short = 512 if n % 512 == 0 else n
    tiles = n // short
    dma = pltpu.SemaphoreType.DMA

    def held(*dims, dtype=F32):
        return pltpu.VMEM(dims, dtype)

    half = rows // parts // 2
    got = call(
        lambda *r: cross_kernel(parts, short, *r), "cross", 32,
        [smem(), apart, apart],
        [(apart, near(half, p))] * (2 * parts),
        [
            held(n, k, dtype=BF16),
            held(n, 2 * p, dtype=BF16),
            held(k, short, dtype=BF16),
            held(k, short, dtype=BF16),
            held(rows, p),
            dma((tiles, 2)), dma((parts, 2)),
        ],
        2 * n * rows * p, 2 * n * (k + 2 * p),
        core, earlier, snapshots,
    )
    own, other = summed(got[:parts], got[parts:], 1)

    u, w, z, h, t, send, keep = call(
        lambda *r: first_kernel(parts, short, scale, *r), "first", 50,
        [smem()] + [apart] * (2 * parts + 2),
        [
            (apart, far(n, p)),
            (apart, far(n, 2 * p, dtype=BF16)),
            (apart, far(k, p)),
            (apart, far(k, p)),
            (inside, near(p, p)),
            (inside, near(p, p)),
            (inside, near(p, p)),
        ],
        [
            held(rows, p),
            held(n, k, dtype=BF16),
            held(n, 2 * p, dtype=BF16),
            held(n, p),
            held(n, 2 * p, dtype=BF16),
            held(k, p),
            held(k, p),
            held(k, 3 * p, dtype=BF16),
            held(k, k, dtype=BF16),
            held(k, k, dtype=BF16),
            held(2 * p, p),
            held(p, p),
            dma((2 * parts,)), dma((tiles, 2)), dma((tiles, 2)), dma((2,)),
        ],
        2 * n * p * (3 * k + 4 * p) + 12 * k * k * p, n * (2 * k + 12 * p),
        core, *own, *other, earlier, snapshots,
    )
    own, other = summed_at_once(send, keep)

    got = call(
        lambda *r: second_kernel(3, short, scale, *r), "second", 46,
        [smem()] + [apart] * 4 + [inside] + [apart] * 4,
        [
            (apart, far(n, p, dtype=BF16)),
            (apart, far(n, 2 * p, dtype=BF16)),
            (inside, near(p, p)),
            (inside, near(p, p)),
        ] + [(inside, near(p, p))] * 6,
        [
            held(2 * p, p),
            held(k, p),
            held(k, p),
            held(n, k, dtype=BF16),
            held(n, p),
            held(n, 2 * p, dtype=BF16),
            held(n, 2 * p, dtype=BF16),
            held(n, p, dtype=BF16),
            held(n, 2 * p, dtype=BF16),
            held(p, p),
            held(2 * p, p, dtype=BF16),
            held(p, p, dtype=BF16),
            held(p, p, dtype=BF16),
            held(k, p, dtype=BF16),
            held(p, p, dtype=BF16),
            held(6 * p, p),
            held(p, p),
            dma((2,)), dma((2,)), dma((tiles, 4)), dma((tiles, 2)),
        ],
        2 * n * p * (k + 15 * p), n * (2 * k + 18 * p),
        core, own, other, fixed(z), fixed(h), t, earlier, fixed(u), fixed(w), later,
    )
    q_one, w2, r_one, expected = got[:4]
    own, other = summed(got[4:7], got[7:], 2)

    return tuple(call(
        lambda *r: last_kernel(3, short, *r), "last", 26,
        [smem()] + [apart] * 6 + [inside] * 2 + [apart] * 2,
        [
            (apart, far(n, 2 * p, dtype=BF16)),
            (inside, shape(2, p, p)),
            (inside, shape(2 * p, 2 * p)),
        ],
        [
            held(6 * p, p),
            held(n, p, dtype=BF16),
            held(n, 2 * p, dtype=BF16),
            held(n, 2 * p, dtype=BF16),
            held(p, p),
            held(p, p),
            held(2 * p, p, dtype=BF16),
            held(p, p, dtype=BF16),
            held(p, p, dtype=BF16),
            dma((6,)), dma((tiles, 2)), dma((tiles, 1)),
        ],
        2 * n * p * 4 * p, n * 10 * p,
        core, *own, *other, expected, r_one, fixed(q_one), fixed(w2),
    ))


def solution(mesh):
    spec = P(("rows", "grp"), None)
    return jax.shard_map(
        body,
        mesh=mesh,
        in_specs=(spec, spec, spec),
        out_specs=(spec, P(), P()),
        check_vma=False,
    )
```

```python
import jax
import jax.numpy as jnp
from jax import lax
from jax.experimental import pallas as pl
from jax.experimental.pallas import tpu as pltpu
from jax.sharding import PartitionSpec as P

AXES = ("rows", "grp")
HIGHEST = lax.Precision.HIGHEST
BF16 = jnp.bfloat16
F32 = jnp.float32
MIB = 2**20


def dot(a, b):
    return jnp.dot(a, b, preferred_element_type=F32)


def full(a, b):
    return jnp.dot(a, b, precision=HIGHEST, preferred_element_type=F32)


def wide(x):
    return x.astype(F32)


def split(x):
    high = x.astype(BF16)
    return high, (x - wide(high)).astype(BF16)


def thrice(a, b):
    return dot(a[0], b[0]) + dot(a[0], b[1]) + dot(a[1], b[0])


def factor_tile(groups, emit):
    count = len(groups)
    lane = lax.broadcasted_iota(jnp.int32, (8, 128), 1)
    sub = lax.broadcasted_iota(jnp.int32, (8, 128), 0)
    rows = list(groups)
    wide_strip = 4
    ups, boths = [], []
    for k in range(count):
        base = 8 * k
        first = k - k % wide_strip
        end = min(first + wide_strip, count)
        block = (lane >= 8 * first) & (lane < 8 * end)
        strip = rows[k]
        inside = (lane >= base) & (lane < base + 8)
        eye = jnp.where(lane == base + sub, 1.0, 0.0).astype(F32)
        mixed = jnp.where(inside, eye, strip)
        cols = [jnp.broadcast_to(strip[:, base + j:base + j + 1], (8, 128)) for j in range(8)]
        entry = {}
        for j in range(8):
            for i in range(j, 8):
                entry[i, j] = jnp.broadcast_to(cols[j][i:i + 1, :], (8, 128))
        scale = []
        low = {}
        for j in range(8):
            r = lax.rsqrt(entry[j, j])
            scale.append(r)
            for i in range(j + 1, 8):
                low[i, j] = entry[i, j] * r
            for c in range(j + 1, 8):
                for i in range(c, 8):
                    entry[i, c] = entry[i, c] - low[i, j] * low[c, j]
        upper, both = [], []
        for j in range(8):
            u = jnp.broadcast_to(strip[j:j + 1, :], (8, 128))
            v = jnp.broadcast_to(mixed[j:j + 1, :], (8, 128))
            for i in range(j):
                u = u - low[j, i] * upper[i]
                v = v - low[j, i] * both[i]
            upper.append(u * scale[j])
            both.append(v * scale[j])
        out_r = upper[0]
        out_m = both[0]
        for j in range(1, 8):
            out_r = jnp.where(sub == j, upper[j], out_r)
            out_m = jnp.where(sub == j, both[j], out_m)
        up = jnp.where(lane >= base + sub, out_r, 0.0)
        emit(k, up, jnp.where(lane <= base + sub, out_m, 0.0))
        ups.append(up)
        boths.append(jnp.where(block & (lane > base + sub), 0.0, out_m))
        for g in range(k + 1, end):
            w = rows[g]
            new = jnp.where(inside, 0.0, w)
            left = []
            for j in range(8):
                c = jnp.broadcast_to(w[:, base + j:base + j + 1], (8, 128))
                for i in range(j):
                    c = c - left[i] * low[j, i]
                c = c * scale[j]
                left.append(c)
                new = new - c * both[j]
            rows[g] = new
        if k + 1 == end and end < count:
            take = full(jnp.concatenate(ups, axis=0).T, jnp.concatenate(boths, axis=0))
            for g in range(end, count):
                rows[g] = jnp.where(block, 0.0, rows[g]) - take[8 * g:8 * g + 8]
            ups, boths = [], []


def factor(r_ref, m_ref):
    n = r_ref.shape[0]
    h = 128

    def step(t, carry):
        top = pl.multiple_of(t * h, h)
        groups = [r_ref[pl.ds(pl.multiple_of(top + 8 * g, 8), 8), pl.ds(top, h)] for g in range(h // 8)]

        def emit(k, r, m):
            at = pl.ds(pl.multiple_of(top + 8 * k, 8), 8)
            r_ref[at, pl.ds(top, h)] = r
            m_ref[at, pl.ds(top, h)] = m

        factor_tile(groups, emit)

        @pl.when(t == 0)
        def _():
            inv = m_ref[:h, :h]
            u = full(inv, r_ref[:h, h:])
            ut = u.T
            r_ref[:h, h:] = u
            r_ref[h:, h:] = r_ref[h:, h:] - full(ut, u)
            m_ref[h:, :h] = full(ut, inv)
            r_ref[h:, :h] = jnp.zeros((n - h, h), F32)
            m_ref[:h, h:] = jnp.zeros((h, n - h), F32)

        return carry

    lax.fori_loop(0, n // h, step, 0)
    m_ref[h:, :h] = -full(m_ref[h:, h:], m_ref[h:, :h])


def begin(copies, sems):
    for n, (source, target) in enumerate(copies):
        pltpu.make_async_copy(source, target, sems.at[n]).start()


def finish(copies, sems):
    for n, (source, target) in enumerate(copies):
        pltpu.make_async_copy(source, target, sems.at[n]).wait()


def places(core_ref, own, other, total_ref):
    mine = core_ref[0]
    copies = []
    at = 0
    for a, b in zip(own, other):
        h = a.shape[0]
        copies.append((a, total_ref.at[pl.ds(pl.multiple_of(at + mine * h, 8), h)]))
        copies.append((b, total_ref.at[pl.ds(pl.multiple_of(at + (1 - mine) * h, 8), h)]))
        at += 2 * h
    return copies


def tile_rows(i, tile):
    return pl.ds(pl.multiple_of(i * tile, tile), tile)


def at_tile(pairs, i, tile):
    rows = tile_rows(i, tile)
    return [(a.at[rows], b.at[rows]) for a, b in pairs]


def deal(core_ref, total_ref, scale, sends, keeps):
    mine = core_ref[0]
    at = 0
    for send, keep in zip(sends, keeps):
        h = send.shape[0]
        keep[...] = total_ref[pl.ds(pl.multiple_of(at + mine * h, 8), h)] * scale
        send[...] = total_ref[pl.ds(pl.multiple_of(at + (1 - mine) * h, 8), h)] * scale
        at += 2 * h


def cross_kernel(parts, scale, core_ref, e_ref, x_ref, *refs):
    sends, keeps, acc = refs[:parts], refs[parts:2 * parts], refs[-1]
    k = e_ref.shape[1]
    p = x_ref.shape[1] // 2
    step = pl.program_id(0)

    @pl.when(step == 0)
    def _():
        acc[...] = jnp.zeros_like(acc)

    et = e_ref[...].T
    at = 0
    for c in range(2):
        acc[at:at + k] += dot(et, x_ref[:, c * p:(c + 1) * p])
        at += k
    for j in range(k // p):
        m = (j + 1) * p
        acc[at:at + m] += dot(et[:m], e_ref[:, j * p:(j + 1) * p])
        at += m

    @pl.when(step == pl.num_programs(0) - 1)
    def _():
        deal(core_ref, acc, scale, sends, keeps)


def first_kernel(parts, tile, scale, core_ref, *refs):
    own, other = refs[:parts], refs[parts:2 * parts]
    (e_in, x_in, u_out, w_out, z_out, h_out, t_ref, send, keep,
     total, e_ref, x_ref, u_ref, w_ref, z_ref, h_ref, b_ref, offh, offl, acc, hl,
     sum_sems, in_sems, out_sems, small_sems) = refs[2 * parts:]
    n, k = e_ref.shape
    p = u_ref.shape[1]
    tiles = n // tile
    sums = places(core_ref, own, other, total)
    inputs = [(e_in, e_ref), (x_in, x_ref)]
    outputs = [(u_ref, u_out), (w_ref, w_out)]
    small = [(z_ref, z_out), (h_ref, h_out)]
    begin(sums, sum_sems)
    acc[...] = jnp.zeros_like(acc)
    hl[...] = jnp.zeros_like(hl)
    finish(sums, sum_sems)
    for i in range(tiles):
        begin(at_tile(inputs, i, tile), in_sems.at[i])

    at = 2 * k
    for j in range(k // p):
        cols = slice(j * p, (j + 1) * p)
        for i in range(j + 1):
            block = total[at:at + p]
            at += p
            if i == j:
                a = lax.broadcasted_iota(jnp.int32, (p, p), 0)
                b = lax.broadcasted_iota(jnp.int32, (p, p), 1)
                block = block - jnp.where(a == b, 1.0, 0.0)
            high, low = split(block)
            rows = slice(i * p, (i + 1) * p)
            offh[rows, cols] = high
            offl[rows, cols] = low
            if i < j:
                offh[cols, rows] = high.T
                offl[cols, rows] = low.T
    for c in range(2):
        coef = total[c * k:(c + 1) * k]
        b = coef.astype(BF16)
        b_ref[:, c * p:(c + 1) * p] = b
        after = (coef - wide(b)) - dot(offh[...], b) - dot(offl[...], b)
        if c == 0:
            sb = after.astype(BF16)
            b_ref[:, 2 * p:] = sb
            against = (after - wide(sb)) - dot(offh[...], sb) - dot(offl[...], sb)
            h_ref[...] = against
        else:
            z_ref[...] = after
            high, low = split(against.T)
            t_ref[...] = dot(high, b) + dot(low, b)
    begin(small, small_sems)

    for i in range(tiles):
        finish(at_tile(inputs, i, tile), in_sems.at[i])

    def project(i):
        rows = tile_rows(i, tile)
        t = dot(e_ref[rows, :], b_ref[...])
        once = wide((wide(x_ref[rows, :p]) - t[:, :p]).astype(BF16))
        u_ref[rows, :] = wide(x_ref[rows, p:]) - t[:, p:2 * p]
        high, low = split(once - t[:, 2 * p:])
        w_ref[rows, :p] = high
        w_ref[rows, p:] = low

    def gather(i):
        rows = tile_rows(i, tile)
        high = w_ref[rows, :p]
        both = jnp.concatenate([high.T, w_ref[rows, p:].T], axis=0)
        square = dot(both, high)
        acc[:p] += square[:p]
        hl[...] += square[p:]
        other_two = dot(both, x_ref[rows, p:])
        acc[p:] += other_two[:p] + other_two[p:]

    def step(i, carry):
        gather(i)
        project(i + 1)
        begin(at_tile(outputs, i + 1, tile), out_sems.at[i + 1])
        return carry

    project(0)
    begin(at_tile(outputs, 0, tile), out_sems.at[0])
    lax.fori_loop(0, tiles - 1, step, 0)
    gather(tiles - 1)
    acc[:p] = acc[:p] + hl[...] + hl[...].T
    deal(core_ref, acc, scale, [send], [keep])
    for i in range(tiles):
        finish(at_tile(outputs, i, tile), out_sems.at[i])
    finish(small, small_sems)


def second_kernel(parts, tile, scale, core_ref, own, other, z_in, h_in, t_ref, e_in, u_in, w_in, l_in, *refs):
    q_out, w2_out, r_ref, x_ref = refs[:4]
    sends, keeps = refs[4:4 + parts], refs[4 + parts:4 + 2 * parts]
    (total, z_ref, h_ref, e_ref, u_ref, w_ref, l_ref, q_ref, w2_ref, m_ref, ih, il, db, ub, lb, acc, hl,
     sum_sems, small_sems, in_sems, out_sems) = refs[4 + 2 * parts:]
    p = r_ref.shape[0]
    n = e_ref.shape[0]
    tiles = n // tile
    sums = places(core_ref, [own], [other], total)
    small = [(z_in, z_ref), (h_in, h_ref)]
    inputs = [(e_in, e_ref), (u_in, u_ref), (w_in, w_ref), (l_in, l_ref)]
    outputs = [(q_ref, q_out), (w2_ref, w2_out)]
    begin(sums, sum_sems)
    acc[...] = jnp.zeros_like(acc)
    hl[...] = jnp.zeros_like(hl)
    finish(sums, sum_sems)
    begin(small, small_sems)
    for i in range(tiles):
        begin(at_tile(inputs, i, tile), in_sems.at[i])

    r_ref[...] = total[:p]
    factor(r_ref, m_ref)
    inv = m_ref[...]
    high, low = split(inv.T)
    ih[:p] = high
    ih[p:] = high
    il[...] = low
    d = full(inv, total[p:])
    d_b = d.astype(BF16)
    db[...] = d_b
    finish(small, small_sems)
    inv_s = split(inv)
    against = split(h_ref[...])
    at = split(h_ref[...].T)
    turned = split(dot(high, d_b) + dot(low, d_b))
    upper = (z_ref[...] - thrice(against, turned)).astype(BF16)
    ub[...] = upper
    lower = (d - wide(d_b)) - thrice(inv_s, split(t_ref[...]))
    lower_b = lower.astype(BF16)
    lb[...] = lower_b
    x_ref[...] = (lower - wide(lower_b)) - thrice(inv_s, split(dot(at[0], upper) + dot(at[1], upper)))

    for i in range(tiles):
        finish(at_tile(inputs, i, tile), in_sems.at[i])

    def project(i):
        rows = tile_rows(i, tile)
        q = (dot(w_ref[rows, :], ih[...]) + dot(w_ref[rows, :p], il[...])).astype(BF16)
        q_ref[rows, :] = q
        once = wide((u_ref[rows, :] - dot(q, db[...])).astype(BF16))
        high, low = split(once - dot(e_ref[rows, :], ub[...]) - dot(q, lb[...]))
        w2_ref[rows, :p] = high
        w2_ref[rows, p:] = low

    def gather(i):
        rows = tile_rows(i, tile)
        high, low = w2_ref[rows, :p], w2_ref[rows, p:]
        qt = q_ref[rows, :].T
        left = jnp.concatenate([high.T, low.T, qt], axis=0)
        square = dot(left, high)
        acc[:p] += square[:p]
        hl[...] += square[p:2 * p]
        acc[p:2 * p] += square[2 * p:] + dot(qt, low)
        for c in range(2):
            mixed = dot(left, l_ref[rows, c * p:(c + 1) * p])
            acc[(2 + c) * p:(3 + c) * p] += mixed[:p] + mixed[p:2 * p]
            acc[(4 + c) * p:(5 + c) * p] += mixed[2 * p:]

    def step(i, carry):
        gather(i)
        project(i + 1)
        begin(at_tile(outputs, i + 1, tile), out_sems.at[i + 1])
        return carry

    project(0)
    begin(at_tile(outputs, 0, tile), out_sems.at[0])
    lax.fori_loop(0, tiles - 1, step, 0)
    gather(tiles - 1)
    acc[:p] = acc[:p] + hl[...] + hl[...].T
    deal(core_ref, acc, scale, sends, keeps)
    for i in range(tiles):
        finish(at_tile(outputs, i, tile), out_sems.at[i])


def last_kernel(parts, tile, core_ref, *refs):
    own, other = refs[:parts], refs[parts:2 * parts]
    (x_ref, r1_ref, q_in, w_in, basis_out, factors, shift,
     total, q_ref, w_ref, basis, r_ref, m_ref, ih, il, back, sum_sems, in_sems, out_sems) = refs[2 * parts:]
    p = r_ref.shape[0]
    tiles = q_ref.shape[0] // tile
    sums = places(core_ref, own, other, total)
    inputs = [(q_in, q_ref), (w_in, w_ref)]
    outputs = [(basis, basis_out)]
    begin(sums, sum_sems)
    finish(sums, sum_sems)
    for i in range(tiles):
        begin(at_tile(inputs, i, tile), in_sems.at[i])

    res = total[p:2 * p]
    off = res - x_ref[...]
    off_b = off.astype(BF16)
    offt = off.T.astype(BF16)
    cut = dot(offt, res.astype(BF16))
    r_ref[...] = total[:p] - cut - cut.T + dot(offt, off_b)
    factor(r_ref, m_ref)
    inv = m_ref[...]
    high, low = split(inv.T)
    ih[:p] = high
    ih[p:] = high
    il[...] = low
    back[...] = dot(off_b, high).astype(BF16)

    def step(i, carry):
        rows = tile_rows(i, tile)
        finish(at_tile(inputs, i, tile), in_sems.at[i])
        q = dot(w_ref[rows, :], ih[...]) + dot(w_ref[rows, :p], il[...]) - dot(q_ref[rows, :], back[...])
        basis[rows, :p] = q_ref[rows, :]
        basis[rows, p:] = q.astype(BF16)
        begin(at_tile(outputs, i, tile), out_sems.at[i])
        return carry

    lax.fori_loop(0, tiles, step, 0)
    inv_s = split(m_ref[...])
    factors[0] = r1_ref[...]
    factors[1] = r_ref[...]
    for c in range(2):
        cols = slice(c * p, (c + 1) * p)
        early = total[(4 + c) * p:(5 + c) * p]
        shift[:p, cols] = early
        late = total[(2 + c) * p:(3 + c) * p] - dot(offt, early.astype(BF16))
        shift[p:, cols] = thrice(inv_s, split(late))
    for i in range(tiles):
        finish(at_tile(outputs, i, tile), out_sems.at[i])


def exchange(x, axis, bit):
    size = lax.axis_size(axis)
    return lax.ppermute(x, axis, [(i, i ^ (1 << bit)) for i in range(size)])


def summed(sends, keeps, tail):
    bits = list(range(lax.axis_size("rows").bit_length() - 1))
    turn, last = bits[:-1], bits[-1:]
    orders = [turn[n % len(turn):] + turn[:n % len(turn)] + last for n in range(len(sends))]
    me = lax.axis_index("rows")
    terms = [[keep, exchange(send, "grp", 0)] for send, keep in zip(sends, keeps)]
    halving = len(bits) - tail
    for step in range(halving):
        for n, order in enumerate(orders):
            bit = order[step]
            half = terms[n][0].shape[0] // 2
            mine = (me >> bit) & 1
            send, keep = (
                sum(lax.dynamic_slice_in_dim(x, at * half, half, 0) for x in terms[n])
                for at in (1 - mine, mine)
            )
            terms[n] = [keep, exchange(send, "rows", bit)]
    parts = [a + b for a, b in terms]
    for step in range(halving, len(bits)):
        for n, order in enumerate(orders):
            parts[n] = parts[n] + exchange(parts[n], "rows", order[step])
    for step in reversed(range(halving)):
        for n, order in enumerate(orders):
            x, bit = parts[n], order[step]
            other = exchange(x, "rows", bit)
            mine = ((me >> bit) & 1) == 1
            parts[n] = jnp.concatenate([jnp.where(mine, other, x), jnp.where(mine, x, other)], axis=0)
    return parts, [exchange(x, "grp", 0) for x in parts]


def summed_at_once(send, keep):
    size = lax.axis_size("rows")
    x = keep + exchange(send, "grp", 0)
    got = lax.all_to_all(x, "rows", 0, 0, tiled=True)
    mine = got.reshape(size, x.shape[0] // size, x.shape[1]).sum(0)
    same = jnp.broadcast_to(mine[None], (size,) + mine.shape).reshape(x.shape)
    x = lax.all_to_all(same, "rows", 0, 0, tiled=True)
    return x, exchange(x, "grp", 0)


def body(earlier, snapshots, later):
    n, k = earlier.shape
    p = snapshots.shape[1] // 2
    devices = lax.axis_size(AXES)
    scale = 1.0 / (n * devices)
    core = lax.axis_index("grp").astype(jnp.int32).reshape(1)
    blocks = k // p
    rows = (2 * blocks + blocks * (blocks + 1) // 2) * p
    unit = 2 * devices * 8
    parts = 3 if rows % (3 * unit) == 0 else 1
    tile = 1024 if n % 1024 == 0 else n

    def smem():
        return pl.BlockSpec(memory_space=pltpu.SMEM)

    def whole(*shape):
        return pl.BlockSpec(shape, lambda i: (0,) * len(shape))

    def tiled(cols):
        return pl.BlockSpec((tile, cols), lambda i: (i, 0))

    def shape(*dims, dtype=F32):
        return jax.ShapeDtypeStruct(dims, dtype)

    def near(*dims, dtype=F32):
        return pltpu.VMEM(dims, dtype)

    def far(*dims, dtype=F32):
        return pltpu.HBM(dims, dtype)

    apart = pl.BlockSpec(memory_space=pl.ANY)
    inside = pl.BlockSpec(memory_space=pltpu.VMEM)

    def fixed(x):
        return pltpu.with_memory_space_constraint(x, pltpu.HBM)

    earlier, snapshots, later = fixed(earlier), fixed(snapshots), fixed(later)

    def call(kernel, name, room, ins, outs, scratch, flops, size, *args, grid=None):
        return pl.pallas_call(
            kernel,
            grid=(n // tile,) if grid is None else grid,
            in_specs=[s for s in ins],
            out_specs=[s for s, _ in outs],
            out_shape=[s for _, s in outs],
            scratch_shapes=scratch,
            name=name,
            cost_estimate=pl.CostEstimate(flops=flops, bytes_accessed=size, transcendentals=0),
            compiler_params=pltpu.CompilerParams(
                vmem_limit_bytes=room * MIB
            ),
        )(*args)

    short = 512 if n % 512 == 0 else n
    tiles = n // short
    dma = pltpu.SemaphoreType.DMA

    def held(*dims, dtype=F32):
        return pltpu.VMEM(dims, dtype)

    half = rows // parts // 2
    halves = [(whole(half, p), near(half, p))] * (2 * parts)
    got = call(
        lambda *r: cross_kernel(parts, scale, *r), "cross", 32,
        [smem(), tiled(k), tiled(2 * p)],
        halves,
        [pltpu.VMEM((rows, p), F32)],
        2 * n * rows * p, 2 * n * (k + 2 * p),
        core, earlier, snapshots,
    )
    own, other = summed(got[:parts], got[parts:], 1)

    short = 512 if n % 512 == 0 else n
    tiles = n // short
    dma = pltpu.SemaphoreType.DMA

    def held(*dims, dtype=F32):
        return pltpu.VMEM(dims, dtype)

    u, w, z, h, t, send, keep = call(
        lambda *r: first_kernel(parts, short, scale, *r), "first", 50,
        [smem()] + [apart] * (2 * parts + 2),
        [
            (apart, far(n, p)),
            (apart, far(n, 2 * p, dtype=BF16)),
            (apart, far(k, p)),
            (apart, far(k, p)),
            (inside, near(p, p)),
            (inside, near(p, p)),
            (inside, near(p, p)),
        ],
        [
            held(rows, p),
            held(n, k, dtype=BF16),
            held(n, 2 * p, dtype=BF16),
            held(n, p),
            held(n, 2 * p, dtype=BF16),
            held(k, p),
            held(k, p),
            held(k, 3 * p, dtype=BF16),
            held(k, k, dtype=BF16),
            held(k, k, dtype=BF16),
            held(2 * p, p),
            held(p, p),
            dma((2 * parts,)), dma((tiles, 2)), dma((tiles, 2)), dma((2,)),
        ],
        2 * n * p * (3 * k + 4 * p) + 12 * k * k * p, n * (2 * k + 12 * p),
        core, *own, *other, earlier, snapshots, grid=(),
    )
    own, other = summed_at_once(send, keep)

    got = call(
        lambda *r: second_kernel(3, short, scale, *r), "second", 46,
        [smem()] + [apart] * 4 + [inside] + [apart] * 4,
        [
            (apart, far(n, p, dtype=BF16)),
            (apart, far(n, 2 * p, dtype=BF16)),
            (inside, near(p, p)),
            (inside, near(p, p)),
        ] + [(inside, near(p, p))] * 6,
        [
            held(2 * p, p),
            held(k, p),
            held(k, p),
            held(n, k, dtype=BF16),
            held(n, p),
            held(n, 2 * p, dtype=BF16),
            held(n, 2 * p, dtype=BF16),
            held(n, p, dtype=BF16),
            held(n, 2 * p, dtype=BF16),
            held(p, p),
            held(2 * p, p, dtype=BF16),
            held(p, p, dtype=BF16),
            held(p, p, dtype=BF16),
            held(k, p, dtype=BF16),
            held(p, p, dtype=BF16),
            held(6 * p, p),
            held(p, p),
            dma((2,)), dma((2,)), dma((tiles, 4)), dma((tiles, 2)),
        ],
        2 * n * p * (k + 15 * p), n * (2 * k + 18 * p),
        core, own, other, fixed(z), fixed(h), t, earlier, fixed(u), fixed(w), later, grid=(),
    )
    q_one, w2, r_one, expected = got[:4]
    own, other = summed(got[4:7], got[7:], 2)

    return tuple(call(
        lambda *r: last_kernel(3, short, *r), "last", 26,
        [smem()] + [apart] * 6 + [inside] * 2 + [apart] * 2,
        [
            (apart, far(n, 2 * p, dtype=BF16)),
            (inside, shape(2, p, p)),
            (inside, shape(2 * p, 2 * p)),
        ],
        [
            held(6 * p, p),
            held(n, p, dtype=BF16),
            held(n, 2 * p, dtype=BF16),
            held(n, 2 * p, dtype=BF16),
            held(p, p),
            held(p, p),
            held(2 * p, p, dtype=BF16),
            held(p, p, dtype=BF16),
            held(p, p, dtype=BF16),
            dma((6,)), dma((tiles, 2)), dma((tiles, 1)),
        ],
        2 * n * p * 4 * p, n * 10 * p,
        core, *own, *other, expected, r_one, fixed(q_one), fixed(w2), grid=(),
    ))


def solution(mesh):
    spec = P(("rows", "grp"), None)
    return jax.shard_map(
        body,
        mesh=mesh,
        in_specs=(spec, spec, spec),
        out_specs=(spec, P(), P()),
        check_vma=False,
    )
```

```python
import jax
import jax.numpy as jnp
from jax import lax
from jax.experimental import pallas as pl
from jax.experimental.pallas import tpu as pltpu
from jax.sharding import PartitionSpec as P

AXES = ("rows", "grp")
HIGHEST = lax.Precision.HIGHEST
BF16 = jnp.bfloat16
F32 = jnp.float32
MIB = 2**20


def dot(a, b):
    return jnp.dot(a, b, preferred_element_type=F32)


def full(a, b):
    return jnp.dot(a, b, precision=HIGHEST, preferred_element_type=F32)


def wide(x):
    return x.astype(F32)


def split(x):
    high = x.astype(BF16)
    return high, (x - wide(high)).astype(BF16)


def thrice(a, b):
    return dot(a[0], b[0]) + dot(a[0], b[1]) + dot(a[1], b[0])


def factor_tile(groups, emit):
    count = len(groups)
    lane = lax.broadcasted_iota(jnp.int32, (8, 128), 1)
    sub = lax.broadcasted_iota(jnp.int32, (8, 128), 0)
    rows = list(groups)
    wide_strip = 8
    ups, boths = [], []
    for k in range(count):
        base = 8 * k
        first = k - k % wide_strip
        end = min(first + wide_strip, count)
        block = (lane >= 8 * first) & (lane < 8 * end)
        strip = rows[k]
        inside = (lane >= base) & (lane < base + 8)
        eye = jnp.where(lane == base + sub, 1.0, 0.0).astype(F32)
        mixed = jnp.where(inside, eye, strip)
        cols = [jnp.broadcast_to(strip[:, base + j:base + j + 1], (8, 128)) for j in range(8)]
        entry = {}
        for j in range(8):
            for i in range(j, 8):
                entry[i, j] = jnp.broadcast_to(cols[j][i:i + 1, :], (8, 128))
        scale = []
        low = {}
        for j in range(8):
            r = lax.rsqrt(entry[j, j])
            scale.append(r)
            for i in range(j + 1, 8):
                low[i, j] = entry[i, j] * r
            for c in range(j + 1, 8):
                for i in range(c, 8):
                    entry[i, c] = entry[i, c] - low[i, j] * low[c, j]
        upper, both = [], []
        for j in range(8):
            u = jnp.broadcast_to(strip[j:j + 1, :], (8, 128))
            v = jnp.broadcast_to(mixed[j:j + 1, :], (8, 128))
            for i in range(j):
                u = u - low[j, i] * upper[i]
                v = v - low[j, i] * both[i]
            upper.append(u * scale[j])
            both.append(v * scale[j])
        out_r = upper[0]
        out_m = both[0]
        for j in range(1, 8):
            out_r = jnp.where(sub == j, upper[j], out_r)
            out_m = jnp.where(sub == j, both[j], out_m)
        up = jnp.where(lane >= base + sub, out_r, 0.0)
        emit(k, up, jnp.where(lane <= base + sub, out_m, 0.0))
        ups.append(up)
        boths.append(jnp.where(block & (lane > base + sub), 0.0, out_m))
        for g in range(k + 1, end):
            w = rows[g]
            new = jnp.where(inside, 0.0, w)
            left = []
            for j in range(8):
                c = jnp.broadcast_to(w[:, base + j:base + j + 1], (8, 128))
                for i in range(j):
                    c = c - left[i] * low[j, i]
                c = c * scale[j]
                left.append(c)
                new = new - c * both[j]
            rows[g] = new
        if k + 1 == end and end < count:
            take = full(jnp.concatenate(ups, axis=0).T, jnp.concatenate(boths, axis=0))
            for g in range(end, count):
                rows[g] = jnp.where(block, 0.0, rows[g]) - take[8 * g:8 * g + 8]
            ups, boths = [], []


def factor(r_ref, m_ref):
    n = r_ref.shape[0]
    h = 128

    def step(t, carry):
        top = pl.multiple_of(t * h, h)
        groups = [r_ref[pl.ds(pl.multiple_of(top + 8 * g, 8), 8), pl.ds(top, h)] for g in range(h // 8)]

        def emit(k, r, m):
            at = pl.ds(pl.multiple_of(top + 8 * k, 8), 8)
            r_ref[at, pl.ds(top, h)] = r
            m_ref[at, pl.ds(top, h)] = m

        factor_tile(groups, emit)

        @pl.when(t == 0)
        def _():
            inv = m_ref[:h, :h]
            u = full(inv, r_ref[:h, h:])
            ut = u.T
            r_ref[:h, h:] = u
            r_ref[h:, h:] = r_ref[h:, h:] - full(ut, u)
            m_ref[h:, :h] = full(ut, inv)
            r_ref[h:, :h] = jnp.zeros((n - h, h), F32)
            m_ref[:h, h:] = jnp.zeros((h, n - h), F32)

        return carry

    lax.fori_loop(0, n // h, step, 0)
    m_ref[h:, :h] = -full(m_ref[h:, h:], m_ref[h:, :h])


def begin(copies, sems):
    for n, (source, target) in enumerate(copies):
        pltpu.make_async_copy(source, target, sems.at[n]).start()


def finish(copies, sems):
    for n, (source, target) in enumerate(copies):
        pltpu.make_async_copy(source, target, sems.at[n]).wait()


def places(core_ref, own, other, total_ref):
    mine = core_ref[0]
    copies = []
    at = 0
    for a, b in zip(own, other):
        h = a.shape[0]
        copies.append((a, total_ref.at[pl.ds(pl.multiple_of(at + mine * h, 8), h)]))
        copies.append((b, total_ref.at[pl.ds(pl.multiple_of(at + (1 - mine) * h, 8), h)]))
        at += 2 * h
    return copies


def tile_rows(i, tile):
    return pl.ds(pl.multiple_of(i * tile, tile), tile)


def at_tile(pairs, i, tile):
    rows = tile_rows(i, tile)
    return [(a.at[rows], b.at[rows]) for a, b in pairs]


def deal(core_ref, total_ref, scale, sends, keeps):
    mine = core_ref[0]
    at = 0
    for send, keep in zip(sends, keeps):
        h = send.shape[0]
        keep[...] = total_ref[pl.ds(pl.multiple_of(at + mine * h, 8), h)] * scale
        send[...] = total_ref[pl.ds(pl.multiple_of(at + (1 - mine) * h, 8), h)] * scale
        at += 2 * h


def cross_kernel(parts, scale, core_ref, e_ref, x_ref, *refs):
    sends, keeps, acc = refs[:parts], refs[parts:2 * parts], refs[-1]
    k = e_ref.shape[1]
    p = x_ref.shape[1] // 2
    step = pl.program_id(0)

    @pl.when(step == 0)
    def _():
        acc[...] = jnp.zeros_like(acc)

    et = e_ref[...].T
    at = 0
    for c in range(2):
        acc[at:at + k] += dot(et, x_ref[:, c * p:(c + 1) * p])
        at += k
    for j in range(k // p):
        m = (j + 1) * p
        acc[at:at + m] += dot(et[:m], e_ref[:, j * p:(j + 1) * p])
        at += m

    @pl.when(step == pl.num_programs(0) - 1)
    def _():
        deal(core_ref, acc, scale, sends, keeps)


def first_kernel(parts, tile, scale, core_ref, *refs):
    own, other = refs[:parts], refs[parts:2 * parts]
    (e_in, x_in, u_out, w_out, z_out, h_out, t_ref, send, keep,
     total, e_ref, x_ref, u_ref, w_ref, z_ref, h_ref, b_ref, offh, offl, acc, hl,
     sum_sems, in_sems, out_sems, small_sems) = refs[2 * parts:]
    n, k = e_ref.shape
    p = u_ref.shape[1]
    tiles = n // tile
    sums = places(core_ref, own, other, total)
    inputs = [(e_in, e_ref), (x_in, x_ref)]
    outputs = [(u_ref, u_out), (w_ref, w_out)]
    small = [(z_ref, z_out), (h_ref, h_out)]
    begin(sums, sum_sems)
    acc[...] = jnp.zeros_like(acc)
    hl[...] = jnp.zeros_like(hl)
    finish(sums, sum_sems)
    for i in range(tiles):
        begin(at_tile(inputs, i, tile), in_sems.at[i])

    at = 2 * k
    for j in range(k // p):
        cols = slice(j * p, (j + 1) * p)
        for i in range(j + 1):
            block = total[at:at + p]
            at += p
            if i == j:
                a = lax.broadcasted_iota(jnp.int32, (p, p), 0)
                b = lax.broadcasted_iota(jnp.int32, (p, p), 1)
                block = block - jnp.where(a == b, 1.0, 0.0)
            high, low = split(block)
            rows = slice(i * p, (i + 1) * p)
            offh[rows, cols] = high
            offl[rows, cols] = low
            if i < j:
                offh[cols, rows] = high.T
                offl[cols, rows] = low.T
    for c in range(2):
        coef = total[c * k:(c + 1) * k]
        b = coef.astype(BF16)
        b_ref[:, c * p:(c + 1) * p] = b
        after = (coef - wide(b)) - dot(offh[...], b) - dot(offl[...], b)
        if c == 0:
            sb = after.astype(BF16)
            b_ref[:, 2 * p:] = sb
            against = (after - wide(sb)) - dot(offh[...], sb) - dot(offl[...], sb)
            h_ref[...] = against
        else:
            z_ref[...] = after
            high, low = split(against)
            bt = b.T
            t_ref[...] = (dot(bt, high) + dot(bt, low)).T
    begin(small, small_sems)

    for i in range(tiles):
        finish(at_tile(inputs, i, tile), in_sems.at[i])

    def project(i):
        rows = tile_rows(i, tile)
        t = dot(e_ref[rows, :], b_ref[...])
        once = wide((wide(x_ref[rows, :p]) - t[:, :p]).astype(BF16))
        u_ref[rows, :] = wide(x_ref[rows, p:]) - t[:, p:2 * p]
        high, low = split(once - t[:, 2 * p:])
        w_ref[rows, :p] = high
        w_ref[rows, p:] = low

    def gather(i):
        rows = tile_rows(i, tile)
        high = w_ref[rows, :p]
        both = jnp.concatenate([high.T, w_ref[rows, p:].T], axis=0)
        square = dot(both, high)
        acc[:p] += square[:p]
        hl[...] += square[p:]
        other_two = dot(both, x_ref[rows, p:])
        acc[p:] += other_two[:p] + other_two[p:]

    def step(i, carry):
        gather(i)
        project(i + 1)
        begin(at_tile(outputs, i + 1, tile), out_sems.at[i + 1])
        return carry

    project(0)
    begin(at_tile(outputs, 0, tile), out_sems.at[0])
    lax.fori_loop(0, tiles - 1, step, 0)
    gather(tiles - 1)
    acc[:p] = acc[:p] + hl[...] + hl[...].T
    deal(core_ref, acc, scale, [send], [keep])
    for i in range(tiles):
        finish(at_tile(outputs, i, tile), out_sems.at[i])
    finish(small, small_sems)


def second_kernel(parts, tile, scale, core_ref, own, other, z_in, h_in, t_ref, e_in, u_in, w_in, l_in, *refs):
    q_out, w2_out, r_ref, x_ref = refs[:4]
    sends, keeps = refs[4:4 + parts], refs[4 + parts:4 + 2 * parts]
    (total, z_ref, h_ref, e_ref, u_ref, w_ref, l_ref, q_ref, w2_ref, m_ref, ih, il, db, ub, lb, acc, hl,
     sum_sems, small_sems, in_sems, out_sems) = refs[4 + 2 * parts:]
    p = r_ref.shape[0]
    n = e_ref.shape[0]
    tiles = n // tile
    sums = places(core_ref, [own], [other], total)
    small = [(z_in, z_ref), (h_in, h_ref)]
    inputs = [(e_in, e_ref), (u_in, u_ref), (w_in, w_ref), (l_in, l_ref)]
    outputs = [(q_ref, q_out), (w2_ref, w2_out)]
    begin(sums, sum_sems)
    acc[...] = jnp.zeros_like(acc)
    hl[...] = jnp.zeros_like(hl)
    finish(sums, sum_sems)
    begin(small, small_sems)
    for i in range(tiles):
        begin(at_tile(inputs, i, tile), in_sems.at[i])

    r_ref[...] = total[:p]
    factor(r_ref, m_ref)
    inv = m_ref[...]
    high, low = split(inv.T)
    ih[:p] = high
    ih[p:] = high
    il[...] = low
    d = full(inv, total[p:])
    d_b = d.astype(BF16)
    db[...] = d_b
    finish(small, small_sems)
    inv_s = split(inv)
    against = split(h_ref[...])
    turned = split(dot(high, d_b) + dot(low, d_b))
    upper = (z_ref[...] - thrice(against, turned)).astype(BF16)
    ub[...] = upper
    lower = (d - wide(d_b)) - thrice(inv_s, split(t_ref[...]))
    lower_b = lower.astype(BF16)
    lb[...] = lower_b
    upt = upper.T
    both = (dot(upt, against[0]) + dot(upt, against[1])).T
    x_ref[...] = (lower - wide(lower_b)) - thrice(inv_s, split(both))

    for i in range(tiles):
        finish(at_tile(inputs, i, tile), in_sems.at[i])

    def project(i):
        rows = tile_rows(i, tile)
        q = (dot(w_ref[rows, :], ih[...]) + dot(w_ref[rows, :p], il[...])).astype(BF16)
        q_ref[rows, :] = q
        once = wide((u_ref[rows, :] - dot(q, db[...])).astype(BF16))
        high, low = split(once - dot(e_ref[rows, :], ub[...]) - dot(q, lb[...]))
        w2_ref[rows, :p] = high
        w2_ref[rows, p:] = low

    def gather(i):
        rows = tile_rows(i, tile)
        high, low = w2_ref[rows, :p], w2_ref[rows, p:]
        qt = q_ref[rows, :].T
        left = jnp.concatenate([high.T, low.T, qt], axis=0)
        square = dot(left, high)
        acc[:p] += square[:p]
        hl[...] += square[p:2 * p]
        acc[p:2 * p] += square[2 * p:] + dot(qt, low)
        for c in range(2):
            mixed = dot(left, l_ref[rows, c * p:(c + 1) * p])
            acc[(2 + c) * p:(3 + c) * p] += mixed[:p] + mixed[p:2 * p]
            acc[(4 + c) * p:(5 + c) * p] += mixed[2 * p:]

    def step(i, carry):
        gather(i)
        project(i + 1)
        begin(at_tile(outputs, i + 1, tile), out_sems.at[i + 1])
        return carry

    project(0)
    begin(at_tile(outputs, 0, tile), out_sems.at[0])
    lax.fori_loop(0, tiles - 1, step, 0)
    gather(tiles - 1)
    acc[:p] = acc[:p] + hl[...] + hl[...].T
    deal(core_ref, acc, scale, sends, keeps)
    for i in range(tiles):
        finish(at_tile(outputs, i, tile), out_sems.at[i])


def last_kernel(parts, tile, core_ref, *refs):
    own, other = refs[:parts], refs[parts:2 * parts]
    (x_ref, r1_ref, q_in, w_in, basis_out, factors, shift,
     total, q_ref, w_ref, basis, r_ref, m_ref, ih, il, back, sum_sems, in_sems, out_sems) = refs[2 * parts:]
    p = r_ref.shape[0]
    tiles = q_ref.shape[0] // tile
    sums = places(core_ref, own, other, total)
    inputs = [(q_in, q_ref), (w_in, w_ref)]
    outputs = [(basis, basis_out)]
    begin(sums, sum_sems)
    finish(sums, sum_sems)
    for i in range(tiles):
        begin(at_tile(inputs, i, tile), in_sems.at[i])

    res = total[p:2 * p]
    off = res - x_ref[...]
    off_b = off.astype(BF16)
    offt = off.T.astype(BF16)
    cut = dot(offt, res.astype(BF16))
    r_ref[...] = total[:p] - cut - cut.T + dot(offt, off_b)
    factor(r_ref, m_ref)
    inv = m_ref[...]
    high, low = split(inv.T)
    ih[:p] = high
    ih[p:] = high
    il[...] = low
    back[...] = dot(off_b, high).astype(BF16)

    def step(i, carry):
        rows = tile_rows(i, tile)
        finish(at_tile(inputs, i, tile), in_sems.at[i])
        q = dot(w_ref[rows, :], ih[...]) + dot(w_ref[rows, :p], il[...]) - dot(q_ref[rows, :], back[...])
        basis[rows, :p] = q_ref[rows, :]
        basis[rows, p:] = q.astype(BF16)
        begin(at_tile(outputs, i, tile), out_sems.at[i])
        return carry

    lax.fori_loop(0, tiles, step, 0)
    inv_s = split(m_ref[...])
    factors[0] = r1_ref[...]
    factors[1] = r_ref[...]
    for c in range(2):
        cols = slice(c * p, (c + 1) * p)
        early = total[(4 + c) * p:(5 + c) * p]
        shift[:p, cols] = early
        late = total[(2 + c) * p:(3 + c) * p] - dot(offt, early.astype(BF16))
        shift[p:, cols] = thrice(inv_s, split(late))
    for i in range(tiles):
        finish(at_tile(outputs, i, tile), out_sems.at[i])


def exchange(x, axis, bit):
    size = lax.axis_size(axis)
    return lax.ppermute(x, axis, [(i, i ^ (1 << bit)) for i in range(size)])


def summed(sends, keeps, tail):
    bits = list(range(lax.axis_size("rows").bit_length() - 1))
    turn, last = bits[:-1], bits[-1:]
    orders = [turn[n % len(turn):] + turn[:n % len(turn)] + last for n in range(len(sends))]
    me = lax.axis_index("rows")
    terms = [[keep, exchange(send, "grp", 0)] for send, keep in zip(sends, keeps)]
    halving = len(bits) - tail
    for step in range(halving):
        for n, order in enumerate(orders):
            bit = order[step]
            half = terms[n][0].shape[0] // 2
            mine = (me >> bit) & 1
            send, keep = (
                sum(lax.dynamic_slice_in_dim(x, at * half, half, 0) for x in terms[n])
                for at in (1 - mine, mine)
            )
            terms[n] = [keep, exchange(send, "rows", bit)]
    parts = [a + b for a, b in terms]
    for step in range(halving, len(bits)):
        for n, order in enumerate(orders):
            parts[n] = parts[n] + exchange(parts[n], "rows", order[step])
    for step in reversed(range(halving)):
        for n, order in enumerate(orders):
            x, bit = parts[n], order[step]
            other = exchange(x, "rows", bit)
            mine = ((me >> bit) & 1) == 1
            parts[n] = jnp.concatenate([jnp.where(mine, other, x), jnp.where(mine, x, other)], axis=0)
    return parts, [exchange(x, "grp", 0) for x in parts]


def summed_at_once(send, keep):
    size = lax.axis_size("rows")
    x = keep + exchange(send, "grp", 0)
    got = lax.all_to_all(x, "rows", 0, 0, tiled=True)
    mine = got.reshape(size, x.shape[0] // size, x.shape[1]).sum(0)
    same = jnp.broadcast_to(mine[None], (size,) + mine.shape).reshape(x.shape)
    x = lax.all_to_all(same, "rows", 0, 0, tiled=True)
    return x, exchange(x, "grp", 0)


def body(earlier, snapshots, later):
    n, k = earlier.shape
    p = snapshots.shape[1] // 2
    devices = lax.axis_size(AXES)
    scale = 1.0 / (n * devices)
    core = lax.axis_index("grp").astype(jnp.int32).reshape(1)
    blocks = k // p
    rows = (2 * blocks + blocks * (blocks + 1) // 2) * p
    unit = 2 * devices * 8
    parts = 3 if rows % (3 * unit) == 0 else 1
    tile = 1024 if n % 1024 == 0 else n

    def smem():
        return pl.BlockSpec(memory_space=pltpu.SMEM)

    def whole(*shape):
        return pl.BlockSpec(shape, lambda i: (0,) * len(shape))

    def tiled(cols):
        return pl.BlockSpec((tile, cols), lambda i: (i, 0))

    def shape(*dims, dtype=F32):
        return jax.ShapeDtypeStruct(dims, dtype)

    def near(*dims, dtype=F32):
        return pltpu.VMEM(dims, dtype)

    def far(*dims, dtype=F32):
        return pltpu.HBM(dims, dtype)

    apart = pl.BlockSpec(memory_space=pl.ANY)
    inside = pl.BlockSpec(memory_space=pltpu.VMEM)

    def fixed(x):
        return pltpu.with_memory_space_constraint(x, pltpu.HBM)

    earlier, snapshots, later = fixed(earlier), fixed(snapshots), fixed(later)

    def call(kernel, name, room, ins, outs, scratch, flops, size, *args, grid=None):
        return pl.pallas_call(
            kernel,
            grid=(n // tile,) if grid is None else grid,
            in_specs=[s for s in ins],
            out_specs=[s for s, _ in outs],
            out_shape=[s for _, s in outs],
            scratch_shapes=scratch,
            name=name,
            cost_estimate=pl.CostEstimate(flops=flops, bytes_accessed=size, transcendentals=0),
            compiler_params=pltpu.CompilerParams(
                vmem_limit_bytes=room * MIB
            ),
        )(*args)

    short = 512 if n % 512 == 0 else n
    tiles = n // short
    dma = pltpu.SemaphoreType.DMA

    def held(*dims, dtype=F32):
        return pltpu.VMEM(dims, dtype)

    half = rows // parts // 2
    halves = [(whole(half, p), near(half, p))] * (2 * parts)
    got = call(
        lambda *r: cross_kernel(parts, scale, *r), "cross", 32,
        [smem(), tiled(k), tiled(2 * p)],
        halves,
        [pltpu.VMEM((rows, p), F32)],
        2 * n * rows * p, 2 * n * (k + 2 * p),
        core, earlier, snapshots,
    )
    own, other = summed(got[:parts], got[parts:], 1)

    short = 512 if n % 512 == 0 else n
    tiles = n // short
    dma = pltpu.SemaphoreType.DMA

    def held(*dims, dtype=F32):
        return pltpu.VMEM(dims, dtype)

    u, w, z, h, t, send, keep = call(
        lambda *r: first_kernel(parts, short, scale, *r), "first", 50,
        [smem()] + [apart] * (2 * parts + 2),
        [
            (apart, far(n, p)),
            (apart, far(n, 2 * p, dtype=BF16)),
            (apart, far(k, p)),
            (apart, far(k, p)),
            (inside, near(p, p)),
            (inside, near(p, p)),
            (inside, near(p, p)),
        ],
        [
            held(rows, p),
            held(n, k, dtype=BF16),
            held(n, 2 * p, dtype=BF16),
            held(n, p),
            held(n, 2 * p, dtype=BF16),
            held(k, p),
            held(k, p),
            held(k, 3 * p, dtype=BF16),
            held(k, k, dtype=BF16),
            held(k, k, dtype=BF16),
            held(2 * p, p),
            held(p, p),
            dma((2 * parts,)), dma((tiles, 2)), dma((tiles, 2)), dma((2,)),
        ],
        2 * n * p * (3 * k + 4 * p) + 12 * k * k * p, n * (2 * k + 12 * p),
        core, *own, *other, earlier, snapshots, grid=(),
    )
    own, other = summed_at_once(send, keep)

    got = call(
        lambda *r: second_kernel(3, short, scale, *r), "second", 46,
        [smem()] + [apart] * 4 + [inside] + [apart] * 4,
        [
            (apart, far(n, p, dtype=BF16)),
            (apart, far(n, 2 * p, dtype=BF16)),
            (inside, near(p, p)),
            (inside, near(p, p)),
        ] + [(inside, near(p, p))] * 6,
        [
            held(2 * p, p),
            held(k, p),
            held(k, p),
            held(n, k, dtype=BF16),
            held(n, p),
            held(n, 2 * p, dtype=BF16),
            held(n, 2 * p, dtype=BF16),
            held(n, p, dtype=BF16),
            held(n, 2 * p, dtype=BF16),
            held(p, p),
            held(2 * p, p, dtype=BF16),
            held(p, p, dtype=BF16),
            held(p, p, dtype=BF16),
            held(k, p, dtype=BF16),
            held(p, p, dtype=BF16),
            held(6 * p, p),
            held(p, p),
            dma((2,)), dma((2,)), dma((tiles, 4)), dma((tiles, 2)),
        ],
        2 * n * p * (k + 15 * p), n * (2 * k + 18 * p),
        core, own, other, fixed(z), fixed(h), t, earlier, fixed(u), fixed(w), later, grid=(),
    )
    q_one, w2, r_one, expected = got[:4]
    own, other = summed(got[4:7], got[7:], 2)

    return tuple(call(
        lambda *r: last_kernel(3, short, *r), "last", 26,
        [smem()] + [apart] * 6 + [inside] * 2 + [apart] * 2,
        [
            (apart, far(n, 2 * p, dtype=BF16)),
            (inside, shape(2, p, p)),
            (inside, shape(2 * p, 2 * p)),
        ],
        [
            held(6 * p, p),
            held(n, p, dtype=BF16),
            held(n, 2 * p, dtype=BF16),
            held(n, 2 * p, dtype=BF16),
            held(p, p),
            held(p, p),
            held(2 * p, p, dtype=BF16),
            held(p, p, dtype=BF16),
            held(p, p, dtype=BF16),
            dma((6,)), dma((tiles, 2)), dma((tiles, 1)),
        ],
        2 * n * p * 4 * p, n * 10 * p,
        core, *own, *other, expected, r_one, fixed(q_one), fixed(w2), grid=(),
    ))


def solution(mesh):
    spec = P(("rows", "grp"), None)
    return jax.shard_map(
        body,
        mesh=mesh,
        in_specs=(spec, spec, spec),
        out_specs=(spec, P(), P()),
        check_vma=False,
    )
```

```python
import jax
import jax.numpy as jnp
from jax import lax
from jax.experimental import pallas as pl
from jax.experimental.pallas import tpu as pltpu
from jax.sharding import PartitionSpec as P

AXES = ("rows", "grp")
HIGHEST = lax.Precision.HIGHEST
BF16 = jnp.bfloat16
F32 = jnp.float32
MIB = 2**20


def dot(a, b):
    return jnp.dot(a, b, preferred_element_type=F32)


def full(a, b):
    return jnp.dot(a, b, precision=HIGHEST, preferred_element_type=F32)


def wide(x):
    return x.astype(F32)


def split(x):
    high = x.astype(BF16)
    return high, (x - wide(high)).astype(BF16)


def thrice(a, b):
    return dot(a[0], b[0]) + dot(a[0], b[1]) + dot(a[1], b[0])


def factor_tile(groups, emit):
    count = len(groups)
    lane = lax.broadcasted_iota(jnp.int32, (8, 128), 1)
    sub = lax.broadcasted_iota(jnp.int32, (8, 128), 0)
    rows = list(groups)
    for k in range(count):
        base = 8 * k
        strip = rows[k]
        inside = (lane >= base) & (lane < base + 8)
        eye = jnp.where(lane == base + sub, 1.0, 0.0).astype(F32)
        mixed = jnp.where(inside, eye, strip)
        cols = [jnp.broadcast_to(strip[:, base + j:base + j + 1], (8, 128)) for j in range(8)]
        entry = {}
        for j in range(8):
            for i in range(j, 8):
                entry[i, j] = jnp.broadcast_to(cols[j][i:i + 1, :], (8, 128))
        scale = []
        low = {}
        for j in range(8):
            r = lax.rsqrt(entry[j, j])
            scale.append(r)
            for i in range(j + 1, 8):
                low[i, j] = entry[i, j] * r
            for c in range(j + 1, 8):
                for i in range(c, 8):
                    entry[i, c] = entry[i, c] - low[i, j] * low[c, j]
        upper, both = [], []
        for j in range(8):
            u = jnp.broadcast_to(strip[j:j + 1, :], (8, 128))
            v = jnp.broadcast_to(mixed[j:j + 1, :], (8, 128))
            for i in range(j):
                u = u - low[j, i] * upper[i]
                v = v - low[j, i] * both[i]
            upper.append(u * scale[j])
            both.append(v * scale[j])
        out_r = upper[0]
        out_m = both[0]
        for j in range(1, 8):
            out_r = jnp.where(sub == j, upper[j], out_r)
            out_m = jnp.where(sub == j, both[j], out_m)
        emit(
            k,
            jnp.where(lane >= base + sub, out_r, 0.0),
            jnp.where(lane <= base + sub, out_m, 0.0),
        )
        for g in range(k + 1, count):
            w = rows[g]
            new = jnp.where(inside, 0.0, w)
            left = []
            for j in range(8):
                c = jnp.broadcast_to(w[:, base + j:base + j + 1], (8, 128))
                for i in range(j):
                    c = c - left[i] * low[j, i]
                c = c * scale[j]
                left.append(c)
                new = new - c * both[j]
            rows[g] = new


def factor(r_ref, m_ref):
    n = r_ref.shape[0]
    h = 128

    def step(t, carry):
        top = pl.multiple_of(t * h, h)
        groups = [r_ref[pl.ds(pl.multiple_of(top + 8 * g, 8), 8), pl.ds(top, h)] for g in range(h // 8)]

        def emit(k, r, m):
            at = pl.ds(pl.multiple_of(top + 8 * k, 8), 8)
            r_ref[at, pl.ds(top, h)] = r
            m_ref[at, pl.ds(top, h)] = m

        factor_tile(groups, emit)

        @pl.when(t == 0)
        def _():
            inv = m_ref[:h, :h]
            u = full(inv, r_ref[:h, h:])
            ut = u.T
            r_ref[:h, h:] = u
            r_ref[h:, h:] = r_ref[h:, h:] - full(ut, u)
            m_ref[h:, :h] = full(ut, inv)
            r_ref[h:, :h] = jnp.zeros((n - h, h), F32)
            m_ref[:h, h:] = jnp.zeros((h, n - h), F32)

        return carry

    lax.fori_loop(0, n // h, step, 0)
    m_ref[h:, :h] = -full(m_ref[h:, h:], m_ref[h:, :h])


def begin(copies, sems):
    for n, (source, target) in enumerate(copies):
        pltpu.make_async_copy(source, target, sems.at[n]).start()


def finish(copies, sems):
    for n, (source, target) in enumerate(copies):
        pltpu.make_async_copy(source, target, sems.at[n]).wait()


def places(core_ref, own, other, total_ref):
    mine = core_ref[0]
    copies = []
    at = 0
    for a, b in zip(own, other):
        h = a.shape[0]
        copies.append((a, total_ref.at[pl.ds(pl.multiple_of(at + mine * h, 8), h)]))
        copies.append((b, total_ref.at[pl.ds(pl.multiple_of(at + (1 - mine) * h, 8), h)]))
        at += 2 * h
    return copies


def tile_rows(i, tile):
    return pl.ds(pl.multiple_of(i * tile, tile), tile)


def at_tile(pairs, i, tile):
    rows = tile_rows(i, tile)
    return [(a.at[rows], b.at[rows]) for a, b in pairs]


def deal(core_ref, total_ref, scale, sends, keeps):
    mine = core_ref[0]
    at = 0
    for send, keep in zip(sends, keeps):
        h = send.shape[0]
        keep[...] = total_ref[pl.ds(pl.multiple_of(at + mine * h, 8), h)] * scale
        send[...] = total_ref[pl.ds(pl.multiple_of(at + (1 - mine) * h, 8), h)] * scale
        at += 2 * h


def cross_kernel(parts, scale, core_ref, e_ref, x_ref, *refs):
    sends, keeps, acc = refs[:parts], refs[parts:2 * parts], refs[-1]
    k = e_ref.shape[1]
    p = x_ref.shape[1] // 2
    step = pl.program_id(0)

    @pl.when(step == 0)
    def _():
        acc[...] = jnp.zeros_like(acc)

    et = e_ref[...].T
    got = dot(et, x_ref[...])
    for c in range(2):
        acc[c * k:(c + 1) * k] += got[:, c * p:(c + 1) * p]
    at = 2 * k
    for j in range(k // p):
        m = (j + 1) * p
        acc[at:at + m] += dot(et[:m], e_ref[:, j * p:(j + 1) * p])
        at += m

    @pl.when(step == pl.num_programs(0) - 1)
    def _():
        deal(core_ref, acc, scale, sends, keeps)


def first_kernel(parts, tile, scale, core_ref, *refs):
    own, other = refs[:parts], refs[parts:2 * parts]
    (e_in, x_in, u_out, w_out, z_out, h_out, t_ref, send, keep,
     total, e_ref, x_ref, u_ref, w_ref, z_ref, h_ref, b_ref, offh, offl, acc, hl,
     sum_sems, in_sems, out_sems, small_sems) = refs[2 * parts:]
    n, k = e_ref.shape
    p = u_ref.shape[1]
    tiles = n // tile
    sums = places(core_ref, own, other, total)
    inputs = [(e_in, e_ref), (x_in, x_ref)]
    outputs = [(u_ref, u_out), (w_ref, w_out)]
    small = [(z_ref, z_out), (h_ref, h_out)]
    begin(sums, sum_sems)
    acc[...] = jnp.zeros_like(acc)
    hl[...] = jnp.zeros_like(hl)
    finish(sums, sum_sems)
    for i in range(tiles):
        begin(at_tile(inputs, i, tile), in_sems.at[i])

    at = 2 * k
    for j in range(k // p):
        cols = slice(j * p, (j + 1) * p)
        for i in range(j + 1):
            block = total[at:at + p]
            at += p
            if i == j:
                a = lax.broadcasted_iota(jnp.int32, (p, p), 0)
                b = lax.broadcasted_iota(jnp.int32, (p, p), 1)
                block = block - jnp.where(a == b, 1.0, 0.0)
            high, low = split(block)
            rows = slice(i * p, (i + 1) * p)
            offh[rows, cols] = high
            offl[rows, cols] = low
            if i < j:
                offh[cols, rows] = high.T
                offl[cols, rows] = low.T
    for c in range(2):
        coef = total[c * k:(c + 1) * k]
        b = coef.astype(BF16)
        b_ref[:, c * p:(c + 1) * p] = b
        after = (coef - wide(b)) - dot(offh[...], b) - dot(offl[...], b)
        if c == 0:
            sb = after.astype(BF16)
            b_ref[:, 2 * p:] = sb
            against = (after - wide(sb)) - dot(offh[...], sb) - dot(offl[...], sb)
            h_ref[...] = against
        else:
            z_ref[...] = after
            high, low = split(against.T)
            t_ref[...] = dot(high, b) + dot(low, b)
    begin(small, small_sems)

    for i in range(tiles):
        finish(at_tile(inputs, i, tile), in_sems.at[i])

    def project(i):
        rows = tile_rows(i, tile)
        t = dot(e_ref[rows, :], b_ref[...])
        once = wide((wide(x_ref[rows, :p]) - t[:, :p]).astype(BF16))
        u_ref[rows, :] = wide(x_ref[rows, p:]) - t[:, p:2 * p]
        high, low = split(once - t[:, 2 * p:])
        w_ref[rows, :p] = high
        w_ref[rows, p:] = low

    def gather(i):
        rows = tile_rows(i, tile)
        high = w_ref[rows, :p]
        both = jnp.concatenate([high.T, w_ref[rows, p:].T], axis=0)
        got = dot(both, jnp.concatenate([high, x_ref[rows, p:]], axis=1))
        acc[:p] += got[:p, :p]
        hl[...] += got[p:, :p]
        acc[p:] += got[:p, p:] + got[p:, p:]

    def step(i, carry):
        gather(i)
        project(i + 1)
        begin(at_tile(outputs, i + 1, tile), out_sems.at[i + 1])
        return carry

    project(0)
    begin(at_tile(outputs, 0, tile), out_sems.at[0])
    lax.fori_loop(0, tiles - 1, step, 0)
    gather(tiles - 1)
    acc[:p] = acc[:p] + hl[...] + hl[...].T
    deal(core_ref, acc, scale, [send], [keep])
    for i in range(tiles):
        finish(at_tile(outputs, i, tile), out_sems.at[i])
    finish(small, small_sems)


def second_kernel(parts, tile, scale, core_ref, own, other, z_in, h_in, t_ref, e_in, u_in, w_in, l_in, *refs):
    q_out, w2_out, r_ref, x_ref = refs[:4]
    sends, keeps = refs[4:4 + parts], refs[4 + parts:4 + 2 * parts]
    (total, z_ref, h_ref, e_ref, u_ref, w_ref, l_ref, q_ref, w2_ref, m_ref, ih, il, db, ub, lb, acc, hl,
     sum_sems, small_sems, in_sems, out_sems) = refs[4 + 2 * parts:]
    p = r_ref.shape[0]
    n = e_ref.shape[0]
    tiles = n // tile
    sums = places(core_ref, [own], [other], total)
    small = [(z_in, z_ref), (h_in, h_ref)]
    inputs = [(e_in, e_ref), (u_in, u_ref), (w_in, w_ref), (l_in, l_ref)]
    outputs = [(q_ref, q_out), (w2_ref, w2_out)]
    begin(sums, sum_sems)
    acc[...] = jnp.zeros_like(acc)
    hl[...] = jnp.zeros_like(hl)
    finish(sums, sum_sems)
    begin(small, small_sems)
    for i in range(tiles):
        begin(at_tile(inputs, i, tile), in_sems.at[i])

    r_ref[...] = total[:p]
    factor(r_ref, m_ref)
    inv = m_ref[...]
    high, low = split(inv.T)
    ih[:p] = high
    ih[p:] = high
    il[...] = low
    d = full(inv, total[p:])
    d_b = d.astype(BF16)
    db[...] = d_b
    finish(small, small_sems)
    inv_s = split(inv)
    against = split(h_ref[...])
    at = split(h_ref[...].T)
    turned = split(dot(high, d_b) + dot(low, d_b))
    upper = (z_ref[...] - thrice(against, turned)).astype(BF16)
    ub[...] = upper
    lower = (d - wide(d_b)) - thrice(inv_s, split(t_ref[...]))
    lower_b = lower.astype(BF16)
    lb[...] = lower_b
    x_ref[...] = (lower - wide(lower_b)) - thrice(inv_s, split(dot(at[0], upper) + dot(at[1], upper)))

    for i in range(tiles):
        finish(at_tile(inputs, i, tile), in_sems.at[i])

    def project(i):
        rows = tile_rows(i, tile)
        q = (dot(w_ref[rows, :], ih[...]) + dot(w_ref[rows, :p], il[...])).astype(BF16)
        q_ref[rows, :] = q
        once = wide((u_ref[rows, :] - dot(q, db[...])).astype(BF16))
        high, low = split(once - dot(e_ref[rows, :], ub[...]) - dot(q, lb[...]))
        w2_ref[rows, :p] = high
        w2_ref[rows, p:] = low

    def gather(i):
        rows = tile_rows(i, tile)
        high, low = w2_ref[rows, :p], w2_ref[rows, p:]
        qt = q_ref[rows, :].T
        left = jnp.concatenate([high.T, low.T, qt], axis=0)
        got = dot(left, jnp.concatenate([high, l_ref[rows, :]], axis=1))
        acc[:p] += got[:p, :p]
        hl[...] += got[p:2 * p, :p]
        acc[p:2 * p] += got[2 * p:, :p] + dot(qt, low)
        for c in range(2):
            cols = slice((1 + c) * p, (2 + c) * p)
            acc[(2 + c) * p:(3 + c) * p] += got[:p, cols] + got[p:2 * p, cols]
            acc[(4 + c) * p:(5 + c) * p] += got[2 * p:, cols]

    def step(i, carry):
        gather(i)
        project(i + 1)
        begin(at_tile(outputs, i + 1, tile), out_sems.at[i + 1])
        return carry

    project(0)
    begin(at_tile(outputs, 0, tile), out_sems.at[0])
    lax.fori_loop(0, tiles - 1, step, 0)
    gather(tiles - 1)
    acc[:p] = acc[:p] + hl[...] + hl[...].T
    deal(core_ref, acc, scale, sends, keeps)
    for i in range(tiles):
        finish(at_tile(outputs, i, tile), out_sems.at[i])


def last_kernel(parts, tile, core_ref, *refs):
    own, other = refs[:parts], refs[parts:2 * parts]
    (x_ref, r1_ref, q_in, w_in, basis_out, factors, shift,
     total, q_ref, w_ref, basis, r_ref, m_ref, ih, il, back, sum_sems, in_sems, out_sems) = refs[2 * parts:]
    p = r_ref.shape[0]
    tiles = q_ref.shape[0] // tile
    sums = places(core_ref, own, other, total)
    inputs = [(q_in, q_ref), (w_in, w_ref)]
    outputs = [(basis, basis_out)]
    begin(sums, sum_sems)
    finish(sums, sum_sems)
    for i in range(tiles):
        begin(at_tile(inputs, i, tile), in_sems.at[i])

    res = total[p:2 * p]
    off = res - x_ref[...]
    off_b = off.astype(BF16)
    offt = off.T.astype(BF16)
    cut = dot(offt, res.astype(BF16))
    r_ref[...] = total[:p] - cut - cut.T + dot(offt, off_b)
    factor(r_ref, m_ref)
    inv = m_ref[...]
    high, low = split(inv.T)
    ih[:p] = high
    ih[p:] = high
    il[...] = low
    back[...] = dot(off_b, high).astype(BF16)

    def step(i, carry):
        rows = tile_rows(i, tile)
        finish(at_tile(inputs, i, tile), in_sems.at[i])
        q = dot(w_ref[rows, :], ih[...]) + dot(w_ref[rows, :p], il[...]) - dot(q_ref[rows, :], back[...])
        basis[rows, :p] = q_ref[rows, :]
        basis[rows, p:] = q.astype(BF16)
        begin(at_tile(outputs, i, tile), out_sems.at[i])
        return carry

    lax.fori_loop(0, tiles, step, 0)
    inv_s = split(m_ref[...])
    factors[0] = r1_ref[...]
    factors[1] = r_ref[...]
    for c in range(2):
        cols = slice(c * p, (c + 1) * p)
        early = total[(4 + c) * p:(5 + c) * p]
        shift[:p, cols] = early
        late = total[(2 + c) * p:(3 + c) * p] - dot(offt, early.astype(BF16))
        shift[p:, cols] = thrice(inv_s, split(late))
    for i in range(tiles):
        finish(at_tile(outputs, i, tile), out_sems.at[i])


def exchange(x, axis, bit):
    size = lax.axis_size(axis)
    return lax.ppermute(x, axis, [(i, i ^ (1 << bit)) for i in range(size)])


def summed(sends, keeps, tail):
    bits = list(range(lax.axis_size("rows").bit_length() - 1))
    turn, last = bits[:-1], bits[-1:]
    orders = [turn[n % len(turn):] + turn[:n % len(turn)] + last for n in range(len(sends))]
    me = lax.axis_index("rows")
    parts = [keep + exchange(send, "grp", 0) for send, keep in zip(sends, keeps)]
    halving = len(bits) - tail
    for step in range(halving):
        for n, order in enumerate(orders):
            x, bit = parts[n], order[step]
            half = x.shape[0] // 2
            mine = (me >> bit) & 1
            send = lax.dynamic_slice_in_dim(x, (1 - mine) * half, half, 0)
            keep = lax.dynamic_slice_in_dim(x, mine * half, half, 0)
            parts[n] = keep + exchange(send, "rows", bit)
    for step in range(halving, len(bits)):
        for n, order in enumerate(orders):
            parts[n] = parts[n] + exchange(parts[n], "rows", order[step])
    for step in reversed(range(halving)):
        for n, order in enumerate(orders):
            x, bit = parts[n], order[step]
            other = exchange(x, "rows", bit)
            mine = ((me >> bit) & 1) == 1
            parts[n] = jnp.concatenate([jnp.where(mine, other, x), jnp.where(mine, x, other)], axis=0)
    return parts, [exchange(x, "grp", 0) for x in parts]


def summed_at_once(send, keep):
    size = lax.axis_size("rows")
    x = keep + exchange(send, "grp", 0)
    got = lax.all_to_all(x, "rows", 0, 0, tiled=True)
    mine = got.reshape(size, x.shape[0] // size, x.shape[1]).sum(0)
    same = jnp.broadcast_to(mine[None], (size,) + mine.shape).reshape(x.shape)
    x = lax.all_to_all(same, "rows", 0, 0, tiled=True)
    return x, exchange(x, "grp", 0)


def body(earlier, snapshots, later):
    n, k = earlier.shape
    p = snapshots.shape[1] // 2
    devices = lax.axis_size(AXES)
    scale = 1.0 / (n * devices)
    core = lax.axis_index("grp").astype(jnp.int32).reshape(1)
    blocks = k // p
    rows = (2 * blocks + blocks * (blocks + 1) // 2) * p
    unit = 2 * devices * 8
    parts = 3 if rows % (3 * unit) == 0 else 1
    tile = 1024 if n % 1024 == 0 else n

    def smem():
        return pl.BlockSpec(memory_space=pltpu.SMEM)

    def whole(*shape):
        return pl.BlockSpec(shape, lambda i: (0,) * len(shape))

    def tiled(cols):
        return pl.BlockSpec((tile, cols), lambda i: (i, 0))

    def shape(*dims, dtype=F32):
        return jax.ShapeDtypeStruct(dims, dtype)

    def near(*dims, dtype=F32):
        return pltpu.VMEM(dims, dtype)

    def far(*dims, dtype=F32):
        return pltpu.HBM(dims, dtype)

    apart = pl.BlockSpec(memory_space=pl.ANY)
    inside = pl.BlockSpec(memory_space=pltpu.VMEM)

    def fixed(x):
        return pltpu.with_memory_space_constraint(x, pltpu.HBM)

    earlier, snapshots, later = fixed(earlier), fixed(snapshots), fixed(later)

    def call(kernel, name, room, ins, outs, scratch, flops, size, *args, grid=None):
        return pl.pallas_call(
            kernel,
            grid=(n // tile,) if grid is None else grid,
            in_specs=[s for s in ins],
            out_specs=[s for s, _ in outs],
            out_shape=[s for _, s in outs],
            scratch_shapes=scratch,
            name=name,
            cost_estimate=pl.CostEstimate(flops=flops, bytes_accessed=size, transcendentals=0),
            compiler_params=pltpu.CompilerParams(
                vmem_limit_bytes=room * MIB
            ),
        )(*args)

    short = 512 if n % 512 == 0 else n
    tiles = n // short
    dma = pltpu.SemaphoreType.DMA

    def held(*dims, dtype=F32):
        return pltpu.VMEM(dims, dtype)

    half = rows // parts // 2
    halves = [(whole(half, p), near(half, p))] * (2 * parts)
    got = call(
        lambda *r: cross_kernel(parts, scale, *r), "cross", 32,
        [smem(), tiled(k), tiled(2 * p)],
        halves,
        [pltpu.VMEM((rows, p), F32)],
        2 * n * rows * p, 2 * n * (k + 2 * p),
        core, earlier, snapshots,
    )
    own, other = summed(got[:parts], got[parts:], 1)

    short = 512 if n % 512 == 0 else n
    tiles = n // short
    dma = pltpu.SemaphoreType.DMA

    def held(*dims, dtype=F32):
        return pltpu.VMEM(dims, dtype)

    u, w, z, h, t, send, keep = call(
        lambda *r: first_kernel(parts, short, scale, *r), "first", 50,
        [smem()] + [apart] * (2 * parts + 2),
        [
            (apart, far(n, p)),
            (apart, far(n, 2 * p, dtype=BF16)),
            (apart, far(k, p)),
            (apart, far(k, p)),
            (inside, near(p, p)),
            (inside, near(p, p)),
            (inside, near(p, p)),
        ],
        [
            held(rows, p),
            held(n, k, dtype=BF16),
            held(n, 2 * p, dtype=BF16),
            held(n, p),
            held(n, 2 * p, dtype=BF16),
            held(k, p),
            held(k, p),
            held(k, 3 * p, dtype=BF16),
            held(k, k, dtype=BF16),
            held(k, k, dtype=BF16),
            held(2 * p, p),
            held(p, p),
            dma((2 * parts,)), dma((tiles, 2)), dma((tiles, 2)), dma((2,)),
        ],
        2 * n * p * (3 * k + 4 * p) + 12 * k * k * p, n * (2 * k + 12 * p),
        core, *own, *other, earlier, snapshots, grid=(),
    )
    own, other = summed_at_once(send, keep)

    got = call(
        lambda *r: second_kernel(3, short, scale, *r), "second", 46,
        [smem()] + [apart] * 4 + [inside] + [apart] * 4,
        [
            (apart, far(n, p, dtype=BF16)),
            (apart, far(n, 2 * p, dtype=BF16)),
            (inside, near(p, p)),
            (inside, near(p, p)),
        ] + [(inside, near(p, p))] * 6,
        [
            held(2 * p, p),
            held(k, p),
            held(k, p),
            held(n, k, dtype=BF16),
            held(n, p),
            held(n, 2 * p, dtype=BF16),
            held(n, 2 * p, dtype=BF16),
            held(n, p, dtype=BF16),
            held(n, 2 * p, dtype=BF16),
            held(p, p),
            held(2 * p, p, dtype=BF16),
            held(p, p, dtype=BF16),
            held(p, p, dtype=BF16),
            held(k, p, dtype=BF16),
            held(p, p, dtype=BF16),
            held(6 * p, p),
            held(p, p),
            dma((2,)), dma((2,)), dma((tiles, 4)), dma((tiles, 2)),
        ],
        2 * n * p * (k + 15 * p), n * (2 * k + 18 * p),
        core, own, other, fixed(z), fixed(h), t, earlier, fixed(u), fixed(w), later, grid=(),
    )
    q_one, w2, r_one, expected = got[:4]
    own, other = summed(got[4:7], got[7:], 2)

    return tuple(call(
        lambda *r: last_kernel(3, short, *r), "last", 26,
        [smem()] + [apart] * 6 + [inside] * 2 + [apart] * 2,
        [
            (apart, far(n, 2 * p, dtype=BF16)),
            (inside, shape(2, p, p)),
            (inside, shape(2 * p, 2 * p)),
        ],
        [
            held(6 * p, p),
            held(n, p, dtype=BF16),
            held(n, 2 * p, dtype=BF16),
            held(n, 2 * p, dtype=BF16),
            held(p, p),
            held(p, p),
            held(2 * p, p, dtype=BF16),
            held(p, p, dtype=BF16),
            held(p, p, dtype=BF16),
            dma((6,)), dma((tiles, 2)), dma((tiles, 1)),
        ],
        2 * n * p * 4 * p, n * 10 * p,
        core, *own, *other, expected, r_one, fixed(q_one), fixed(w2), grid=(),
    ))


def solution(mesh):
    spec = P(("rows", "grp"), None)
    return jax.shard_map(
        body,
        mesh=mesh,
        in_specs=(spec, spec, spec),
        out_specs=(spec, P(), P()),
        check_vma=False,
    )
```
